32 devices in a mesh: rows: 16 (over z, x, core), pair: 2 (over y).
Axes of the slice: x: 2, y: 2, z: 4, core: 2. Of those that a mesh axis runs over, the one named last changes fastest.
Arguments:
- tokens: bfloat16 [16, 1024, 1024], P('rows', 'pair'), may hold values from -6 to 6
- cotangent: bfloat16 [16, 1024, 1024], P('rows', 'pair'), may hold values from -6 to 6
- gains: bfloat16 [1024, 2], P('rows', 'pair'), may hold values from 0.099609375 to 1.8984375
- w_qkv: bfloat16 [1024, 3072], P('rows', 'pair'), may hold values from -0.1875 to 0.1875
- w_out: bfloat16 [1024, 1024], P('rows', 'pair'), may hold values from -3 to 3
- w_up: bfloat16 [1024, 4096], P('rows', 'pair'), may hold values from -0.1875 to 0.1875
- w_down: bfloat16 [4096, 1024], P('rows', 'pair'), may hold values from -0.09375 to 0.09375
- phone_len: int32 [16, 2], P('rows'), may hold values from 20 to 400, as said below
- prompt_len: int32 [16, 2], P('rows'), may hold values from 1 to 471, as said below
- target_len: int32 [16, 2], P('rows'), may hold values from 1 to 511, as said below
Outputs:
- mixed: bfloat16 [16, 1024, 1024], P('rows', 'pair')
- grad_tokens: float32 [16, 1024, 1024], P('rows', 'pair')
- grad_gains: float32 [1024, 2], P('rows', 'pair')
- grad_qkv: float32 [1024, 3072], P('rows', 'pair')
- grad_out: float32 [1024, 1024], P('rows', 'pair')
- grad_up: float32 [1024, 4096], P('rows', 'pair')
- grad_down: float32 [4096, 1024], P('rows', 'pair')
The draws below stay inside these ranges and needn't reach their ends.
Inputs may be any that keep to these rules, and one draw needn't show every extreme that they name: `phone_len`: some row, drawn from the seed, has a segment of exactly 400 phonemes, and some other row has 20 in every segment; a row's phoneme and prompt lengths sum to 512. `prompt_len`: A row's phoneme and prompt lengths sum to 512. `target_len`: A row's target lengths sum to 512.
All inputs are finite; a program needn't handle non-finite values.
Results may differ from the reference program's by a relative error of at most 0.014.
Values may be sent and summed in bfloat16 or wider, within the bound.
No kernel may reach another device: no remote copies, remote signals or barrier semaphores. Data moves between devices by JAX's collectives and lax.ppermute only.
A program may use at most 192 MiB of HBM per device.

```python
import jax
import jax.numpy as jnp
from jax import lax

D = 1024
HEADS = 16
HEAD_DIM = 64
FF = 4096
TOK_DEV = 512
PHON_MIN = 20
PHON_MAX = 400
SEGS = 2
PACKS = 16


def split_total(subkey, totals, pieces):
    width_cut = TOK_DEV - 1
    candidates = jnp.arange(width_cut, dtype=jnp.int32)
    noise_bits = jax.random.randint(subkey, (PACKS, width_cut), 0, 1 << 14, dtype=jnp.int32)
    scores = noise_bits * TOK_DEV + candidates[None, :]
    scores = jnp.where(candidates[None, :] + 1 <= totals[:, None] - 1, scores, scores + (1 << 29))
    chosen = jnp.argsort(scores, axis=1)[:, :pieces - 1].astype(jnp.int32) + 1
    chosen = jnp.sort(chosen, axis=1)
    bounds = jnp.concatenate([jnp.zeros((PACKS, 1), jnp.int32), chosen, totals[:, None].astype(jnp.int32)], axis=1)
    return bounds[:, 1:] - bounds[:, :-1]


def segment_lengths(base_key):
    subkeys = jax.random.split(base_key, 7)
    seg_index = jnp.arange(SEGS, dtype=jnp.int32)[None, :]
    row_index = jnp.arange(PACKS, dtype=jnp.int32)
    other_cap = min(PHON_MAX, (TOK_DEV - SEGS - PHON_MAX) // (SEGS - 1))
    chosen = jax.random.randint(subkeys[1], (PACKS, 1), 0, SEGS, dtype=jnp.int32)
    is_chosen = seg_index == chosen
    big_phones = jax.random.randint(subkeys[0], (PACKS, SEGS), PHON_MIN, PHON_MAX + 1, dtype=jnp.int32)
    small_phones = jax.random.randint(subkeys[5], (PACKS, SEGS), PHON_MIN, other_cap + 1, dtype=jnp.int32)
    phones = jnp.where(is_chosen, big_phones, small_phones).astype(jnp.int32)
    top_row = jax.random.randint(subkeys[4], (), 0, PACKS, dtype=jnp.int32)
    offset = jax.random.randint(subkeys[6], (), 1, PACKS, dtype=jnp.int32)
    extreme_row = (top_row + offset) % PACKS
    in_top = (row_index == top_row)[:, None]
    in_extreme = (row_index == extreme_row)[:, None]
    phones = jnp.where(in_top & is_chosen, PHON_MAX, phones).astype(jnp.int32)
    phones = jnp.where(in_extreme, PHON_MIN, phones).astype(jnp.int32)
    remaining = (TOK_DEV - jnp.sum(phones, axis=1)).astype(jnp.int32)
    prompts = split_total(subkeys[2], remaining, SEGS)
    targets = split_total(subkeys[3], jnp.full((PACKS,), TOK_DEV, jnp.int32), SEGS)
    prompt_big = jnp.where(is_chosen, remaining[:, None] - (SEGS - 1), 1).astype(jnp.int32)
    target_big = jnp.where(is_chosen, TOK_DEV - (SEGS - 1), 1).astype(jnp.int32)
    prompts = jnp.where(in_extreme, prompt_big, prompts).astype(jnp.int32)
    targets = jnp.where(in_extreme, target_big, targets).astype(jnp.int32)
    return (phones, prompts, targets)


def draw_phone_len(key, part):
    shared = segment_lengths(key)
    return shared[0]


def draw_prompt_len(key, part):
    shared = segment_lengths(key)
    return shared[1]


def draw_target_len(key, part):
    shared = segment_lengths(key)
    return shared[2]


def level_of(stream_key, extent, cuts, low, top_value):
    factor_of, own = 1.0, jax.random.fold_in(stream_key, 6)
    for position, parts in cuts:
        steps = jnp.exp(jax.random.uniform(jax.random.fold_in(own, position), (parts,), jnp.float32, low / len(cuts), top_value / len(cuts)))
        factor_of = factor_of * jnp.repeat(steps, extent[position] // parts).reshape([-1 if axis == position else 1 for axis in range(len(extent))])
    return factor_of


def gaussian(key, dims, deviation, limit, cuts=(), kind=jnp.bfloat16):
    entries = deviation * jax.random.normal(key, dims, jnp.float32)
    if cuts:
        entries = entries * level_of(key, dims, cuts, -0.22, 0.18)
    return jnp.clip(entries, -limit, limit).astype(kind)


def setup_inputs(seed: int = 0) -> dict:
    key_of = jax.random.split(jax.random.key(seed), 11)
    tokens = gaussian(key_of[0], (PACKS, 2 * TOK_DEV, D), 1.0, 6.0, ((0, 16), (1, 2)))
    cotangent = gaussian(key_of[1], (PACKS, 2 * TOK_DEV, D), 1.0, 6.0, ((0, 16), (1, 2)))
    gains = jnp.clip(1.0 + 0.18 * jax.random.normal(key_of[2], (D, 2), jnp.float32), 0.099609375, 1.8984375).astype(jnp.bfloat16)
    w_qkv = gaussian(key_of[3], (D, 3 * D), D ** -0.5, 0.1875, ((0, 16), (1, 2)))
    w_out = gaussian(key_of[4], (D, D), 4 ** -0.5, 3.0, ((0, 16), (1, 2)))
    w_up = gaussian(key_of[5], (D, FF), D ** -0.5, 0.1875, ((0, 16), (1, 2)))
    w_down = gaussian(key_of[6], (FF, D), FF ** -0.5, 0.09375, ((0, 16), (1, 2)))
    phone_len = draw_phone_len(jax.random.fold_in(key_of[10], 71), 0)
    prompt_len = draw_prompt_len(jax.random.fold_in(key_of[10], 71), 0)
    target_len = draw_target_len(jax.random.fold_in(key_of[10], 71), 0)
    return dict(tokens=tokens, cotangent=cotangent, gains=gains, w_qkv=w_qkv, w_out=w_out, w_up=w_up, w_down=w_down, phone_len=phone_len, prompt_len=prompt_len, target_len=target_len)


epsilon = 1e-05

@jax.custom_vjp
def low(v):
    return lax.optimization_barrier(v.astype(jnp.bfloat16)).astype(jnp.float32)

@jax.custom_vjp
def low_back(v):
    return v

def low_keep(v):
    return (low(v), None)

def low_pass(kept, grad):
    return (grad,)

def back_keep(v):
    return (v, None)

def back_low(kept, grad):
    return (low(grad),)
low.defvjp(low_keep, low_pass)
low_back.defvjp(back_keep, back_low)

def slot_layout(side_index, phones, prompts, targets, slot_count):
    lengths = jnp.where(side_index == 0, phones + prompts, targets).astype(jnp.int32)
    seg_ends = jnp.cumsum(lengths).astype(jnp.int32)
    starts = seg_ends - lengths
    places = jnp.arange(slot_count, dtype=jnp.int32)
    segment = lax.optimization_barrier(jnp.sum((places[:, None] >= seg_ends[None, :]).astype(jnp.int32), axis=1)).astype(jnp.int32)
    onehot = (segment[:, None] == jnp.arange(lengths.shape[0], dtype=jnp.int32)[None, :]).astype(jnp.int32)
    within = places - lax.optimization_barrier(jnp.sum(onehot * starts[None, :], axis=1)).astype(jnp.int32)
    phone_here = lax.optimization_barrier(jnp.sum(onehot * phones[None, :], axis=1)).astype(jnp.int32)
    is_phone = jnp.logical_and(side_index == 0, within < phone_here)
    ordering = places + side_index * slot_count
    return (segment, is_phone, ordering)

def permitted(query_side, key_side):
    query_seg, query_phone, query_order = query_side
    key_seg, key_phone, key_order = key_side
    same_seg = query_seg[:, None] == key_seg[None, :]
    earlier = key_order[None, :] <= query_order[:, None]
    return same_seg & (key_phone[None, :] | jnp.logical_not(query_phone)[:, None] & earlier)

def normalize(values, gain_row):
    centred = values - lax.optimization_barrier(jnp.mean(values, axis=-1, keepdims=True))
    spread = lax.optimization_barrier(jnp.mean(centred * centred, axis=-1, keepdims=True))
    return centred * lax.rsqrt(spread + epsilon) * gain_row

def exact_gelu(values):
    return jax.nn.gelu(values, approximate=False)

def attend_block(queries, key_heads, value_heads, allowed):
    highest = lax.Precision.HIGHEST
    scores = jnp.einsum('qhd,khd->hqk', queries, key_heads, precision=highest) * HEAD_DIM ** (-0.5)
    scores = low_back(scores)
    scores = jnp.where(allowed[None], scores, -1e+30)
    row_max = lax.optimization_barrier(jnp.max(scores, axis=-1, keepdims=True))
    exponents = jnp.exp(scores - row_max)
    attn_probs = exponents / lax.optimization_barrier(jnp.sum(exponents, axis=-1, keepdims=True))
    return jnp.einsum('hqk,khd->qhd', low(attn_probs), value_heads, precision=highest)

def row_forward(inputs, gains, w_qkv, w_out, w_up, w_down, layout):
    highest = lax.Precision.HIGHEST
    model_width = inputs.shape[1]
    total_slots = inputs.shape[0]
    normed_in = low(normalize(inputs, gains[:, 0]))
    projected = low_back(low(jnp.dot(normed_in, w_qkv, precision=highest)))
    queries = projected[:, :model_width].reshape(total_slots, HEADS, HEAD_DIM)
    key_heads = projected[:, model_width:2 * model_width].reshape(total_slots, HEADS, HEAD_DIM)
    value_heads = projected[:, 2 * model_width:].reshape(total_slots, HEADS, HEAD_DIM)
    block_rows = min(512, total_slots)

    def one_block(start):
        query_part = lax.dynamic_slice_in_dim(queries, start, block_rows, 0)
        query_layout = tuple((lax.dynamic_slice_in_dim(member, start, block_rows, 0) for member in layout))
        return attend_block(query_part, key_heads, value_heads, permitted(query_layout, layout))
    block_starts = jnp.arange(total_slots // block_rows, dtype=jnp.int32) * block_rows
    head_mix = lax.map(jax.checkpoint(one_block), block_starts)
    attended = low_back(low(head_mix.reshape(total_slots, model_width)))
    branch = low_back(jnp.dot(attended, w_out, precision=highest))
    middle = inputs + branch
    normed_mid = low(normalize(middle, gains[:, 1]))
    pre_act = low_back(jnp.dot(normed_mid, w_up, precision=highest))
    activated = low(exact_gelu(pre_act))
    return middle + low_back(jnp.dot(activated, w_down, precision=highest))

def reference(tokens, cotangent, gains, w_qkv, w_out, w_up, w_down, phone_len, prompt_len, target_len):
    params = tuple((member.astype(jnp.float32) for member in (gains, w_qkv, w_out, w_up, w_down)))
    span = tokens.shape[1] // 2

    def one_row(running, row_data):
        inputs, cot_row, phones, prompts, targets = row_data
        first = slot_layout(0, phones, prompts, targets, span)
        second = slot_layout(1, phones, prompts, targets, span)
        layout = tuple((jnp.concatenate([left_part, right_part]) for left_part, right_part in zip(first, second)))

        def forward(inputs_f, gains_f, qkv_f, out_f, up_f, down_f):
            return row_forward(inputs_f, gains_f, qkv_f, out_f, up_f, down_f, layout)
        result, pullback = jax.vjp(forward, inputs.astype(jnp.float32), *params)
        gradients = pullback(cot_row.astype(jnp.float32))
        updated = tuple((acc + new_term for acc, new_term in zip(running, gradients[1:])))
        return (updated, (result.astype(jnp.bfloat16), gradients[0]))
    zeros_start = tuple((jnp.zeros_like(member) for member in params))
    totals, outputs = lax.scan(one_row, zeros_start, (tokens, cotangent, phone_len, prompt_len, target_len))
    mixed_rows, grad_rows = outputs
    return (mixed_rows, grad_rows, totals[0], totals[1], totals[2], totals[3], totals[4])
```

```python
import jax
import jax.numpy as jnp
from jax import lax
from jax.sharding import PartitionSpec as P

HEADS = 16
HEAD_DIM = 64


epsilon = 1e-05


def passed_along(value, axis, steps):
    count = lax.axis_size(axis)
    leading, last = (max(0, -steps), min(count, count - steps))
    return lax.ppermute(value, axis, [(source, source + steps) for source in range(leading, last)])


def slot_layout(side_index, phones, prompts, targets, slot_count):
    lengths = jnp.where(side_index == 0, phones + prompts, targets)
    count = lengths.shape[0]
    seg_ends = jnp.stack([sum(lengths[i] for i in range(upto + 1)) for upto in range(count)])
    starts = seg_ends - lengths
    places = jnp.arange(slot_count, dtype=jnp.int32)
    segment = jnp.sum((places[:, None] >= seg_ends[None, :]).astype(jnp.int32), axis=1)
    onehot = (segment[:, None] == jnp.arange(lengths.shape[0], dtype=jnp.int32)[None, :]).astype(
        jnp.int32
    )
    within = places - jnp.sum(onehot * starts[None, :], axis=1)
    phone_here = jnp.sum(onehot * phones[None, :], axis=1)
    is_phone = jnp.logical_and(side_index == 0, within < phone_here)
    ordering = places + side_index * slot_count
    return (segment, is_phone, ordering)


def permitted(query_side, key_side):
    query_seg, query_phone, query_order = query_side
    key_seg, key_phone, key_order = key_side
    same_seg = query_seg[:, None] == key_seg[None, :]
    earlier = key_order[None, :] <= query_order[:, None]
    return same_seg & (key_phone[None, :] | jnp.logical_not(query_phone)[:, None] & earlier)


def normalize(values, gain_row):
    centred = values - jnp.mean(values, axis=-1, keepdims=True)
    spread = jnp.mean(centred * centred, axis=-1, keepdims=True)
    return centred * lax.rsqrt(spread + epsilon) * gain_row


def exact_gelu(values):
    return jax.nn.gelu(values, approximate=False)


def softmax_rows(query_piece, key_piece, allowed):
    scores = jnp.einsum(
        "qhd,khd->hqk", query_piece, key_piece, preferred_element_type=jnp.float32
    ) * HEAD_DIM ** (-0.5)
    scores = jnp.where(allowed[None], scores, -1e30)
    row_max = jnp.max(scores, axis=-1, keepdims=True)
    exponents = jnp.exp(scores - row_max)
    return exponents / jnp.sum(exponents, axis=-1, keepdims=True)


def shards(tokens, cotangent, gains, w_qkv, w_out, w_up, w_down, phone_len, prompt_len, target_len):
    slot_count = tokens.shape[1]
    model_width = tokens.shape[2]
    inputs = tokens[0].astype(jnp.float32)
    side_index = lax.axis_index("pair")
    paired = (
        lax.all_gather(gains, "pair", axis=1, tiled=True),
        lax.all_gather(w_qkv, "pair", axis=1, tiled=True),
        lax.all_gather(w_out, "pair", axis=1, tiled=True),
        lax.all_gather(w_up, "pair", axis=1, tiled=True),
        lax.all_gather(w_down, "pair", axis=1, tiled=True),
    )
    gain_all, qkv_all, out_all, up_all, down_all = (
        lax.all_gather(paired[0], "rows", axis=0, tiled=True),
        lax.all_gather(paired[1], "rows", axis=0, tiled=True),
        lax.all_gather(paired[2], "rows", axis=0, tiled=True),
        lax.all_gather(paired[3], "rows", axis=0, tiled=True),
        lax.all_gather(paired[4], "rows", axis=0, tiled=True),
    )
    gain_first = gain_all[:, 0].astype(jnp.float32)
    gain_second = gain_all[:, 1].astype(jnp.float32)
    phones = phone_len[0]
    prompts = prompt_len[0]
    targets = target_len[0]
    own_layout = slot_layout(side_index, phones, prompts, targets, slot_count)
    far_layout = slot_layout(0, phones, prompts, targets, slot_count)
    key_layout = tuple(
        (
            jnp.concatenate([far_part, own_part])
            for far_part, own_part in zip(far_layout, own_layout)
        )
    )
    far_live = jnp.concatenate(
        [jnp.full((slot_count,), side_index == 1), jnp.ones((slot_count,), dtype=bool)]
    )
    normed_in, norm_first_back = jax.vjp(normalize, inputs, gain_first)
    normed_low = normed_in.astype(jnp.bfloat16)
    projected = jnp.dot(normed_low, qkv_all, preferred_element_type=jnp.float32).astype(
        jnp.bfloat16
    )
    queries = projected[:, :model_width]
    near_pairs = projected[:, model_width:]
    far_pairs = passed_along(near_pairs, "pair", 1)
    key_value = jnp.concatenate([far_pairs, near_pairs], axis=0)
    block_rows = min(512, slot_count)
    per_group = min(4, HEADS)
    group_width = per_group * HEAD_DIM
    groups = HEADS // per_group
    steps_total = slot_count // block_rows * groups
    key_count = 2 * slot_count

    def piece_of(item_index):
        row_start = item_index // groups * block_rows
        col_start = item_index % groups * group_width
        query_piece = lax.dynamic_slice(
            queries, (row_start, col_start), (block_rows, group_width)
        ).reshape(block_rows, per_group, HEAD_DIM)
        key_piece = lax.dynamic_slice(key_value, (0, col_start), (key_count, group_width)).reshape(
            key_count, per_group, HEAD_DIM
        )
        value_piece = lax.dynamic_slice(
            key_value, (0, model_width + col_start), (key_count, group_width)
        ).reshape(key_count, per_group, HEAD_DIM)
        query_layout = tuple((member for member in own_layout))
        allowed = permitted(query_layout, key_layout) & far_live[None, :]
        attn_probs = softmax_rows(query_piece, key_piece, allowed)
        return (row_start, col_start, query_piece, key_piece, value_piece, attn_probs)

    def forward_step(item_index, attended):
        row_start, col_start, query_piece, key_piece, value_piece, attn_probs = piece_of(item_index)
        head_mix = jnp.einsum(
            "hqk,khd->qhd",
            attn_probs.astype(jnp.bfloat16),
            value_piece,
            preferred_element_type=jnp.float32,
        )
        return lax.dynamic_update_slice(
            attended, head_mix.reshape(block_rows, group_width), (row_start, col_start)
        )

    attended = lax.fori_loop(
        0, steps_total, forward_step, jnp.zeros((slot_count, model_width), jnp.float32)
    )
    attended_low = attended.astype(jnp.bfloat16)
    middle = inputs + jnp.dot(attended_low, out_all, preferred_element_type=jnp.float32)
    normed_mid, norm_second_back = jax.vjp(normalize, middle, gain_second)
    normed_mid_low = normed_mid.astype(jnp.bfloat16)
    pre_act = jnp.dot(normed_mid_low, up_all, preferred_element_type=jnp.float32)
    activated, gelu_back = jax.vjp(exact_gelu, pre_act)
    activated_low = activated.astype(jnp.bfloat16)
    result = middle + jnp.dot(activated_low, down_all, preferred_element_type=jnp.float32)
    mixed_out = result.astype(jnp.bfloat16)[None]
    qkv_back, out_back, up_back, down_back = (qkv_all, out_all, up_all, down_all)
    grad_result = cotangent[0]
    grad_down = jnp.dot(activated_low.T, grad_result, preferred_element_type=jnp.float32)
    grad_act = jnp.dot(grad_result, down_back.T, preferred_element_type=jnp.float32)
    grad_pre = gelu_back(grad_act)[0].astype(jnp.bfloat16)
    grad_up = jnp.dot(normed_mid_low.T, grad_pre, preferred_element_type=jnp.float32)
    grad_normed_mid = jnp.dot(grad_pre, up_back.T, preferred_element_type=jnp.float32)
    grad_middle_norm, grad_gain_second = norm_second_back(grad_normed_mid)
    grad_middle = grad_result.astype(jnp.float32) + grad_middle_norm
    grad_branch = grad_middle.astype(jnp.bfloat16)
    grad_out = jnp.dot(attended_low.T, grad_branch, preferred_element_type=jnp.float32)
    grad_attended = jnp.dot(grad_branch, out_back.T, preferred_element_type=jnp.float32).astype(
        jnp.bfloat16
    )

    def backward_step(item_index, running):
        grad_queries, grad_pairs = running
        row_start, col_start, query_piece, key_piece, value_piece, attn_probs = piece_of(item_index)
        grad_piece = lax.dynamic_slice(
            grad_attended, (row_start, col_start), (block_rows, group_width)
        ).reshape(block_rows, per_group, HEAD_DIM)
        grad_probs = jnp.einsum(
            "qhd,khd->hqk", grad_piece, value_piece, preferred_element_type=jnp.float32
        )
        centre = jnp.sum(grad_probs * attn_probs, axis=-1, keepdims=True)
        grad_scores = (attn_probs * (grad_probs - centre)).astype(jnp.bfloat16)
        score_scale = HEAD_DIM ** (-0.5)
        query_grad = (
            jnp.einsum("hqk,khd->qhd", grad_scores, key_piece, preferred_element_type=jnp.float32)
            * score_scale
        )
        key_grad = (
            jnp.einsum("hqk,qhd->khd", grad_scores, query_piece, preferred_element_type=jnp.float32)
            * score_scale
        )
        value_grad = jnp.einsum(
            "hqk,qhd->khd",
            attn_probs.astype(jnp.bfloat16),
            grad_piece,
            preferred_element_type=jnp.float32,
        )
        grad_queries = lax.dynamic_update_slice(
            grad_queries, query_grad.reshape(block_rows, group_width), (row_start, col_start)
        )
        key_old = lax.dynamic_slice(grad_pairs, (0, col_start), (key_count, group_width))
        grad_pairs = lax.dynamic_update_slice(
            grad_pairs, key_old + key_grad.reshape(key_count, group_width), (0, col_start)
        )
        value_old = lax.dynamic_slice(
            grad_pairs, (0, model_width + col_start), (key_count, group_width)
        )
        grad_pairs = lax.dynamic_update_slice(
            grad_pairs,
            value_old + value_grad.reshape(key_count, group_width),
            (0, model_width + col_start),
        )
        return (grad_queries, grad_pairs)

    start_state = (
        jnp.zeros((slot_count, model_width), jnp.float32),
        jnp.zeros((key_count, 2 * model_width), jnp.float32),
    )
    grad_queries, grad_pairs = lax.fori_loop(0, steps_total, backward_step, start_state)
    returned = passed_along(grad_pairs[:slot_count].astype(jnp.bfloat16), "pair", -1).astype(
        jnp.float32
    )
    grad_near = (grad_pairs[slot_count:] + returned).astype(jnp.bfloat16)
    grad_projected = jnp.concatenate([grad_queries.astype(jnp.bfloat16), grad_near], axis=1)
    grad_qkv = jnp.dot(normed_low.T, grad_projected, preferred_element_type=jnp.float32)
    grad_normed_in = jnp.dot(grad_projected, qkv_back.T, preferred_element_type=jnp.float32)
    grad_inputs_norm, grad_gain_first = norm_first_back(grad_normed_in)
    grad_tokens = (grad_middle + grad_inputs_norm)[None]
    grad_gains = jnp.stack([grad_gain_first, grad_gain_second], axis=1)
    strips = (
        lax.psum_scatter(grad_gains, "rows", scatter_dimension=0, tiled=True),
        lax.psum_scatter(grad_qkv.astype(jnp.bfloat16), "rows", scatter_dimension=0, tiled=True),
        lax.psum_scatter(grad_out.astype(jnp.bfloat16), "rows", scatter_dimension=0, tiled=True),
        lax.psum_scatter(grad_up.astype(jnp.bfloat16), "rows", scatter_dimension=0, tiled=True),
        lax.psum_scatter(grad_down.astype(jnp.bfloat16), "rows", scatter_dimension=0, tiled=True),
    )
    owned = (
        lax.psum_scatter(
            strips[0].astype(jnp.bfloat16), "pair", scatter_dimension=1, tiled=True
        ).astype(jnp.float32),
        lax.psum_scatter(
            strips[1].astype(jnp.bfloat16), "pair", scatter_dimension=1, tiled=True
        ).astype(jnp.float32),
        lax.psum_scatter(
            strips[2].astype(jnp.bfloat16), "pair", scatter_dimension=1, tiled=True
        ).astype(jnp.float32),
        lax.psum_scatter(
            strips[3].astype(jnp.bfloat16), "pair", scatter_dimension=1, tiled=True
        ).astype(jnp.float32),
        lax.psum_scatter(
            strips[4].astype(jnp.bfloat16), "pair", scatter_dimension=1, tiled=True
        ).astype(jnp.float32),
    )
    return (mixed_out, grad_tokens, owned[0], owned[1], owned[2], owned[3], owned[4])


def solution(mesh):
    return jax.shard_map(
        shards,
        mesh=mesh,
        in_specs=(
            P("rows", "pair", None),
            P("rows", "pair", None),
            P("rows", "pair"),
            P("rows", "pair"),
            P("rows", "pair"),
            P("rows", "pair"),
            P("rows", "pair"),
            P("rows", None),
            P("rows", None),
            P("rows", None),
        ),
        out_specs=(
            P("rows", "pair", None),
            P("rows", "pair", None),
            P("rows", "pair"),
            P("rows", "pair"),
            P("rows", "pair"),
            P("rows", "pair"),
            P("rows", "pair"),
        ),
        check_vma=False,
    )
```

```python
import functools

import jax
import jax.numpy as jnp
from jax import lax
from jax.experimental import pallas as pl
from jax.experimental.pallas import tpu as pltpu
from jax.sharding import PartitionSpec as P

HEADS = 16
HEAD_DIM = 64


epsilon = 1e-05


def passed_along(value, axis, steps):
    count = lax.axis_size(axis)
    leading, last = (max(0, -steps), min(count, count - steps))
    return lax.ppermute(value, axis, [(source, source + steps) for source in range(leading, last)])


def slot_layout(side_index, phones, prompts, targets, slot_count):
    lengths = jnp.where(side_index == 0, phones + prompts, targets)
    count = lengths.shape[0]
    seg_ends = jnp.stack([sum(lengths[i] for i in range(upto + 1)) for upto in range(count)])
    starts = seg_ends - lengths
    places = jnp.arange(slot_count, dtype=jnp.int32)
    segment = jnp.sum((places[:, None] >= seg_ends[None, :]).astype(jnp.int32), axis=1)
    onehot = (segment[:, None] == jnp.arange(lengths.shape[0], dtype=jnp.int32)[None, :]).astype(
        jnp.int32
    )
    within = places - jnp.sum(onehot * starts[None, :], axis=1)
    phone_here = jnp.sum(onehot * phones[None, :], axis=1)
    is_phone = jnp.logical_and(side_index == 0, within < phone_here)
    ordering = places + side_index * slot_count
    return (segment, is_phone, ordering)


def permitted(query_side, key_side):
    query_seg, query_phone, query_order = query_side
    key_seg, key_phone, key_order = key_side
    same_seg = query_seg[:, None] == key_seg[None, :]
    earlier = key_order[None, :] <= query_order[:, None]
    return same_seg & (key_phone[None, :] | jnp.logical_not(query_phone)[:, None] & earlier)


def normalize(values, gain_row):
    centred = values - jnp.mean(values, axis=-1, keepdims=True)
    spread = jnp.mean(centred * centred, axis=-1, keepdims=True)
    return centred * lax.rsqrt(spread + epsilon) * gain_row


def exact_gelu(values):
    return jax.nn.gelu(values, approximate=False)


def softmax_rows(query_piece, key_piece, allowed):
    scores = jnp.einsum(
        "qhd,khd->hqk", query_piece, key_piece, preferred_element_type=jnp.float32
    ) * HEAD_DIM ** (-0.5)
    scores = jnp.where(allowed[None], scores, -1e30)
    row_max = jnp.max(scores, axis=-1, keepdims=True)
    exponents = jnp.exp(scores - row_max)
    return exponents / jnp.sum(exponents, axis=-1, keepdims=True)


def shards(tokens, cotangent, gains, w_qkv, w_out, w_up, w_down, phone_len, prompt_len, target_len):
    slot_count = tokens.shape[1]
    model_width = tokens.shape[2]
    inputs = tokens[0].astype(jnp.float32)
    side_index = lax.axis_index("pair")
    paired = (
        lax.all_gather(gains, "pair", axis=1, tiled=True),
        lax.all_gather(w_qkv, "pair", axis=1, tiled=True),
        lax.all_gather(w_out, "pair", axis=1, tiled=True),
        lax.all_gather(w_up, "pair", axis=1, tiled=True),
        lax.all_gather(w_down, "pair", axis=1, tiled=True),
    )
    gain_all, qkv_all, out_all, up_all, down_all = (
        lax.all_gather(paired[0], "rows", axis=0, tiled=True),
        lax.all_gather(paired[1], "rows", axis=0, tiled=True),
        lax.all_gather(paired[2], "rows", axis=0, tiled=True),
        lax.all_gather(paired[3], "rows", axis=0, tiled=True),
        lax.all_gather(paired[4], "rows", axis=0, tiled=True),
    )
    gain_first = gain_all[:, 0].astype(jnp.float32)
    gain_second = gain_all[:, 1].astype(jnp.float32)
    phones = phone_len[0]
    prompts = prompt_len[0]
    targets = target_len[0]
    own_layout = slot_layout(side_index, phones, prompts, targets, slot_count)
    far_layout = slot_layout(0, phones, prompts, targets, slot_count)
    key_layout = tuple(
        (
            jnp.concatenate([far_part, own_part])
            for far_part, own_part in zip(far_layout, own_layout)
        )
    )
    far_live = jnp.concatenate(
        [jnp.full((slot_count,), side_index == 1), jnp.ones((slot_count,), dtype=bool)]
    )
    normed_in, norm_first_back = jax.vjp(normalize, inputs, gain_first)
    normed_low = normed_in.astype(jnp.bfloat16)
    projected = jnp.dot(normed_low, qkv_all, preferred_element_type=jnp.float32).astype(
        jnp.bfloat16
    )
    queries = projected[:, :model_width]
    near_pairs = projected[:, model_width:]
    far_pairs = passed_along(near_pairs, "pair", 1)
    key_value = jnp.concatenate([far_pairs, near_pairs], axis=0)
    block_rows = min(512, slot_count)
    per_group = min(4, HEADS)
    group_width = per_group * HEAD_DIM
    groups = HEADS // per_group
    steps_total = slot_count // block_rows * groups
    key_count = 2 * slot_count

    def piece_of(item_index):
        row_start = item_index // groups * block_rows
        col_start = item_index % groups * group_width
        query_piece = lax.dynamic_slice(
            queries, (row_start, col_start), (block_rows, group_width)
        ).reshape(block_rows, per_group, HEAD_DIM)
        key_piece = lax.dynamic_slice(key_value, (0, col_start), (key_count, group_width)).reshape(
            key_count, per_group, HEAD_DIM
        )
        value_piece = lax.dynamic_slice(
            key_value, (0, model_width + col_start), (key_count, group_width)
        ).reshape(key_count, per_group, HEAD_DIM)
        query_layout = tuple((member for member in own_layout))
        allowed = permitted(query_layout, key_layout) & far_live[None, :]
        attn_probs = softmax_rows(query_piece, key_piece, allowed)
        return (row_start, col_start, query_piece, key_piece, value_piece, attn_probs)

    def forward_step(item_index, attended):
        row_start, col_start, query_piece, key_piece, value_piece, attn_probs = piece_of(item_index)
        head_mix = jnp.einsum(
            "hqk,khd->qhd",
            attn_probs.astype(jnp.bfloat16),
            value_piece,
            preferred_element_type=jnp.float32,
        )
        return lax.dynamic_update_slice(
            attended, head_mix.reshape(block_rows, group_width), (row_start, col_start)
        )

    attended = lax.fori_loop(
        0, steps_total, forward_step, jnp.zeros((slot_count, model_width), jnp.float32)
    )
    attended_low = attended.astype(jnp.bfloat16)
    middle = inputs + jnp.dot(attended_low, out_all, preferred_element_type=jnp.float32)
    normed_mid, norm_second_back = jax.vjp(normalize, middle, gain_second)
    normed_mid_low = normed_mid.astype(jnp.bfloat16)
    pre_act = jnp.dot(normed_mid_low, up_all, preferred_element_type=jnp.float32)
    activated, gelu_back = jax.vjp(exact_gelu, pre_act)
    activated_low = activated.astype(jnp.bfloat16)
    result = middle + jnp.dot(activated_low, down_all, preferred_element_type=jnp.float32)
    mixed_out = result.astype(jnp.bfloat16)[None]
    qkv_back, out_back, up_back, down_back = (qkv_all, out_all, up_all, down_all)
    grad_result = cotangent[0]
    grad_down = jnp.dot(activated_low.T, grad_result, preferred_element_type=jnp.float32)
    grad_act = jnp.dot(grad_result, down_back.T, preferred_element_type=jnp.float32)
    grad_pre = gelu_back(grad_act)[0].astype(jnp.bfloat16)
    grad_up = jnp.dot(normed_mid_low.T, grad_pre, preferred_element_type=jnp.float32)
    grad_normed_mid = jnp.dot(grad_pre, up_back.T, preferred_element_type=jnp.float32)
    grad_middle_norm, grad_gain_second = norm_second_back(grad_normed_mid)
    grad_middle = grad_result.astype(jnp.float32) + grad_middle_norm
    grad_branch = grad_middle.astype(jnp.bfloat16)
    grad_out = jnp.dot(attended_low.T, grad_branch, preferred_element_type=jnp.float32)
    grad_attended = jnp.dot(grad_branch, out_back.T, preferred_element_type=jnp.float32).astype(
        jnp.bfloat16
    )

    def backward_step(item_index, running):
        grad_queries, grad_pairs = running
        row_start, col_start, query_piece, key_piece, value_piece, attn_probs = piece_of(item_index)
        grad_piece = lax.dynamic_slice(
            grad_attended, (row_start, col_start), (block_rows, group_width)
        ).reshape(block_rows, per_group, HEAD_DIM)
        grad_probs = jnp.einsum(
            "qhd,khd->hqk", grad_piece, value_piece, preferred_element_type=jnp.float32
        )
        centre = jnp.sum(grad_probs * attn_probs, axis=-1, keepdims=True)
        grad_scores = (attn_probs * (grad_probs - centre)).astype(jnp.bfloat16)
        score_scale = HEAD_DIM ** (-0.5)
        query_grad = (
            jnp.einsum("hqk,khd->qhd", grad_scores, key_piece, preferred_element_type=jnp.float32)
            * score_scale
        )
        key_grad = (
            jnp.einsum("hqk,qhd->khd", grad_scores, query_piece, preferred_element_type=jnp.float32)
            * score_scale
        )
        value_grad = jnp.einsum(
            "hqk,qhd->khd",
            attn_probs.astype(jnp.bfloat16),
            grad_piece,
            preferred_element_type=jnp.float32,
        )
        grad_queries = lax.dynamic_update_slice(
            grad_queries, query_grad.reshape(block_rows, group_width), (row_start, col_start)
        )
        key_old = lax.dynamic_slice(grad_pairs, (0, col_start), (key_count, group_width))
        grad_pairs = lax.dynamic_update_slice(
            grad_pairs, key_old + key_grad.reshape(key_count, group_width), (0, col_start)
        )
        value_old = lax.dynamic_slice(
            grad_pairs, (0, model_width + col_start), (key_count, group_width)
        )
        grad_pairs = lax.dynamic_update_slice(
            grad_pairs,
            value_old + value_grad.reshape(key_count, group_width),
            (0, model_width + col_start),
        )
        return (grad_queries, grad_pairs)

    start_state = (
        jnp.zeros((slot_count, model_width), jnp.float32),
        jnp.zeros((key_count, 2 * model_width), jnp.float32),
    )
    grad_queries, grad_pairs = lax.fori_loop(0, steps_total, backward_step, start_state)
    returned = passed_along(grad_pairs[:slot_count].astype(jnp.bfloat16), "pair", -1).astype(
        jnp.float32
    )
    grad_near = (grad_pairs[slot_count:] + returned).astype(jnp.bfloat16)
    grad_projected = jnp.concatenate([grad_queries.astype(jnp.bfloat16), grad_near], axis=1)
    grad_qkv = jnp.dot(normed_low.T, grad_projected, preferred_element_type=jnp.float32)
    grad_normed_in = jnp.dot(grad_projected, qkv_back.T, preferred_element_type=jnp.float32)
    grad_inputs_norm, grad_gain_first = norm_first_back(grad_normed_in)
    grad_tokens = (grad_middle + grad_inputs_norm)[None]
    grad_gains = jnp.stack([grad_gain_first, grad_gain_second], axis=1)
    strips = (
        lax.psum_scatter(grad_gains, "rows", scatter_dimension=0, tiled=True),
        lax.psum_scatter(grad_qkv.astype(jnp.bfloat16), "rows", scatter_dimension=0, tiled=True),
        lax.psum_scatter(grad_out.astype(jnp.bfloat16), "rows", scatter_dimension=0, tiled=True),
        lax.psum_scatter(grad_up.astype(jnp.bfloat16), "rows", scatter_dimension=0, tiled=True),
        lax.psum_scatter(grad_down.astype(jnp.bfloat16), "rows", scatter_dimension=0, tiled=True),
    )
    owned = (
        lax.psum_scatter(
            strips[0].astype(jnp.bfloat16), "pair", scatter_dimension=1, tiled=True
        ).astype(jnp.float32),
        lax.psum_scatter(
            strips[1].astype(jnp.bfloat16), "pair", scatter_dimension=1, tiled=True
        ).astype(jnp.float32),
        lax.psum_scatter(
            strips[2].astype(jnp.bfloat16), "pair", scatter_dimension=1, tiled=True
        ).astype(jnp.float32),
        lax.psum_scatter(
            strips[3].astype(jnp.bfloat16), "pair", scatter_dimension=1, tiled=True
        ).astype(jnp.float32),
        lax.psum_scatter(
            strips[4].astype(jnp.bfloat16), "pair", scatter_dimension=1, tiled=True
        ).astype(jnp.float32),
    )
    return (mixed_out, grad_tokens, owned[0], owned[1], owned[2], owned[3], owned[4])


LINE = 4
HALF = 512
NEG = -1e30
bf16 = jnp.bfloat16
f32 = jnp.float32
VMEM_LIMIT = 56 * 1024 * 1024


def params(limit=VMEM_LIMIT):
    return pltpu.CompilerParams(vmem_limit_bytes=limit)


def cost(flops, nbytes, trans=0):
    return pl.CostEstimate(flops=flops // 64, bytes_accessed=nbytes // 64, transcendentals=trans // 64)


def whole():
    return pl.BlockSpec(memory_space=pltpu.VMEM)


def hbm():
    return pl.BlockSpec(memory_space=pl.ANY)


def dot(a, b, contract):
    return lax.dot_general(a, b, ((contract[:1], contract[1:]), ((), ())), preferred_element_type=f32)


def row_pairs(target):
    pairs = []
    for r in range(LINE * 4):
        z, x, c = target(r // 4, r // 2 % 2, r % 2)
        pairs.append((r, z % LINE * 4 + x * 2 + c))
    return pairs


def shift_z(v, k):
    return lax.ppermute(v, "rows", row_pairs(lambda z, x, c: (z + k, x, c)))


def swap_x(v):
    return lax.ppermute(v, "rows", row_pairs(lambda z, x, c: (z, 1 - x, c)))


def swap_c(v):
    return lax.ppermute(v, "rows", row_pairs(lambda z, x, c: (z, x, 1 - c)))


def swap_y(v):
    return lax.ppermute(v, "pair", [(0, 1), (1, 0)])


def along_line(shard):
    return jnp.stack([shard] + [shift_z(shard, k) for k in range(1, LINE)])


def summed_line(parts):
    total = parts[0].astype(f32)
    for k in range(1, LINE):
        total = total + shift_z(parts[k], k).astype(f32)
    return total


def plus(a, b):
    return (a.astype(f32) + b.astype(f32)).astype(bf16)


def after(value, *others):
    return lax.optimization_barrier((value, others))[0]


def place_of(info, z_abs, x_abs):
    dx = lax.rem(info[1] + x_abs, 2)
    return dx, lax.rem(info[0] - z_abs + LINE, LINE), lax.rem(z_abs - info[0] + LINE, LINE)


def weight_copies(info, a_ref, b_ref, w_ref, sems, halves, start_col=0, cols=None):
    rows = a_ref.shape[1]
    cols = cols or a_ref.shape[2]
    out = []
    for y_abs in range(halves):
        out.append([])
        for z_abs in range(LINE):
            group = []
            for x_abs in range(2):
                dx, dz, _ = place_of(info, z_abs, x_abs)
                index = dx * LINE + dz
                if halves == 2:
                    index = index + lax.rem(info[3] + y_abs, 2) * 2 * LINE
                for own in (0, 1):
                    core = info[2] if own == 0 else 1 - info[2]
                    start = pl.multiple_of((z_abs * 2 + x_abs) * 2 * rows + core * rows, rows)
                    group.append(
                        pltpu.make_async_copy(
                            (a_ref, b_ref)[own].at[index, :, pl.ds(start_col, cols)],
                            w_ref.at[pl.ds(start, rows), pl.ds(y_abs * cols, cols)],
                            sems.at[(y_abs * LINE * 2 + z_abs * 2 + x_abs) * 2 + own],
                        )
                    )
            out[-1].append(group)
    return out


def start(copies):
    for y in copies:
        for group in y:
            for c in group:
                c.start()


def wait(copies, y=None, z=None):
    for i, by_z in enumerate(copies):
        for j, group in enumerate(by_z):
            if y in (None, i) and z in (None, j):
                for c in group:
                    c.wait()


def project_kernel(info, xo_ref, xt_ref, a_ref, b_ref, out_ref, g_ref, w_ref, gcol_ref, nin_ref, sems):
    copies = weight_copies(info, a_ref, b_ref, w_ref, sems, 1, 0, 1536)
    gains = weight_copies(info, a_ref, b_ref, gcol_ref, sems.at[pl.ds(16, 16)], 1, 1536, 128)
    start(gains)
    start(copies)
    wait(gains)
    both = gcol_ref[...].T.astype(f32)[:2]
    g_ref[...] = both
    side = info[3]
    for part, x_ref in ((0, xo_ref), (1, xt_ref)):
        at = side if part == 0 else 1 - side
        tokens = pl.ds(pl.multiple_of(at * HALF, HALF), HALF)
        nin_ref[tokens, :] = (centred(x_ref[...].astype(f32))[0] * both[:1]).astype(bf16)
        if part == 0:
            wait(copies)
        for n in range(2):
            cols = slice(n * 768, n * 768 + 768)
            out_ref[tokens, cols] = dot(nin_ref[tokens, :], w_ref[:, cols], (1, 0)).astype(bf16)


def project(info, x_own, x_other, a, b):
    block = lambda *shape: pl.BlockSpec(shape, lambda i, s: (0,) * len(shape))
    return pl.pallas_call(
        project_kernel,
        grid_spec=pltpu.PrefetchScalarGridSpec(
            num_scalar_prefetch=1,
            grid=(1,),
            in_specs=[block(HALF, 1024), block(HALF, 1024), hbm(), hbm()],
            out_specs=[block(1024, 1536), block(2, 1024)],
            scratch_shapes=[
                pltpu.VMEM((1024, 1536), bf16),
                pltpu.VMEM((1024, 128), bf16),
                pltpu.VMEM((1024, 1024), bf16),
                pltpu.SemaphoreType.DMA((32,)),
            ],
        ),
        out_shape=[jax.ShapeDtypeStruct((1024, 1536), bf16), jax.ShapeDtypeStruct((2, 1024), f32)],
        compiler_params=params(),
        cost_estimate=cost(2 * 1024 * 1024 * 1536, 8 << 20),
        name="project",
    )(info, x_own, x_other, a, b)


TILES = ((0, 512), (256, 512), (512, 768), (768, 1024))


def own_lanes(v, head):
    lane = lax.broadcasted_iota(jnp.int32, v.shape, 1)
    return jnp.where((lane >= 64) if head else (lane < 64), v, jnp.zeros_like(v))


def attend_kernel(info, q_ref, k_ref, v_ref, bias_ref, keep_ref, send_ref, lse_ref):
    side = info[3]
    v_t = v_ref[...].T
    for tile, (start, seen) in enumerate(TILES):
        q_tile = q_ref[start : start + 256, :] * jnp.asarray(0.125, bf16)
        pieces = []
        for head in range(2):
            s = dot(k_ref[:seen, :], own_lanes(q_tile, head), (1, 1))
            s = s + bias_ref[:seen, start : start + 256]
            top = jnp.max(s, axis=0, keepdims=True)
            p = jnp.exp(s - top)
            total = jnp.sum(p, axis=0, keepdims=True)
            lse_ref[0, head : head + 1, start : start + 256] = top + jnp.log(total)
            mixed = dot(v_t[head * 64 : head * 64 + 64, :seen], p.astype(bf16), (1, 0))
            pieces.append(mixed * (1.0 / total))
        done = jnp.concatenate(pieces, axis=0).T.astype(bf16)
        half, row = tile // 2, tile % 2 * 256

        @pl.when(side == half)
        def _():
            keep_ref[row : row + 256, :] = done

        @pl.when(side != half)
        def _():
            send_ref[row : row + 256, :] = done


def head_parts(group):
    return [pl.BlockSpec((1024, 128), lambda h, s, j=j: (0, 6 * group + 2 * j + h)) for j in range(3)]


def attend(info, projected, bias, group):
    piece = pl.BlockSpec((HALF, 128), lambda h, s: (0, h))
    return pl.pallas_call(
        attend_kernel,
        grid_spec=pltpu.PrefetchScalarGridSpec(
            num_scalar_prefetch=1,
            grid=(2,),
            in_specs=[*head_parts(group), pl.BlockSpec((1024, 1024), lambda h, s: (0, 0))],
            out_specs=[piece, piece, pl.BlockSpec((1, 2, 1024), lambda h, s: (h, 0, 0))],
        ),
        out_shape=[
            jax.ShapeDtypeStruct((HALF, 256), bf16),
            jax.ShapeDtypeStruct((HALF, 256), bf16),
            jax.ShapeDtypeStruct((2, 2, 1024), f32),
        ],
        compiler_params=params(),
        cost_estimate=cost(4 * 1024 * 768 * 64 * 4 * 4, 8 << 20, 4 * 768 * 1024),
        name="attend",
    )(info, projected, projected, projected, bias)


def attend_back_kernel(info, q_ref, k_ref, v_ref, bias_ref, lse_ref, keep_ref, send_ref, out_ref, dk_ref, dv_ref):
    side = info[3]
    pair = pl.program_id(0)
    k_t = k_ref[...].T
    dk_ref[...] = jnp.zeros_like(dk_ref)
    dv_ref[...] = jnp.zeros_like(dv_ref)
    for tile, (start, seen) in enumerate(TILES):
        half, row = tile // 2, tile % 2 * 256
        q_tile = q_ref[start : start + 256, :] * jnp.asarray(0.125, bf16)
        g_tile = jnp.where(side == half, keep_ref[row : row + 256, :], send_ref[row : row + 256, :])
        pieces = []
        for head in range(2):
            q_head = own_lanes(q_tile, head)
            g_head = own_lanes(g_tile, head)
            s = dot(k_ref[:seen, :], q_head, (1, 1))
            p = jnp.exp(s + bias_ref[:seen, start : start + 256] - lse_ref[0, head : head + 1, start : start + 256])
            dp = dot(v_ref[:seen, :], g_head, (1, 1))
            centre = jnp.sum(p * dp, axis=0, keepdims=True)
            ds = (p * (dp - centre)).astype(bf16)
            dv_ref[:seen, :] += dot(p.astype(bf16), g_head, (1, 0))
            dk_ref[:seen, :] += dot(ds, q_head, (1, 0))
            pieces.append(dot(k_t[head * 64 : head * 64 + 64, :seen], ds, (1, 0)) * 0.125)
        cols = pl.ds(pl.multiple_of(pair * 128, 128), 128)
        out_ref[start : start + 256, cols] = jnp.concatenate(pieces, axis=0).T.astype(bf16)
    out_ref[:, pl.ds(pl.multiple_of(256 + pair * 128, 128), 128)] = dk_ref[...].astype(bf16)
    out_ref[:, pl.ds(pl.multiple_of(512 + pair * 128, 128), 128)] = dv_ref[...].astype(bf16)


def attend_back(info, projected, bias, lse, keep, other, group):
    piece = pl.BlockSpec((HALF, 128), lambda h, s: (0, h))
    return pl.pallas_call(
        attend_back_kernel,
        grid_spec=pltpu.PrefetchScalarGridSpec(
            num_scalar_prefetch=1,
            grid=(2,),
            in_specs=[
                *head_parts(group),
                pl.BlockSpec((1024, 1024), lambda h, s: (0, 0)),
                pl.BlockSpec((1, 2, 1024), lambda h, s: (h, 0, 0)),
                piece,
                piece,
            ],
            out_specs=pl.BlockSpec((1024, 768), lambda h, s: (0, 0)),
            scratch_shapes=[pltpu.VMEM((1024, 128), f32), pltpu.VMEM((1024, 128), f32)],
        ),
        out_shape=jax.ShapeDtypeStruct((1024, 768), bf16),
        compiler_params=params(),
        cost_estimate=cost(10 * 1024 * 768 * 64 * 4 * 4, 10 << 20, 4 * 768 * 1024),
        name="attend_back",
    )(info, projected, projected, projected, bias, lse, keep, other)


def centred(v):
    off = v - jnp.mean(v, axis=-1, keepdims=True)
    scale = lax.rsqrt(jnp.mean(off * off, axis=-1, keepdims=True) + epsilon)
    return off * scale, scale


def out_kernel(
    info, x_ref, k0, k1, g0, g1, a_ref, b_ref, g_ref, mid_ref, nm_ref, own_ref, oth_ref, w_ref, t_ref, sems
):
    side = info[3]
    copies = weight_copies(info, a_ref, b_ref, w_ref, sems, 2, 2048, 512)
    start(copies)
    for i, ref in enumerate((k0, k1, g0, g1)):
        at = (side if i < 2 else 1 - side) * HALF + i % 2 * 256
        t_ref[pl.ds(pl.multiple_of(at, 256), 256), :] = ref[...].T
    put_parities(info, t_ref, own_ref, oth_ref, 0)
    wait(copies)
    for half in range(2):
        cols = slice(half * 512, half * 512 + 512)
        branch = x_ref[:, cols].astype(f32)
        for i, ref in enumerate((k0, k1, g0, g1)):
            at = (side if i < 2 else 1 - side) * HALF + i % 2 * 256
            branch = branch + dot(ref[...], w_ref[pl.ds(pl.multiple_of(at, 256), 256), cols], (1, 0))
        mid_ref[:, cols] = branch
    normed = (centred(mid_ref[...])[0] * g_ref[1:]).astype(bf16)
    nm_ref[...] = normed
    t_ref[...] = normed.T
    put_parities(info, t_ref, own_ref, oth_ref, 1)


def put_parities(info, t_ref, own_ref, oth_ref, slot):
    for dx in range(2):
        for dz in range(LINE):
            chip = lax.rem(info[0] + dz, LINE) * 2 + lax.rem(info[1] + dx, 2)
            here = pl.multiple_of(chip * 128 + info[2] * 64, 64)
            there = pl.multiple_of(chip * 128 + (1 - info[2]) * 64, 64)
            own_ref[slot, dx * LINE + dz] = t_ref[pl.ds(here, 64), :]
            oth_ref[slot, dx * LINE + dz] = t_ref[pl.ds(there, 64), :]


def attention_out(info, x, keeps, gots, a, b, gain):
    block = lambda *shape: pl.BlockSpec(shape, lambda i, s: (0,) * len(shape))
    return pl.pallas_call(
        out_kernel,
        grid_spec=pltpu.PrefetchScalarGridSpec(
            num_scalar_prefetch=1,
            grid=(1,),
            in_specs=[block(HALF, 1024)] + [block(HALF, 256)] * 4 + [hbm(), hbm(), block(2, 1024)],
            out_specs=[block(HALF, 1024), block(HALF, 1024), block(2, 8, 64, HALF), block(2, 8, 64, HALF)],
            scratch_shapes=[
                pltpu.VMEM((1024, 1024), bf16),
                pltpu.VMEM((1024, HALF), bf16),
                pltpu.SemaphoreType.DMA((32,)),
            ],
        ),
        out_shape=[
            jax.ShapeDtypeStruct((HALF, 1024), f32),
            jax.ShapeDtypeStruct((HALF, 1024), bf16),
            jax.ShapeDtypeStruct((2, 8, 64, HALF), bf16),
            jax.ShapeDtypeStruct((2, 8, 64, HALF), bf16),
        ],
        compiler_params=params(),
        cost_estimate=cost(2 * 512 * 1024 * 1024, 8 << 20),
        name="attention_out",
    )(info, x, *keeps, *gots, a, b, gain)


def up_kernel(info, x_ref, a_ref, b_ref, act0_ref, act1_ref, slope0_ref, slope1_ref, w_ref, sems):
    step = pl.program_id(0)
    copies = weight_copies(info, a_ref, b_ref, w_ref, sems, 2, 0, 2048)

    @pl.when(step == 0)
    def _():
        start(copies)
        wait(copies, y=0)

    @pl.when(step == 2)
    def _():
        wait(copies, y=1)

    for x_abs in range(2):
        dx = lax.rem(info[1] + x_abs, 2)
        for own, act_ref, slope_ref in ((0, act0_ref, slope0_ref), (1, act1_ref, slope1_ref)):
            core = info[2] if own == 0 else 1 - info[2]
            cols = pl.ds(pl.multiple_of(step * 1024 + x_abs * 512 + core * 256, 256), 256)
            pre = dot(x_ref[...], w_ref[:, cols], (1, 0))
            below = 0.5 * (1.0 + lax.erf(pre * 0.7071067811865476))
            act_ref[dx] = (pre * below).astype(bf16)
            slope_ref[dx] = (below + pre * (0.3989422804014327 * jnp.exp(-0.5 * pre * pre))).astype(bf16)


def ff_tile():
    return pl.BlockSpec((2, HALF, 256), lambda n, s: (0, 0, place_of(s, n, 0)[2]))


def up(info, x, a, b):
    shape = jax.ShapeDtypeStruct((2, HALF, 1024), bf16)
    return pl.pallas_call(
        up_kernel,
        grid_spec=pltpu.PrefetchScalarGridSpec(
            num_scalar_prefetch=1,
            grid=(4,),
            in_specs=[pl.BlockSpec((HALF, 1024), lambda n, s: (0, 0)), hbm(), hbm()],
            out_specs=[ff_tile()] * 4,
            scratch_shapes=[pltpu.VMEM((1024, 4096), bf16), pltpu.SemaphoreType.DMA((32,))],
        ),
        out_shape=[shape] * 4,
        compiler_params=params(),
        cost_estimate=cost(2 * 512 * 1024 * 4096 * 2, 17 << 20, 512 * 4096),
        name="up",
    )(info, x, a, b)


def down_kernel(info, act0, act1, slope0, slope1, *refs):
    a, b = refs[:4], refs[4:8]
    cot_ref, mid_ref, out_ref, gp_ref, acc_ref = refs[8:]
    step = pl.program_id(0)
    side = info[3]
    mine = pl.ds(pl.multiple_of(side * 512, 512), 512)
    theirs = pl.ds(pl.multiple_of((1 - side) * 512, 512), 512)
    for dy in range(2):
        total = sum(
            dot(act[dx], shard[dx + 2 * dy][0], (1, 0)) for dx in range(2) for act, shard in ((act0, a), (act1, b))
        )

        @pl.when(step == 0)
        def _():
            acc_ref[dy] = total

        @pl.when(step > 0)
        def _():
            acc_ref[dy] += total

    for dx in range(2):
        for own, shard, slope in ((0, a, slope0), (1, b, slope1)):
            core = info[2] if own == 0 else 1 - info[2]
            back = dot(cot_ref[:, mine], shard[dx][0], (1, 1)) + dot(cot_ref[:, theirs], shard[dx + 2][0], (1, 1))
            cols = pl.ds(pl.multiple_of(lax.rem(info[1] + dx, 2) * 512 + core * 256, 256), 256)
            gp_ref[:, cols] = (back * slope[dx].astype(f32)).astype(bf16)

    @pl.when(step == 3)
    def _():
        out_ref[:, mine] = (mid_ref[:, mine] + acc_ref[0]).astype(bf16)
        out_ref[:, theirs] = (mid_ref[:, theirs] + acc_ref[1]).astype(bf16)


def down(info, acts, slopes, a, b, cot, mid):
    shards = [
        pl.BlockSpec((1, 256, 512), lambda n, s, xy=xy: (xy * LINE + place_of(s, n, 0)[1], 0, 0)) for xy in range(4)
    ]
    full = pl.BlockSpec((HALF, 1024), lambda n, s: (0, 0))
    return pl.pallas_call(
        down_kernel,
        grid_spec=pltpu.PrefetchScalarGridSpec(
            num_scalar_prefetch=1,
            grid=(4,),
            in_specs=[ff_tile()] * 4 + shards + shards + [full, full],
            out_specs=[full, pl.BlockSpec((HALF, 1024), lambda n, s: (0, n))],
            scratch_shapes=[pltpu.VMEM((2, HALF, 512), f32)],
        ),
        out_shape=[jax.ShapeDtypeStruct((HALF, 1024), bf16), jax.ShapeDtypeStruct((HALF, 4096), bf16)],
        compiler_params=params(),
        cost_estimate=cost(4 * 512 * 1024 * 4096, 25 << 20),
        name="down",
    )(info, *acts, *slopes, *[a] * 4, *[b] * 4, cot, mid)


def middle_back_kernel(
    info, gp_ref, a_ref, b_ref, cot_ref, mid_ref, g_ref, gm_ref, gb_ref, keep0, keep1, send0, send1, w_ref, wo_ref, e_ref, sems
):
    copies = weight_copies(info, a_ref, b_ref, w_ref, sems, 2, 0, 2048)
    more = weight_copies(info, a_ref, b_ref, wo_ref, sems.at[pl.ds(32, 32)], 2, 2048, 512)
    start(copies)
    start(more)
    for n in range(4):
        wait(copies, z=n)
        rows = slice(n * 256, n * 256 + 256)
        e_ref[:, rows] = dot(gp_ref[...], w_ref[rows, :], (1, 1))

    e = e_ref[...]
    n, scale = centred(mid_ref[...])
    eg = e * g_ref[1:]
    lean = eg - jnp.mean(eg, axis=-1, keepdims=True) - n * jnp.mean(eg * n, axis=-1, keepdims=True)
    grad = cot_ref[...].astype(f32) + scale * lean
    gm_ref[...] = grad
    low = grad.astype(bf16)
    gb_ref[...] = low
    wait(more)
    side = info[3]
    for i, out in enumerate((keep0, keep1, send0, send1)):
        at = (side if i < 2 else 1 - side) * HALF + i % 2 * 256
        out[...] = dot(low, wo_ref[pl.ds(pl.multiple_of(at, 256), 256), :], (1, 1)).astype(bf16)


def middle_back(info, gp, a, b, cot, mid, gain):
    block = lambda *shape: pl.BlockSpec(shape, lambda i, s: (0,) * len(shape))
    return pl.pallas_call(
        middle_back_kernel,
        grid_spec=pltpu.PrefetchScalarGridSpec(
            num_scalar_prefetch=1,
            grid=(1,),
            in_specs=[
                block(HALF, 4096),
                hbm(),
                hbm(),
                block(HALF, 1024),
                block(HALF, 1024),
                block(2, 1024),
            ],
            out_specs=[block(HALF, 1024), block(HALF, 1024)] + [block(HALF, 256)] * 4,
            scratch_shapes=[
                pltpu.VMEM((1024, 4096), bf16),
                pltpu.VMEM((1024, 1024), bf16),
                pltpu.VMEM((HALF, 1024), f32),
                pltpu.SemaphoreType.DMA((64,)),
            ],
        ),
        out_shape=[jax.ShapeDtypeStruct((HALF, 1024), f32), jax.ShapeDtypeStruct((HALF, 1024), bf16)]
        + [jax.ShapeDtypeStruct((HALF, 256), bf16)] * 4,
        compiler_params=params(),
        cost_estimate=cost(2 * 512 * 1024 * 5120, 20 << 20),
        name="middle_back",
    )(info, gp, a, b, cot, mid, gain)


def down_grad_kernel(info, l0_ref, r0_ref, l1_ref, r1_ref, far_a, far_b, beside, across, own, part_ref, sems):
    g = pl.program_id(0)
    total = (dot(l0_ref[...], r0_ref[0], (1, 0)) + dot(l1_ref[...], r1_ref[0], (1, 0))).astype(bf16)
    for dz in range(LINE):
        part_ref[g, dz] = total[:, dz * 256 : dz * 256 + 256]
    outs = (
        (0, part_ref.at[0, pl.ds(0, 2)], far_a, 0),
        (0, part_ref.at[0, pl.ds(2, 2)], far_b, 1),
        (1, part_ref.at[1], across, 2),
        (2, part_ref.at[2], beside, 3),
        (3, part_ref.at[3], own, 4),
    )
    for at, source, out, sem in outs:

        @pl.when(g == at)
        def _():
            pltpu.make_async_copy(source, out, sems.at[sem]).start()

    @pl.when(g == 3)
    def _():
        for _, source, out, sem in outs:
            pltpu.make_async_copy(source, out, sems.at[sem]).wait()


def down_grad(info, cot_t, act, cot_t_sib, act_sib):
    left = pl.BlockSpec((512, HALF), lambda g, s: (lax.rem(s[3] + 1 - g // 2, 2), 0))
    right = pl.BlockSpec((1, HALF, 1024), lambda g, s: (1 - lax.rem(g, 2), 0, 0))
    return pl.pallas_call(
        down_grad_kernel,
        grid_spec=pltpu.PrefetchScalarGridSpec(
            num_scalar_prefetch=1,
            grid=(4,),
            in_specs=[left, right, left, right],
            out_specs=[hbm()] * 5,
            scratch_shapes=[pltpu.VMEM((4, LINE, 512, 256), bf16), pltpu.SemaphoreType.DMA((5,))],
        ),
        out_shape=[jax.ShapeDtypeStruct((n, 512, 256), bf16) for n in (2, 2, 4, 4, 4)],
        compiler_params=params(),
        cost_estimate=cost(2 * 1024 * 1024 * 2048, 12 << 20),
        name="down_grad",
    )(info, cot_t, act, cot_t_sib, act_sib)


def up_grad_kernel(info, l0_ref, r0_ref, l1_ref, r1_ref, far_a, far_b, beside, across, own):
    g = pl.program_id(0)
    total = dot(l0_ref[...], r0_ref[...], (1, 0)) + dot(l1_ref[...], r1_ref[...], (1, 0))
    total = total.astype(bf16).reshape(8, 64, 1024)

    @pl.when(g < 2)
    def _():
        across[...] = total[:4]
        far_a[...] = total[4:6]
        far_b[...] = total[6:]

    @pl.when(g >= 2)
    def _():
        own[...] = total[:4]
        beside[...] = total[4:]


def up_grad(info, sides_t, gp, sides_t_sib, gp_sib):
    left = pl.BlockSpec((512, HALF), lambda g, s: (1, 0))
    right = pl.BlockSpec((HALF, 1024), lambda g, s: (0, lax.rem(s[3] + 1 - g // 2, 2) * 2 + lax.rem(g, 2)))
    outs = ((2, 0), (2, 0), (4, 2), (4, 0), (4, 2))

    def spec(n, first):
        return pl.BlockSpec((n, 64, 1024), lambda g, s: (0, 0, lax.max(0, lax.min(g - first, 1))))

    return pl.pallas_call(
        up_grad_kernel,
        grid_spec=pltpu.PrefetchScalarGridSpec(
            num_scalar_prefetch=1,
            grid=(4,),
            in_specs=[left, right, left, right],
            out_specs=[spec(n, f) for n, f in outs],
        ),
        out_shape=[jax.ShapeDtypeStruct((n, 64, 2048), bf16) for n, _ in outs],
        compiler_params=params(),
        cost_estimate=cost(2 * 1024 * 512 * 4096, 14 << 20),
        name="up_grad",
    )(info, sides_t.reshape(1024, HALF), gp, sides_t_sib.reshape(1024, HALF), gp_sib)


def out_grad_kernel(info, l0_ref, r0_ref, l1_ref, r1_ref, keep_ref, send_ref):
    for out, at in ((keep_ref, info[3]), (send_ref, 1 - info[3])):
        cols = pl.ds(pl.multiple_of(at * 512, 512), 512)
        total = dot(l0_ref[...], r0_ref[:, cols], (1, 0)) + dot(l1_ref[...], r1_ref[:, cols], (1, 0))
        out[...] = total.astype(bf16).reshape(8, 64, 512)


def out_grad(info, sides_t, gb, sides_t_sib, gb_sib):
    block = lambda *shape: pl.BlockSpec(shape, lambda i, s: (0,) * len(shape))
    return pl.pallas_call(
        out_grad_kernel,
        grid_spec=pltpu.PrefetchScalarGridSpec(
            num_scalar_prefetch=1,
            grid=(1,),
            in_specs=[block(512, HALF), block(HALF, 1024)] * 2,
            out_specs=[block(8, 64, 512)] * 2,
        ),
        out_shape=[jax.ShapeDtypeStruct((8, 64, 512), bf16)] * 2,
        compiler_params=params(),
        cost_estimate=cost(2 * 512 * 1024 * 1024, 4 << 20),
        name="out_grad",
    )(info, sides_t.reshape(1024, HALF), gb, sides_t_sib.reshape(1024, HALF), gb_sib)


def input_part_kernel(group, part, info, d_ref, a_ref, b_ref, *refs):
    out_ref, w_ref, sems = refs[-3:]
    copies = weight_copies(info, a_ref, b_ref, w_ref, sems, 1, group * 768, 768)
    start(copies)
    wait(copies)
    if part is None:
        for half in range(2):
            rows = slice(half * HALF, half * HALF + HALF)
            out_ref[rows, :] = dot(d_ref[rows, :], w_ref[...], (1, 1))
    else:
        out_ref[...] = (refs[0][...] + dot(d_ref[...], w_ref[...], (1, 1))).astype(out_ref.dtype)


def input_part(info, d, a, b, group, part=None, earlier=None):
    side = lambda s: s[3] if part == 0 else 1 - s[3]
    tokens = 2 * HALF if part is None else HALF
    at = (lambda i, s: (0, 0)) if part is None else (lambda i, s: (side(s), 0))
    kind = bf16 if part == 1 else f32
    more = [] if part is None else [earlier]
    return pl.pallas_call(
        functools.partial(input_part_kernel, group, part),
        grid_spec=pltpu.PrefetchScalarGridSpec(
            num_scalar_prefetch=1,
            grid=(1,),
            in_specs=[pl.BlockSpec((tokens, 768), at), hbm(), hbm()] + [pl.BlockSpec((tokens, 1024), at)] * len(more),
            out_specs=pl.BlockSpec((tokens, 1024), lambda i, s: (0, 0)),
            scratch_shapes=[pltpu.VMEM((1024, 768), bf16), pltpu.SemaphoreType.DMA((16,))],
        ),
        out_shape=jax.ShapeDtypeStruct((tokens, 1024), kind),
        compiler_params=params(),
        cost_estimate=cost(2 * tokens * 1024 * 768, 8 << 20),
        name="input_part",
    )(info, d, a, b, *more)


def qkv_grad_kernel(info, l0_ref, r0_ref, l1_ref, r1_ref, *refs):
    beside, own = refs[-2:]
    total = dot(l0_ref[...], r0_ref[...], (1, 0)) + dot(l1_ref[...], r1_ref[...], (1, 0))
    total = total.astype(bf16).reshape(8, 64, 768)
    own[:, :, :768] = total[:4]
    beside[:, :, :768] = total[4:]
    if len(refs) == 4:
        both = (refs[0][...].astype(f32) + refs[1][...].astype(f32)).astype(bf16)
        own[:, :, 768:] = both[:4]
        beside[:, :, 768:] = both[4:]


def qkv_grad(info, nin_t, dproj, nin_t_sib, dproj_sib, more=()):
    block = lambda *shape: pl.BlockSpec(shape, lambda i, s: (0,) * len(shape))
    width = 768 + 512 * bool(more)
    return pl.pallas_call(
        qkv_grad_kernel,
        grid_spec=pltpu.PrefetchScalarGridSpec(
            num_scalar_prefetch=1,
            grid=(1,),
            in_specs=[block(512, 1024), block(1024, 768)] * 2 + [block(8, 64, 512)] * len(more),
            out_specs=[block(4, 64, width)] * 2,
        ),
        out_shape=[jax.ShapeDtypeStruct((4, 64, width), bf16)] * 2,
        compiler_params=params(),
        cost_estimate=cost(2 * 2048 * 512 * 768, 8 << 20),
        name="qkv_grad",
    )(info, nin_t.reshape(512, 1024), dproj, nin_t_sib.reshape(512, 1024), dproj_sib, *more)


def input_norm_kernel(info, xo_ref, xt_ref, g_ref, own_ref, oth_ref, t_ref):
    side = info[3]
    for part, x_ref in ((0, xo_ref), (1, xt_ref)):
        at = side if part == 0 else 1 - side
        normed = (centred(x_ref[...].astype(f32))[0] * g_ref[:1]).astype(bf16)
        t_ref[:, pl.ds(pl.multiple_of(at * HALF, HALF), HALF)] = normed.T
    put_parities(info, t_ref, own_ref, oth_ref, 0)


def input_norm(info, x_own, x_other, gains):
    block = lambda *shape: pl.BlockSpec(shape, lambda i, s: (0,) * len(shape))
    return pl.pallas_call(
        input_norm_kernel,
        grid_spec=pltpu.PrefetchScalarGridSpec(
            num_scalar_prefetch=1,
            grid=(1,),
            in_specs=[block(HALF, 1024), block(HALF, 1024), block(2, 1024)],
            out_specs=[block(1, 8, 64, 1024)] * 2,
            scratch_shapes=[pltpu.VMEM((1024, 1024), bf16)],
        ),
        out_shape=[jax.ShapeDtypeStruct((1, 8, 64, 1024), bf16)] * 2,
        compiler_params=params(),
        cost_estimate=cost(20 << 20, 8 << 20),
        name="input_norm",
    )(info, x_own, x_other, gains)


def slot_bias(phones, prompts, targets):
    places = jnp.arange(HALF, dtype=jnp.int32)
    count = phones.shape[0]
    segs, is_phone = [], None
    for lengths in (phones + prompts, targets):
        ends = jnp.stack([sum(lengths[i] for i in range(upto + 1)) for upto in range(count)])
        seg = jnp.sum((places[:, None] >= ends[None, :]).astype(jnp.int32), axis=1)
        segs.append(seg)
        if is_phone is None:
            onehot = seg[:, None] == jnp.arange(count, dtype=jnp.int32)[None, :]
            phone_ends = jnp.sum(jnp.where(onehot, (ends - lengths + phones)[None, :], 0), axis=1)
            is_phone = places < phone_ends
    seg = jnp.concatenate(segs)
    phone = jnp.concatenate([is_phone, jnp.zeros((HALF,), dtype=bool)])
    order = jnp.arange(2 * HALF, dtype=jnp.int32)
    allowed = (seg[:, None] == seg[None, :]) & (
        phone[:, None] | (jnp.logical_not(phone)[None, :] & (order[:, None] <= order[None, :]))
    )
    return jnp.where(allowed, 0.0, NEG).astype(f32)


def line_shards(tokens, cotangent, gains, w_qkv, w_out, w_up, w_down, phone_len, prompt_len, target_len):
    r = lax.axis_index("rows")
    side = lax.axis_index("pair")
    info = jnp.stack([r // 4, r // 2 % 2, r % 2, side]).astype(jnp.int32)
    x_own = tokens[0]
    cot = cotangent[0]

    gain_lanes = jnp.pad(gains, ((0, 0), (0, 127)))
    crossed = swap_y(jnp.concatenate([w_qkv[:, 512:1024], gain_lanes], axis=1))
    first, middle, last = w_qkv[:, :512], crossed[:, :512], w_qkv[:, 1024:]
    q = jnp.where(side == 0, first, middle)
    k = jnp.where(side == 0, last, first)
    v = jnp.where(side == 0, middle, last)
    gain_own, gain_got = gains, crossed[:, 512:513]
    gain_pair = jnp.where(
        side == 0, jnp.concatenate([gain_own, gain_got], axis=1), jnp.concatenate([gain_got, gain_own], axis=1)
    )
    heads = jnp.concatenate(
        [m[:, i : i + 256] for i in (0, 256) for m in (q, k, v)] + [jnp.pad(gain_pair, ((0, 0), (0, 126)))], axis=1
    )
    heads, x_send = lax.optimization_barrier((heads, x_own))
    pieces = [heads] + [shift_z(heads, j) for j in range(1, LINE)]
    x_other = swap_y(x_send)
    beside = [swap_x(p) for p in pieces]
    pieces, up_out, w_down_in = lax.optimization_barrier((pieces, jnp.concatenate([w_up, w_out], axis=1), w_down))
    up_line = along_line(up_out)
    qkv_line = jnp.stack(pieces)
    qkv_line_sib = swap_c(qkv_line)
    beside = jnp.stack(beside)
    beside_sib = swap_c(beside)
    qkv_a = jnp.concatenate([qkv_line, beside])
    qkv_b = jnp.concatenate([qkv_line_sib, beside_sib])

    bias = slot_bias(phone_len[0], prompt_len[0], target_len[0])
    cot_t = cot.T
    projected, gain_all = project(info, after(x_own, cot_t, bias), x_other, qkv_a, qkv_b)
    projected, up_line, w_down_in = lax.optimization_barrier((projected, up_line, w_down_in))
    up_x, up_y = swap_x(up_line), swap_y(up_line)
    down_line = along_line(w_down_in)
    keep0, send0, lse0 = attend(info, projected, bias, 0)
    bias, keep0, send0, up_x, up_y = lax.optimization_barrier((bias, keep0, send0, up_x, up_y))
    got0 = swap_y(send0)
    up_far = [swap_y(up_x[:2]), swap_x(up_y[2:])]
    keep1, send1, lse1 = attend(info, projected, after(bias, keep0), 1)
    keep1, send1, up_far, down_line = lax.optimization_barrier((keep1, send1, up_far, down_line))
    got1 = swap_y(send1)
    up_a = jnp.concatenate([up_line, up_x, up_y, *up_far])
    up_b = swap_c(up_a)
    down_x, down_y = swap_x(down_line), swap_y(down_line)
    nin_t, nin_t_oth = input_norm(info, after(x_own, keep1, up_a), x_other, gain_all)
    got0, got1, nin_t_oth, cot_t, up_b = lax.optimization_barrier((got0, got1, nin_t_oth, cot_t, up_b))
    nin_t_sib = swap_c(nin_t_oth)
    cot_t_sib = swap_c(cot_t)
    mid, normed_mid, sides_t, sides_t_oth = attention_out(info, x_own, (keep0, keep1), (got0, got1), up_a, up_b, gain_all)
    sides_t_sib = swap_c(sides_t_oth)
    down_x, down_y, normed_mid = lax.optimization_barrier((down_x, down_y, normed_mid))
    down_far = [swap_y(down_x[:2]), swap_x(down_y[2:])]
    act, act_oth, slope, slope_oth = up(info, normed_mid, up_a, up_b)
    down_far, act_oth = lax.optimization_barrier((down_far, act_oth))
    down_a = jnp.concatenate([down_line, down_x, down_y, *down_far])
    down_b = swap_c(down_a)
    act_sib = swap_c(act_oth)
    mixed, gp = down(info, (act, act_oth), (slope, slope_oth), down_a, down_b, cot, mid)
    gp_sib = swap_c(gp)

    far_a, far_b, beside, across, own = down_grad(info, cot_t, after(act, gp), cot_t_sib, act_sib)
    got_a, got_b = swap_x(far_a), swap_y(far_b)
    gm, gb, ga_keep0, ga_keep1, ga_send0, ga_send1 = middle_back(info, after(gp, own), up_a, up_b, cot, mid, gain_all)
    ga_got0, ga_got1 = swap_y(ga_send0), swap_y(ga_send1)
    gb_sib = swap_c(gb)
    got_a, got_b, gb = lax.optimization_barrier((got_a, got_b, gb))
    down_x = swap_x(jnp.concatenate([beside[:2], plus(beside[2:], got_b)]))
    down_y = swap_y(jnp.concatenate([plus(across[:2], got_a), across[2:]]))
    down_own = own
    far_a, far_b, beside, across, own = up_grad(info, sides_t, after(gp, gb), sides_t_sib, gp_sib)
    out_keep, out_send = out_grad(info, sides_t, after(gb, own), sides_t_sib, gb_sib)
    out_got = swap_y(out_send)
    got_a, got_b = swap_x(far_a), swap_y(far_b)
    dproj0 = attend_back(info, projected, after(bias, out_keep), lse0, ga_keep0, ga_got0, 0)
    dproj0_sib = swap_c(dproj0)
    dproj0, down_x, down_y, got_a, got_b = lax.optimization_barrier((dproj0, down_x, down_y, got_a, got_b))
    down_parts = [
        (down_own[k].astype(f32) + down_x[k].astype(f32) + down_y[k].astype(f32)).astype(bf16) for k in range(LINE)
    ]
    down_shift = [shift_z(down_parts[k], k) for k in range(1, LINE)]
    up_x = swap_x(jnp.concatenate([beside[:2], plus(beside[2:], got_b)]))
    up_y = swap_y(jnp.concatenate([plus(across[:2], got_a), across[2:]]))
    up_own = own
    e_first = input_part(info, after(dproj0, down_parts), qkv_a, qkv_b, 0)
    beside, own = qkv_grad(info, nin_t, after(dproj0, e_first), nin_t_sib, dproj0_sib, (out_keep, out_got))
    first_x = swap_x(beside)
    first_own = own
    dproj1 = attend_back(info, projected, after(bias, own), lse1, ga_keep1, ga_got1, 1)
    dproj1_sib = swap_c(dproj1)
    dproj1, up_x, up_y, first_x, down_shift = lax.optimization_barrier((dproj1, up_x, up_y, first_x, down_shift))
    e_send = input_part(info, dproj1, qkv_a, qkv_b, 1, 1, e_first)
    e_got = swap_y(e_send)
    up_parts = [
        (up_own[k].astype(f32) + up_x[k].astype(f32) + up_y[k].astype(f32)).astype(bf16) for k in range(LINE)
    ]
    first_parts = [plus(first_own[k], first_x[k]) for k in range(LINE)]
    up_parts, first_parts, dproj1_late = lax.optimization_barrier((up_parts, first_parts, dproj1))
    up_shift = [shift_z(up_parts[k], k) for k in range(1, LINE)]
    first_shift = [shift_z(first_parts[k], k) for k in range(1, LINE)]
    beside, own = qkv_grad(info, nin_t, after(dproj1_late, e_send), nin_t_sib, dproj1_sib)
    second_x = swap_x(beside)
    e_own = input_part(info, after(dproj1, own), qkv_a, qkv_b, 1, 0, e_first)
    g_down = sum([p.astype(f32) for p in down_shift], down_parts[0].astype(f32)).T
    g_second = summed_line([plus(own[k], after(second_x, e_own)[k]) for k in range(LINE)])
    g_up = sum([p.astype(f32) for p in up_shift], up_parts[0].astype(f32))
    g_first = sum([p.astype(f32) for p in first_shift], first_parts[0].astype(f32))
    g_out = g_first[:, 768:]
    gq, gk, gv = (
        jnp.concatenate([g_first[:, j : j + 256], g_second[:, j : j + 256]], axis=1) for j in (0, 256, 512)
    )

    crossed = swap_y(jnp.where(side == 0, gv, gq))
    g_qkv = jnp.where(
        side == 0, jnp.concatenate([gq, crossed, gk], axis=1), jnp.concatenate([gk, crossed, gv], axis=1)
    )
    in_sum = jnp.sum(w_qkv.astype(f32) * g_qkv, axis=1, keepdims=True)
    mid_sum = jnp.sum(w_up.astype(f32) * g_up, axis=1, keepdims=True)
    gain_sum = jnp.where(side == 0, in_sum, mid_sum) + swap_y(jnp.where(side == 0, mid_sum, in_sum))
    grad_gains = gain_sum / gains.astype(f32)

    n, scale = centred(x_own.astype(f32))
    eg = (e_own + e_got.astype(f32)) * lax.dynamic_slice_in_dim(gain_all, 0, 1, 0)
    lean = eg - jnp.mean(eg, axis=-1, keepdims=True) - n * jnp.mean(eg * n, axis=-1, keepdims=True)
    grad_tokens = gm + scale * lean
    return (mixed[None], grad_tokens[None], grad_gains, g_qkv, g_out, g_up, g_down)


def solution(mesh):
    lined = mesh.shape["rows"] == 4 * LINE and mesh.shape["pair"] == 2
    return jax.shard_map(
        line_shards if lined else shards,
        mesh=mesh,
        in_specs=(
            P("rows", "pair", None),
            P("rows", "pair", None),
            P("rows", "pair"),
            P("rows", "pair"),
            P("rows", "pair"),
            P("rows", "pair"),
            P("rows", "pair"),
            P("rows", None),
            P("rows", None),
            P("rows", None),
        ),
        out_specs=(
            P("rows", "pair", None),
            P("rows", "pair", None),
            P("rows", "pair"),
            P("rows", "pair"),
            P("rows", "pair"),
            P("rows", "pair"),
            P("rows", "pair"),
        ),
        check_vma=False,
    )
```

```python
import functools

import jax
import jax.numpy as jnp
from jax import lax
from jax.experimental import pallas as pl
from jax.experimental.pallas import tpu as pltpu
from jax.sharding import PartitionSpec as P

HEADS = 16
HEAD_DIM = 64


epsilon = 1e-05


def passed_along(value, axis, steps):
    count = lax.axis_size(axis)
    leading, last = (max(0, -steps), min(count, count - steps))
    return lax.ppermute(value, axis, [(source, source + steps) for source in range(leading, last)])


def slot_layout(side_index, phones, prompts, targets, slot_count):
    lengths = jnp.where(side_index == 0, phones + prompts, targets)
    count = lengths.shape[0]
    seg_ends = jnp.stack([sum(lengths[i] for i in range(upto + 1)) for upto in range(count)])
    starts = seg_ends - lengths
    places = jnp.arange(slot_count, dtype=jnp.int32)
    segment = jnp.sum((places[:, None] >= seg_ends[None, :]).astype(jnp.int32), axis=1)
    onehot = (segment[:, None] == jnp.arange(lengths.shape[0], dtype=jnp.int32)[None, :]).astype(
        jnp.int32
    )
    within = places - jnp.sum(onehot * starts[None, :], axis=1)
    phone_here = jnp.sum(onehot * phones[None, :], axis=1)
    is_phone = jnp.logical_and(side_index == 0, within < phone_here)
    ordering = places + side_index * slot_count
    return (segment, is_phone, ordering)


def permitted(query_side, key_side):
    query_seg, query_phone, query_order = query_side
    key_seg, key_phone, key_order = key_side
    same_seg = query_seg[:, None] == key_seg[None, :]
    earlier = key_order[None, :] <= query_order[:, None]
    return same_seg & (key_phone[None, :] | jnp.logical_not(query_phone)[:, None] & earlier)


def normalize(values, gain_row):
    centred = values - jnp.mean(values, axis=-1, keepdims=True)
    spread = jnp.mean(centred * centred, axis=-1, keepdims=True)
    return centred * lax.rsqrt(spread + epsilon) * gain_row


def exact_gelu(values):
    return jax.nn.gelu(values, approximate=False)


def softmax_rows(query_piece, key_piece, allowed):
    scores = jnp.einsum(
        "qhd,khd->hqk", query_piece, key_piece, preferred_element_type=jnp.float32
    ) * HEAD_DIM ** (-0.5)
    scores = jnp.where(allowed[None], scores, -1e30)
    row_max = jnp.max(scores, axis=-1, keepdims=True)
    exponents = jnp.exp(scores - row_max)
    return exponents / jnp.sum(exponents, axis=-1, keepdims=True)


def shards(tokens, cotangent, gains, w_qkv, w_out, w_up, w_down, phone_len, prompt_len, target_len):
    slot_count = tokens.shape[1]
    model_width = tokens.shape[2]
    inputs = tokens[0].astype(jnp.float32)
    side_index = lax.axis_index("pair")
    paired = (
        lax.all_gather(gains, "pair", axis=1, tiled=True),
        lax.all_gather(w_qkv, "pair", axis=1, tiled=True),
        lax.all_gather(w_out, "pair", axis=1, tiled=True),
        lax.all_gather(w_up, "pair", axis=1, tiled=True),
        lax.all_gather(w_down, "pair", axis=1, tiled=True),
    )
    gain_all, qkv_all, out_all, up_all, down_all = (
        lax.all_gather(paired[0], "rows", axis=0, tiled=True),
        lax.all_gather(paired[1], "rows", axis=0, tiled=True),
        lax.all_gather(paired[2], "rows", axis=0, tiled=True),
        lax.all_gather(paired[3], "rows", axis=0, tiled=True),
        lax.all_gather(paired[4], "rows", axis=0, tiled=True),
    )
    gain_first = gain_all[:, 0].astype(jnp.float32)
    gain_second = gain_all[:, 1].astype(jnp.float32)
    phones = phone_len[0]
    prompts = prompt_len[0]
    targets = target_len[0]
    own_layout = slot_layout(side_index, phones, prompts, targets, slot_count)
    far_layout = slot_layout(0, phones, prompts, targets, slot_count)
    key_layout = tuple(
        (
            jnp.concatenate([far_part, own_part])
            for far_part, own_part in zip(far_layout, own_layout)
        )
    )
    far_live = jnp.concatenate(
        [jnp.full((slot_count,), side_index == 1), jnp.ones((slot_count,), dtype=bool)]
    )
    normed_in, norm_first_back = jax.vjp(normalize, inputs, gain_first)
    normed_low = normed_in.astype(jnp.bfloat16)
    projected = jnp.dot(normed_low, qkv_all, preferred_element_type=jnp.float32).astype(
        jnp.bfloat16
    )
    queries = projected[:, :model_width]
    near_pairs = projected[:, model_width:]
    far_pairs = passed_along(near_pairs, "pair", 1)
    key_value = jnp.concatenate([far_pairs, near_pairs], axis=0)
    block_rows = min(512, slot_count)
    per_group = min(4, HEADS)
    group_width = per_group * HEAD_DIM
    groups = HEADS // per_group
    steps_total = slot_count // block_rows * groups
    key_count = 2 * slot_count

    def piece_of(item_index):
        row_start = item_index // groups * block_rows
        col_start = item_index % groups * group_width
        query_piece = lax.dynamic_slice(
            queries, (row_start, col_start), (block_rows, group_width)
        ).reshape(block_rows, per_group, HEAD_DIM)
        key_piece = lax.dynamic_slice(key_value, (0, col_start), (key_count, group_width)).reshape(
            key_count, per_group, HEAD_DIM
        )
        value_piece = lax.dynamic_slice(
            key_value, (0, model_width + col_start), (key_count, group_width)
        ).reshape(key_count, per_group, HEAD_DIM)
        query_layout = tuple((member for member in own_layout))
        allowed = permitted(query_layout, key_layout) & far_live[None, :]
        attn_probs = softmax_rows(query_piece, key_piece, allowed)
        return (row_start, col_start, query_piece, key_piece, value_piece, attn_probs)

    def forward_step(item_index, attended):
        row_start, col_start, query_piece, key_piece, value_piece, attn_probs = piece_of(item_index)
        head_mix = jnp.einsum(
            "hqk,khd->qhd",
            attn_probs.astype(jnp.bfloat16),
            value_piece,
            preferred_element_type=jnp.float32,
        )
        return lax.dynamic_update_slice(
            attended, head_mix.reshape(block_rows, group_width), (row_start, col_start)
        )

    attended = lax.fori_loop(
        0, steps_total, forward_step, jnp.zeros((slot_count, model_width), jnp.float32)
    )
    attended_low = attended.astype(jnp.bfloat16)
    middle = inputs + jnp.dot(attended_low, out_all, preferred_element_type=jnp.float32)
    normed_mid, norm_second_back = jax.vjp(normalize, middle, gain_second)
    normed_mid_low = normed_mid.astype(jnp.bfloat16)
    pre_act = jnp.dot(normed_mid_low, up_all, preferred_element_type=jnp.float32)
    activated, gelu_back = jax.vjp(exact_gelu, pre_act)
    activated_low = activated.astype(jnp.bfloat16)
    result = middle + jnp.dot(activated_low, down_all, preferred_element_type=jnp.float32)
    mixed_out = result.astype(jnp.bfloat16)[None]
    qkv_back, out_back, up_back, down_back = (qkv_all, out_all, up_all, down_all)
    grad_result = cotangent[0]
    grad_down = jnp.dot(activated_low.T, grad_result, preferred_element_type=jnp.float32)
    grad_act = jnp.dot(grad_result, down_back.T, preferred_element_type=jnp.float32)
    grad_pre = gelu_back(grad_act)[0].astype(jnp.bfloat16)
    grad_up = jnp.dot(normed_mid_low.T, grad_pre, preferred_element_type=jnp.float32)
    grad_normed_mid = jnp.dot(grad_pre, up_back.T, preferred_element_type=jnp.float32)
    grad_middle_norm, grad_gain_second = norm_second_back(grad_normed_mid)
    grad_middle = grad_result.astype(jnp.float32) + grad_middle_norm
    grad_branch = grad_middle.astype(jnp.bfloat16)
    grad_out = jnp.dot(attended_low.T, grad_branch, preferred_element_type=jnp.float32)
    grad_attended = jnp.dot(grad_branch, out_back.T, preferred_element_type=jnp.float32).astype(
        jnp.bfloat16
    )

    def backward_step(item_index, running):
        grad_queries, grad_pairs = running
        row_start, col_start, query_piece, key_piece, value_piece, attn_probs = piece_of(item_index)
        grad_piece = lax.dynamic_slice(
            grad_attended, (row_start, col_start), (block_rows, group_width)
        ).reshape(block_rows, per_group, HEAD_DIM)
        grad_probs = jnp.einsum(
            "qhd,khd->hqk", grad_piece, value_piece, preferred_element_type=jnp.float32
        )
        centre = jnp.sum(grad_probs * attn_probs, axis=-1, keepdims=True)
        grad_scores = (attn_probs * (grad_probs - centre)).astype(jnp.bfloat16)
        score_scale = HEAD_DIM ** (-0.5)
        query_grad = (
            jnp.einsum("hqk,khd->qhd", grad_scores, key_piece, preferred_element_type=jnp.float32)
            * score_scale
        )
        key_grad = (
            jnp.einsum("hqk,qhd->khd", grad_scores, query_piece, preferred_element_type=jnp.float32)
            * score_scale
        )
        value_grad = jnp.einsum(
            "hqk,qhd->khd",
            attn_probs.astype(jnp.bfloat16),
            grad_piece,
            preferred_element_type=jnp.float32,
        )
        grad_queries = lax.dynamic_update_slice(
            grad_queries, query_grad.reshape(block_rows, group_width), (row_start, col_start)
        )
        key_old = lax.dynamic_slice(grad_pairs, (0, col_start), (key_count, group_width))
        grad_pairs = lax.dynamic_update_slice(
            grad_pairs, key_old + key_grad.reshape(key_count, group_width), (0, col_start)
        )
        value_old = lax.dynamic_slice(
            grad_pairs, (0, model_width + col_start), (key_count, group_width)
        )
        grad_pairs = lax.dynamic_update_slice(
            grad_pairs,
            value_old + value_grad.reshape(key_count, group_width),
            (0, model_width + col_start),
        )
        return (grad_queries, grad_pairs)

    start_state = (
        jnp.zeros((slot_count, model_width), jnp.float32),
        jnp.zeros((key_count, 2 * model_width), jnp.float32),
    )
    grad_queries, grad_pairs = lax.fori_loop(0, steps_total, backward_step, start_state)
    returned = passed_along(grad_pairs[:slot_count].astype(jnp.bfloat16), "pair", -1).astype(
        jnp.float32
    )
    grad_near = (grad_pairs[slot_count:] + returned).astype(jnp.bfloat16)
    grad_projected = jnp.concatenate([grad_queries.astype(jnp.bfloat16), grad_near], axis=1)
    grad_qkv = jnp.dot(normed_low.T, grad_projected, preferred_element_type=jnp.float32)
    grad_normed_in = jnp.dot(grad_projected, qkv_back.T, preferred_element_type=jnp.float32)
    grad_inputs_norm, grad_gain_first = norm_first_back(grad_normed_in)
    grad_tokens = (grad_middle + grad_inputs_norm)[None]
    grad_gains = jnp.stack([grad_gain_first, grad_gain_second], axis=1)
    strips = (
        lax.psum_scatter(grad_gains, "rows", scatter_dimension=0, tiled=True),
        lax.psum_scatter(grad_qkv.astype(jnp.bfloat16), "rows", scatter_dimension=0, tiled=True),
        lax.psum_scatter(grad_out.astype(jnp.bfloat16), "rows", scatter_dimension=0, tiled=True),
        lax.psum_scatter(grad_up.astype(jnp.bfloat16), "rows", scatter_dimension=0, tiled=True),
        lax.psum_scatter(grad_down.astype(jnp.bfloat16), "rows", scatter_dimension=0, tiled=True),
    )
    owned = (
        lax.psum_scatter(
            strips[0].astype(jnp.bfloat16), "pair", scatter_dimension=1, tiled=True
        ).astype(jnp.float32),
        lax.psum_scatter(
            strips[1].astype(jnp.bfloat16), "pair", scatter_dimension=1, tiled=True
        ).astype(jnp.float32),
        lax.psum_scatter(
            strips[2].astype(jnp.bfloat16), "pair", scatter_dimension=1, tiled=True
        ).astype(jnp.float32),
        lax.psum_scatter(
            strips[3].astype(jnp.bfloat16), "pair", scatter_dimension=1, tiled=True
        ).astype(jnp.float32),
        lax.psum_scatter(
            strips[4].astype(jnp.bfloat16), "pair", scatter_dimension=1, tiled=True
        ).astype(jnp.float32),
    )
    return (mixed_out, grad_tokens, owned[0], owned[1], owned[2], owned[3], owned[4])


LINE = 4
HALF = 512
NEG = -1e30
bf16 = jnp.bfloat16
f32 = jnp.float32
VMEM_LIMIT = 56 * 1024 * 1024


def params(limit=VMEM_LIMIT):
    return pltpu.CompilerParams(vmem_limit_bytes=limit)


PLACES = dict(up_stack=20, attend_1=20, touch=20, attend_back_0=20, mixed=20, down_sum=20, up_parts=20, up_sum=20)


def cost(name):
    return pl.CostEstimate(flops=int(PLACES.get(name, 0.5) * 1.15e9), bytes_accessed=1 << 16, transcendentals=0)


def hbm():
    return pl.BlockSpec(memory_space=pl.ANY)


def block(*shape):
    return pl.BlockSpec(shape, lambda i, s: (0,) * len(shape))


def call(kernel, name, ins, outs, scratch, flops, *args, grid=(1,)):
    out = pl.pallas_call(
        kernel,
        grid_spec=pltpu.PrefetchScalarGridSpec(
            num_scalar_prefetch=1,
            grid=grid,
            in_specs=ins,
            out_specs=[spec for spec, _ in outs],
            scratch_shapes=scratch,
        ),
        out_shape=[shape for _, shape in outs],
        compiler_params=params(),
        cost_estimate=cost(name),
        name=name,
    )(*args)
    return out


def of(kind, *shape):
    return jax.ShapeDtypeStruct(shape, kind)


def dot(a, b, contract):
    return lax.dot_general(a, b, ((contract[:1], contract[1:]), ((), ())), preferred_element_type=f32)


def row_pairs(target):
    pairs = []
    for r in range(LINE * 4):
        z, x, c = target(r // 4, r // 2 % 2, r % 2)
        pairs.append((r, z % LINE * 4 + x * 2 + c))
    return pairs


def shift_z(v, k):
    return lax.ppermute(v, "rows", row_pairs(lambda z, x, c: (z + k, x, c)))


def swap_x(v):
    return lax.ppermute(v, "rows", row_pairs(lambda z, x, c: (z, 1 - x, c)))


def swap_c(v):
    return lax.ppermute(v, "rows", row_pairs(lambda z, x, c: (z, x, 1 - c)))


def swap_y(v):
    return lax.ppermute(v, "pair", [(0, 1), (1, 0)])


def along_line(shard):
    return [shard] + [shift_z(shard, k) for k in range(1, LINE)]


def barrier(*values):
    return lax.optimization_barrier(values)


def after(value, *others):
    return lax.optimization_barrier((value, others))[0]


def qkv_copies(info, refs, w_ref, sems, start_col, cols):
    out = []
    for dx in range(2):
        for dz in range(LINE):
            chip = lax.rem(info[0] + LINE - dz, LINE) * 2 + lax.rem(info[1] + dx, 2)
            for own in (0, 1):
                core = info[2] if own == 0 else 1 - info[2]
                out.append(
                    pltpu.make_async_copy(
                        refs[own * 2 + dx].at[dz, :, pl.ds(start_col, cols)],
                        w_ref.at[pl.ds(pl.multiple_of(chip * 128 + core * 64, 64), 64), :],
                        sems.at[(dx * LINE + dz) * 2 + own],
                    )
                )
    return out


def by_chip(z, x):
    return z * 2 + x


def by_unit(z, x):
    return z // 2 * 4 + x * 2 + z % 2


def piece_copies(info, refs, w_ref, sems, rows, cols, order):
    line, beside, across, far_a, far_b = refs
    out = [[], []]
    for dy in range(2):
        for dx in range(2):
            for dz in range(LINE):
                chip = order(lax.rem(info[0] + LINE - dz, LINE), lax.rem(info[1] + dx, 2))
                ref, at = ((line, dz), (beside, dz), (across, dz), (far_a, dz) if dz < 2 else (far_b, dz + far_b.shape[0] - LINE))[dx + 2 * dy]
                out[dy].append(
                    pltpu.make_async_copy(
                        ref.at[at, :, pl.ds(0, cols)],
                        w_ref.at[pl.ds(pl.multiple_of(chip * rows, rows), rows), pl.ds(dy * cols, cols)],
                        sems.at[(dy * 2 + dx) * LINE + dz],
                    )
                )
    return out


def start(copies):
    for c in copies:
        c.start()


def wait(copies):
    for c in copies:
        c.wait()


def project_kernel(info, xo_ref, xt_ref, *refs):
    out_ref, g_ref, w_ref, gcol_ref, nin_ref, sems = refs[4:]
    copies = qkv_copies(info, refs[:4], w_ref, sems, 0, 1536)
    gains = qkv_copies(info, refs[:4], gcol_ref, sems.at[pl.ds(16, 16)], 1536, 128)
    start(gains)
    start(copies)
    wait(gains)
    both = gcol_ref[...].T.astype(f32)[:2]
    g_ref[...] = both
    side = info[3]
    for part, x_ref in ((0, xo_ref), (1, xt_ref)):
        at = side if part == 0 else 1 - side
        tokens = pl.ds(pl.multiple_of(at * HALF, HALF), HALF)
        nin_ref[tokens, :] = (centred(x_ref[...].astype(f32))[0] * both[:1]).astype(bf16)
        if part == 0:
            wait(copies)
        for n in range(2):
            cols = slice(n * 768, n * 768 + 768)
            out_ref[tokens, cols] = dot(nin_ref[tokens, :], w_ref[:, cols], (1, 0)).astype(bf16)


def project(info, x_own, x_other, pieces):
    return call(
        project_kernel,
        "project",
        [block(HALF, 1024), block(HALF, 1024)] + [hbm()] * 4,
        [(block(1024, 1536), of(bf16, 1024, 1536)), (block(2, 1024), of(f32, 2, 1024))],
        [
            pltpu.VMEM((1024, 1536), bf16),
            pltpu.VMEM((1024, 128), bf16),
            pltpu.VMEM((1024, 1024), bf16),
            pltpu.SemaphoreType.DMA((32,)),
        ],
        2 * 1024 * 1024 * 1536,
        info,
        x_own,
        x_other,
        *pieces,
    )


TILES = ((0, 512), (256, 512), (512, 768), (768, 1024))


def own_lanes(v, head):
    lane = lax.broadcasted_iota(jnp.int32, v.shape, 1)
    return jnp.where((lane >= 64) if head else (lane < 64), v, jnp.zeros_like(v))


def attend_kernel(info, q_ref, k_ref, v_ref, bias_ref, keep_ref, send_ref, lse_ref):
    side = info[3]
    lane = lax.broadcasted_iota(jnp.int32, (256, 128), 1)
    for tile, (first, seen) in enumerate(TILES):
        rows = slice(first, first + 256)
        q_tile = q_ref[rows, :] * jnp.asarray(0.125, bf16)
        done, lse = [], []
        for head in range(2):
            s = dot(own_lanes(q_tile, head), k_ref[:seen, :], (1, 1)) + bias_ref[rows, :seen]
            top = jnp.max(s, axis=1, keepdims=True)
            p = jnp.exp(s - top)
            total = jnp.sum(p, axis=1, keepdims=True)
            lse.append(top + jnp.log(total))
            done.append(dot(p.astype(bf16), v_ref[:seen, :], (1, 0)) * (1.0 / total))
        both = jnp.where(lane < 64, done[0], done[1]).astype(bf16)
        lse_ref[0, :, rows] = jnp.where(lane == 0, lse[0], lse[1]).T[:2]
        half, row = tile // 2, tile % 2 * 256

        @pl.when(side == half)
        def _():
            keep_ref[row : row + 256, :] = both

        @pl.when(side != half)
        def _():
            send_ref[row : row + 256, :] = both


def head_parts(group):
    return [pl.BlockSpec((1024, 128), lambda h, s, j=j: (0, 6 * group + 2 * j + h)) for j in range(3)]


def attend(info, projected, bias, group):
    piece = pl.BlockSpec((HALF, 128), lambda h, s: (0, h))
    return call(
        attend_kernel,
        f"attend_{group}",
        [*head_parts(group), block(1024, 1024)],
        [
            (piece, of(bf16, HALF, 256)),
            (piece, of(bf16, HALF, 256)),
            (pl.BlockSpec((1, 2, 1024), lambda h, s: (h, 0, 0)), of(f32, 2, 2, 1024)),
        ],
        [],
        4 * 1024 * 768 * 64 * 4,
        info,
        projected,
        projected,
        projected,
        bias,
        grid=(2,),
    )


def attend_back_kernel(info, q_ref, k_ref, v_ref, bias_ref, lse_ref, keep_ref, send_ref, out_ref, dk_ref, dv_ref):
    side = info[3]
    pair = pl.program_id(0)
    k_t = k_ref[...].T
    dk_ref[...] = jnp.zeros_like(dk_ref)
    dv_ref[...] = jnp.zeros_like(dv_ref)
    for tile, (start, seen) in enumerate(TILES):
        half, row = tile // 2, tile % 2 * 256
        q_tile = q_ref[start : start + 256, :] * jnp.asarray(0.125, bf16)
        g_tile = jnp.where(side == half, keep_ref[row : row + 256, :], send_ref[row : row + 256, :])
        pieces = []
        for head in range(2):
            q_head = own_lanes(q_tile, head)
            g_head = own_lanes(g_tile, head)
            s = dot(k_ref[:seen, :], q_head, (1, 1))
            p = jnp.exp(s + bias_ref[:seen, start : start + 256] - lse_ref[0, head : head + 1, start : start + 256])
            dp = dot(v_ref[:seen, :], g_head, (1, 1))
            centre = jnp.sum(p * dp, axis=0, keepdims=True)
            ds = (p * (dp - centre)).astype(bf16)
            dv_ref[:seen, :] += dot(p.astype(bf16), g_head, (1, 0))
            dk_ref[:seen, :] += dot(ds, q_head, (1, 0))
            pieces.append(dot(k_t[head * 64 : head * 64 + 64, :seen], ds, (1, 0)) * 0.125)
        cols = pl.ds(pl.multiple_of(pair * 128, 128), 128)
        out_ref[start : start + 256, cols] = jnp.concatenate(pieces, axis=0).T.astype(bf16)
    out_ref[:, pl.ds(pl.multiple_of(256 + pair * 128, 128), 128)] = dk_ref[...].astype(bf16)
    out_ref[:, pl.ds(pl.multiple_of(512 + pair * 128, 128), 128)] = dv_ref[...].astype(bf16)


def attend_back(info, projected, bias, lse, keep, other, group):
    piece = pl.BlockSpec((HALF, 128), lambda h, s: (0, 2 * group + h))
    return pl.pallas_call(
        attend_back_kernel,
        grid_spec=pltpu.PrefetchScalarGridSpec(
            num_scalar_prefetch=1,
            grid=(2,),
            in_specs=[
                *head_parts(group),
                pl.BlockSpec((1024, 1024), lambda h, s: (0, 0)),
                pl.BlockSpec((1, 2, 1024), lambda h, s: (h, 0, 0)),
                piece,
                piece,
            ],
            out_specs=pl.BlockSpec((1024, 768), lambda h, s: (0, 0)),
            scratch_shapes=[pltpu.VMEM((1024, 128), f32), pltpu.VMEM((1024, 128), f32)],
        ),
        out_shape=jax.ShapeDtypeStruct((1024, 768), bf16),
        compiler_params=params(),
        cost_estimate=cost(f"attend_back_{group}"),
        name=f"attend_back_{group}",
    )(info, projected, projected, projected, bias, lse, keep, other)


def centred(v):
    off = v - jnp.mean(v, axis=-1, keepdims=True)
    scale = lax.rsqrt(jnp.mean(off * off, axis=-1, keepdims=True) + epsilon)
    return off * scale, scale


def out_kernel(info, x_ref, k0, k1, g0, g1, w_ref, g_ref, mid_ref, nm_ref, own_ref, oth_ref, t_ref):
    places = [(info[3] if i < 2 else 1 - info[3]) * HALF + i % 2 * 256 for i in range(4)]
    places = [pl.ds(pl.multiple_of(at, 256), 256) for at in places]
    for half in range(2):
        cols = slice(half * 512, half * 512 + 512)
        branch = x_ref[:, cols].astype(f32)
        for at, ref in zip(places, (k0, k1, g0, g1)):
            branch = branch + dot(ref[...], w_ref[half, at, :], (1, 0))
        mid_ref[:, cols] = branch
    nm_ref[...] = (centred(mid_ref[...])[0] * g_ref[1:]).astype(bf16)
    for at, ref in zip(places, (k0, k1, g0, g1)):
        t_ref[at, :] = ref[...].T
    put_parities(info, t_ref, own_ref, oth_ref)


def put_parities(info, t_ref, own_ref, oth_ref):
    for dx in range(2):
        for dz in range(LINE):
            chip = lax.rem(info[0] + dz, LINE) * 2 + lax.rem(info[1] + dx, 2)
            here = pl.multiple_of(chip * 128 + info[2] * 64, 64)
            there = pl.multiple_of(chip * 128 + (1 - info[2]) * 64, 64)
            own_ref[dx * LINE + dz] = t_ref[pl.ds(here, 64), :]
            oth_ref[dx * LINE + dz] = t_ref[pl.ds(there, 64), :]


def attention_out(info, x, keeps, gots, w, gain):
    return call(
        out_kernel,
        "attention_out",
        [block(HALF, 1024)] + [block(HALF, 256)] * 4 + [block(2, 1024, 512), block(2, 1024)],
        [
            (block(HALF, 1024), of(f32, HALF, 1024)),
            (block(HALF, 1024), of(bf16, HALF, 1024)),
            (block(8, 64, HALF), of(bf16, 8, 64, HALF)),
            (block(8, 64, HALF), of(bf16, 8, 64, HALF)),
        ],
        [pltpu.VMEM((1024, HALF), bf16)],
        2 * 512 * 1024 * 1024,
        info,
        x,
        *keeps,
        *gots,
        w,
        gain,
    )


def up_kernel(info, x0_ref, x1_ref, *refs):
    act_ref, slope_ref, w_ref, sems = refs[5:]
    step = pl.program_id(0)
    near, far = piece_copies(info, refs[:5], w_ref, sems, 128, 1024, by_chip)

    @pl.when(step == 0)
    def _():
        start(near)
        start(far)
        wait(near)

    @pl.when(step == 1)
    def _():
        wait(far)

    for part, x_ref in enumerate((x0_ref, x1_ref)):
        rows = slice(part * HALF, part * HALF + HALF)
        for n in range(2):
            cols = slice(n * 512, n * 512 + 512)
            pre = dot(x_ref[...], w_ref[:, pl.ds(pl.multiple_of(step * 1024 + n * 512, 512), 512)], (1, 0))
            below = 0.5 * (1.0 + lax.erf(pre * 0.7071067811865476))
            act_ref[rows, cols] = (pre * below).astype(bf16)
            slope_ref[rows, cols] = (below + pre * (0.3989422804014327 * jnp.exp(-0.5 * pre * pre))).astype(bf16)


def up(info, x_own, x_sib, pieces):
    out = pl.BlockSpec((1024, 1024), lambda n, s: (0, lax.rem(s[3] + n, 2)))
    return call(
        up_kernel,
        "up",
        [block(HALF, 1024)] * 2 + [hbm()] * 5,
        [(out, of(bf16, 1024, 2048))] * 2,
        [pltpu.VMEM((1024, 2048), bf16), pltpu.SemaphoreType.DMA((16,))],
        4 * 512 * 1024 * 4096,
        info,
        x_own,
        x_sib,
        *pieces,
        grid=(2,),
    )


def down_kernel(info, act_ref, slope_ref, c0_ref, c1_ref, mid_ref, *refs):
    keep_ref, send_ref, gp_ref, w_ref, acc_ref, sems = refs[5:]
    step = pl.program_id(0)
    side = info[3]
    near, far = piece_copies(info, refs[:5], w_ref, sems, 256, 512, by_unit)
    mine = pl.ds(pl.multiple_of(side * 512, 512), 512)
    theirs = pl.ds(pl.multiple_of((1 - side) * 512, 512), 512)

    @pl.when(step == 0)
    def _():
        start(near)
        start(far)
        wait(near)
        wait(far)

    units = pl.ds(pl.multiple_of(step * 1024, 1024), 1024)
    for part, cot_ref in enumerate((c0_ref, c1_ref)):
        rows = slice(part * HALF, part * HALF + HALF)
        for n in range(2):
            here = pl.ds(pl.multiple_of(step * 1024 + n * 512, 512), 512)
            cols = slice(n * 512, n * 512 + 512)
            back = dot(cot_ref[:, mine], w_ref[here, :512], (1, 1)) + dot(cot_ref[:, theirs], w_ref[here, 512:], (1, 1))
            gp_ref[rows, cols] = (back * slope_ref[rows, cols].astype(f32)).astype(bf16)
        total = dot(act_ref[rows, :], w_ref[units, :], (1, 0))

        @pl.when(step == 0)
        def _():
            acc_ref[rows, :] = total

        @pl.when(step == 1)
        def _():
            done = total + acc_ref[rows, :]
            if part == 0:
                keep_ref[:, mine] = mid_ref[:, mine] + done[:, :512]
                keep_ref[:, theirs] = mid_ref[:, theirs] + done[:, 512:]
            else:
                send_ref[:, mine] = done[:, :512].astype(bf16)
                send_ref[:, theirs] = done[:, 512:].astype(bf16)


def down(info, act, slope, cot_own, cot_sib, mid, pieces):
    tile = pl.BlockSpec((1024, 1024), lambda n, s: (0, n))
    return call(
        down_kernel,
        "down",
        [tile, tile] + [block(HALF, 1024)] * 3 + [hbm()] * 5,
        [
            (block(HALF, 1024), of(f32, HALF, 1024)),
            (block(HALF, 1024), of(bf16, HALF, 1024)),
            (tile, of(bf16, 1024, 2048)),
        ],
        [pltpu.VMEM((2048, 1024), bf16), pltpu.VMEM((1024, 1024), f32), pltpu.SemaphoreType.DMA((16,))],
        4 * 512 * 1024 * 4096,
        info,
        act,
        slope,
        cot_own,
        cot_sib,
        mid,
        *pieces,
        grid=(2,),
    )


def normed_back_kernel(info, gp_ref, *refs):
    keep_ref, send_ref, w_ref, sems = refs[5:]
    near, far = piece_copies(info, refs[:5], w_ref, sems, 128, 1024, by_chip)
    start(near)
    start(far)
    wait(near)
    wait(far)
    mine = pl.ds(pl.multiple_of(info[3] * 1024, 1024), 1024)
    theirs = pl.ds(pl.multiple_of((1 - info[3]) * 1024, 1024), 1024)
    for part, out in ((1, send_ref), (0, keep_ref)):
        rows = slice(part * HALF, part * HALF + HALF)
        for n in range(2):
            dims = slice(n * 512, n * 512 + 512)
            total = dot(gp_ref[rows, mine], w_ref[dims, :1024], (1, 1)) + dot(gp_ref[rows, theirs], w_ref[dims, 1024:], (1, 1))
            out[:, dims] = total.astype(out.dtype)


def normed_back(info, gp, pieces):
    return call(
        normed_back_kernel,
        "normed_back",
        [block(1024, 2048)] + [hbm()] * 5,
        [(block(HALF, 1024), of(f32, HALF, 1024)), (block(HALF, 1024), of(bf16, HALF, 1024))],
        [pltpu.VMEM((1024, 2048), bf16), pltpu.SemaphoreType.DMA((16,))],
        2 * 512 * 1024 * 4096,
        info,
        gp,
        *pieces,
    )


def middle_back_kernel(info, e0_ref, e1_ref, cot_ref, mid_ref, g_ref, w_ref, gm_ref, gb_ref, keep, send):
    n, scale = centred(mid_ref[...])
    eg = (e0_ref[...] + e1_ref[...].astype(f32)) * g_ref[1:]
    lean = eg - jnp.mean(eg, axis=-1, keepdims=True) - n * jnp.mean(eg * n, axis=-1, keepdims=True)
    grad = cot_ref[...].astype(f32) + scale * lean
    gm_ref[...] = grad
    low = grad.astype(bf16)
    gb_ref[...] = low
    for out, at in ((keep, info[3]), (send, 1 - info[3])):
        rows = pl.ds(pl.multiple_of(at * HALF, HALF), HALF)
        out[...] = (dot(low[:, :512], w_ref[0, rows, :], (1, 1)) + dot(low[:, 512:], w_ref[1, rows, :], (1, 1))).astype(bf16)


def middle_back(info, e_keep, e_got, cot, mid, gain, w):
    return call(
        middle_back_kernel,
        "middle_back",
        [block(HALF, 1024)] * 4 + [block(2, 1024), block(2, 1024, 512)],
        [
            (block(HALF, 1024), of(f32, HALF, 1024)),
            (block(HALF, 1024), of(bf16, HALF, 1024)),
            (block(HALF, 512), of(bf16, HALF, 512)),
            (block(HALF, 512), of(bf16, HALF, 512)),
        ],
        [],
        2 * 512 * 1024 * 1024,
        info,
        e_keep,
        e_got,
        cot,
        mid,
        gain,
        w,
    )


def down_grad_kernel(info, c0_ref, c1_ref, act_ref, far, across, beside, own, t_ref):
    g = pl.program_id(0)

    @pl.when(g == 0)
    def _():
        t_ref[:, :HALF] = c0_ref[...].T
        t_ref[:, HALF:] = c1_ref[...].T

    x = lax.rem(info[1] + 1 - lax.rem(g, 2), 2)
    side = lax.rem(info[3] + 1 - g // 2, 2)
    rows = pl.ds(pl.multiple_of(side * 512, 512), 512)
    for half in range(2):
        units = pl.ds(pl.multiple_of(half * 1024 + x * 512, 512), 512)
        total = dot(t_ref[rows, :], act_ref[:, units], (1, 0)).astype(bf16)
        for j in range(2):
            dz = lax.rem(half * 2 + j - info[0] + LINE, LINE)
            for at, ref in enumerate((far, across, beside, own)):

                @pl.when(g == at)
                def _():
                    ref[dz] = total[:, j * 256 : j * 256 + 256]


def down_grad(info, cot_own, cot_sib, act):
    return call(
        down_grad_kernel,
        "down_grad",
        [block(HALF, 1024), block(HALF, 1024), block(1024, 2048)],
        [(block(LINE, 512, 256), of(bf16, LINE, 512, 256))] * 4,
        [pltpu.VMEM((1024, 1024), bf16)],
        2 * 1024 * 1024 * 2048,
        info,
        cot_own,
        cot_sib,
        act,
        grid=(4,),
    )


def stay(g, first):
    return lax.max(0, lax.min(g - first, 1))


def up_grad_kernel(info, n0_ref, n1_ref, gp_ref, far, across, beside, own, t_ref):
    g = pl.program_id(0)

    @pl.when(g == 0)
    def _():
        for dx in range(2):
            for dz in range(LINE):
                chip = lax.rem(info[0] + dz, LINE) * 2 + lax.rem(info[1] + dx, 2)
                cols = pl.ds(pl.multiple_of(chip * 128, 128), 128)
                rows = slice((dx * LINE + dz) * 128, (dx * LINE + dz) * 128 + 128)
                t_ref[rows, :HALF] = n0_ref[:, cols].T
                t_ref[rows, HALF:] = n1_ref[:, cols].T

    total = dot(t_ref[...], gp_ref[...], (1, 0)).astype(bf16).reshape(8, 128, 512)

    @pl.when(g < 2)
    def _():
        across[...] = total[:4]
        far[...] = total[4:]

    @pl.when(g >= 2)
    def _():
        own[...] = total[:4]
        beside[...] = total[4:]


def up_grad(info, nm_own, nm_sib, gp):
    right = pl.BlockSpec((1024, 512), lambda g, s: (0, lax.rem(s[3] + 1 - g // 2, 2) * 2 + lax.rem(g, 2)))
    return call(
        up_grad_kernel,
        "up_grad",
        [block(HALF, 1024), block(HALF, 1024), right],
        [
            (pl.BlockSpec((LINE, 128, 512), lambda g, s, f=f: (0, 0, stay(g, f))), of(bf16, LINE, 128, 1024))
            for f in (0, 0, 2, 2)
        ],
        [pltpu.VMEM((1024, 1024), bf16)],
        2 * 1024 * 512 * 4096,
        info,
        nm_own,
        nm_sib,
        gp,
        grid=(4,),
    )


def out_grad_kernel(info, l0_ref, r0_ref, l1_ref, r1_ref, keep_ref, send_ref):
    for out, at in ((keep_ref, info[3]), (send_ref, 1 - info[3])):
        cols = pl.ds(pl.multiple_of(at * 512, 512), 512)
        total = dot(l0_ref[...], r0_ref[:, cols], (1, 0)) + dot(l1_ref[...], r1_ref[:, cols], (1, 0))
        out[...] = total.astype(bf16).reshape(8, 64, 512)


def out_grad(info, att_t, gb, att_t_sib, gb_sib):
    return call(
        out_grad_kernel,
        "out_grad",
        [block(512, HALF), block(HALF, 1024)] * 2,
        [(block(8, 64, 512), of(bf16, 8, 64, 512))] * 2,
        [],
        2 * 512 * 1024 * 1024,
        info,
        att_t.reshape(512, HALF),
        gb,
        att_t_sib.reshape(512, HALF),
        gb_sib,
    )


def input_back_kernel(info, d0_ref, d1_ref, *refs):
    keep_ref, send_ref, w_ref, sems = refs[4:]
    copies = qkv_copies(info, refs[:4], w_ref, sems, 0, 1536)
    start(copies)
    wait(copies)
    for part, out in ((1, send_ref), (0, keep_ref)):
        at = info[3] if part == 0 else 1 - info[3]
        slots = pl.ds(pl.multiple_of(at * HALF, HALF), HALF)
        for n in range(2):
            dims = slice(n * 512, n * 512 + 512)
            total = dot(d0_ref[slots, :], w_ref[dims, :768], (1, 1)) + dot(d1_ref[slots, :], w_ref[dims, 768:], (1, 1))
            out[:, dims] = total.astype(out.dtype)


def input_back(info, d0, d1, pieces):
    return call(
        input_back_kernel,
        "input_back",
        [block(1024, 768)] * 2 + [hbm()] * 4,
        [(block(HALF, 1024), of(f32, HALF, 1024)), (block(HALF, 1024), of(bf16, HALF, 1024))],
        [pltpu.VMEM((1024, 1536), bf16), pltpu.SemaphoreType.DMA((16,))],
        2 * 1024 * 1024 * 1536,
        info,
        d0,
        d1,
        *pieces,
    )


def qkv_grad_kernel(info, l0_ref, r0_ref, l1_ref, r1_ref, *refs):
    beside, own = refs[-2:]
    total = dot(l0_ref[...], r0_ref[...], (1, 0)) + dot(l1_ref[...], r1_ref[...], (1, 0))
    total = total.astype(bf16).reshape(8, 64, 768)
    own[:, :, :768] = total[:4]
    beside[:, :, :768] = total[4:]
    if len(refs) == 4:
        both = (refs[0][...].astype(f32) + refs[1][...].astype(f32)).astype(bf16)
        own[:, :, 768:] = both[:4]
        beside[:, :, 768:] = both[4:]


def qkv_grad(info, nin_t, dproj, nin_t_sib, dproj_sib, more=()):
    width = 768 + 512 * bool(more)
    return call(
        qkv_grad_kernel,
        "qkv_grad",
        [block(512, 1024), block(1024, 768)] * 2 + [block(8, 64, 512)] * len(more),
        [(block(4, 64, width), of(bf16, 4, 64, width))] * 2,
        [],
        2 * 2048 * 512 * 768,
        info,
        nin_t.reshape(512, 1024),
        dproj,
        nin_t_sib.reshape(512, 1024),
        dproj_sib,
        *more,
    )


def input_norm_kernel(info, xo_ref, xt_ref, g_ref, own_ref, oth_ref, t_ref):
    side = info[3]
    for part, x_ref in ((0, xo_ref), (1, xt_ref)):
        at = side if part == 0 else 1 - side
        normed = (centred(x_ref[...].astype(f32))[0] * g_ref[:1]).astype(bf16)
        t_ref[:, pl.ds(pl.multiple_of(at * HALF, HALF), HALF)] = normed.T
    put_parities(info, t_ref, own_ref, oth_ref)


def input_norm(info, x_own, x_other, gains):
    return call(
        input_norm_kernel,
        "input_norm",
        [block(HALF, 1024), block(HALF, 1024), block(2, 1024)],
        [(block(8, 64, 1024), of(bf16, 8, 64, 1024))] * 2,
        [pltpu.VMEM((1024, 1024), bf16)],
        20 << 20,
        info,
        x_own,
        x_other,
        gains,
    )


def heads_kernel(info, w_ref, got_ref, gain_ref, out_ref):
    side = info[3] == 0
    first, middle, last = w_ref[:, :512], got_ref[:, :512], w_ref[:, 1024:]
    q = jnp.where(side, first, middle)
    k = jnp.where(side, last, first)
    v = jnp.where(side, middle, last)
    for i in range(2):
        for j, part in enumerate((q, k, v)):
            out_ref[:, i * 768 + j * 256 : i * 768 + j * 256 + 256] = part[:, i * 256 : i * 256 + 256]
    lane = lax.broadcasted_iota(jnp.int32, (w_ref.shape[0], 128), 1)
    mine = jnp.broadcast_to(gain_ref[...].astype(f32), lane.shape)
    theirs = jnp.broadcast_to(got_ref[:, 512:513].astype(f32), lane.shape)
    out_ref[:, 1536:] = jnp.where((lane == 0) == side, mine, theirs).astype(bf16)


def heads_of(info, w, got, gains):
    return call(
        heads_kernel,
        "heads",
        [block(64, 1536), block(64, 640), block(64, 1)],
        [(block(64, 1664), of(bf16, 64, 1664))],
        [],
        1 << 16,
        info,
        w,
        got,
        gains,
    )[0]


def by_core_kernel(info, up_ref, own_ref, oth_ref):
    for ref, core in ((own_ref, info[2]), (oth_ref, 1 - info[2])):
        for i, to in enumerate((0, 2, 1, 3)):
            ref[:, to * 256 : to * 256 + 256] = up_ref[:, pl.ds(pl.multiple_of(i * 512 + core * 256, 256), 256)]


def by_core(info, w_up):
    return call(
        by_core_kernel,
        "by_core",
        [block(64, 2048)],
        [(block(64, 1024), of(bf16, 64, 1024))] * 2,
        [],
        1 << 16,
        info,
        w_up,
    )


def both_rows_kernel(info, own_ref, got_ref, out_ref):
    out_ref[pl.ds(pl.multiple_of(info[2] * 64, 64), 64), :] = own_ref[...]
    out_ref[pl.ds(pl.multiple_of((1 - info[2]) * 64, 64), 64), :] = got_ref[...]


def both_rows(info, own, got):
    return call(
        both_rows_kernel,
        "both_rows",
        [block(64, 1024)] * 2,
        [(block(128, 1024), of(bf16, 128, 1024))],
        [],
        1 << 16,
        info,
        own,
        got,
    )[0]


def added_kernel(info, a_ref, b_ref, out_ref):
    out_ref[...] = (a_ref[...].astype(f32) + b_ref[...].astype(f32)).astype(bf16)


def added(info, a, b, name="added"):
    steps = 2
    spec = pl.BlockSpec((a.shape[0] // steps, *a.shape[1:]), lambda i, s: (i,) + (0,) * (a.ndim - 1))
    return call(added_kernel, name, [spec, spec], [(spec, of(bf16, *a.shape))], [], 0, info, a, b, grid=(steps,))[0]


def line_parts_kernel(info, a_ref, b_ref, c_ref, *outs):
    for k, out in enumerate(outs):
        out[...] = (a_ref[k].astype(f32) + b_ref[k].astype(f32) + c_ref[k].astype(f32)).astype(bf16)


def line_parts(info, own, from_x, from_y, name):
    spec, out = block(*own.shape), block(*own.shape[1:])
    return call(
        line_parts_kernel, name, [spec] * 3, [(out, of(bf16, *own.shape[1:]))] * LINE, [], 0, info, own, from_x, from_y
    )


def qkv_parts_kernel(info, a_ref, ax_ref, b_ref, bx_ref, *outs):
    for k, out in enumerate(outs):
        out[:, :1280] = (a_ref[k].astype(f32) + ax_ref[k].astype(f32)).astype(bf16)
        out[:, 1280:] = (b_ref[k].astype(f32) + bx_ref[k].astype(f32)).astype(bf16)


def qkv_parts(info, a, a_x, b, b_x):
    return call(
        qkv_parts_kernel,
        "qkv_parts",
        [block(4, 64, 1280)] * 2 + [block(4, 64, 768)] * 2,
        [(block(64, 2048), of(bf16, 64, 2048))] * LINE,
        [],
        0,
        info,
        a,
        a_x,
        b,
        b_x,
    )


def stack_kernel(info, *refs):
    for k in range(LINE):
        refs[LINE][k] = refs[k][...]


def stacked(info, parts, name):
    shape = parts[0].shape
    return call(
        stack_kernel, name, [block(*shape)] * LINE, [(block(LINE, *shape), of(bf16, LINE, *shape))], [], 0, info, *parts
    )[0]


def touch_kernel(info, a_ref, out_ref):
    out_ref[...] = a_ref[...]


def touch(info, a):
    return call(touch_kernel, "touch", [block(*a.shape)], [(block(*a.shape), of(a.dtype, *a.shape))], [], 0, info, a)[0]


def summed(refs, *at):
    total = refs[0][at].astype(f32)
    for ref in refs[1:]:
        total = total + ref[at].astype(f32)
    return total


def down_sum_kernel(info, *refs):
    refs[4][...] = summed(refs[:4]).T


def down_sum(info, parts):
    return call(
        down_sum_kernel,
        "down_sum",
        [block(512, 256)] * 4,
        [(block(256, 512), of(f32, 256, 512))],
        [],
        0,
        info,
        *parts,
    )[0]


def up_sum_kernel(info, *refs):
    for out, core in ((refs[4], info[2]), (refs[5], 1 - info[2])):
        out[...] = summed(refs[:4], pl.ds(pl.multiple_of(core * 64, 64), 64))


def up_sum(info, parts):
    return call(
        up_sum_kernel,
        "up_sum",
        [block(128, 1024)] * 4,
        [(block(64, 1024), of(f32, 64, 1024))] * 2,
        [],
        0,
        info,
        *parts,
    )


def up_whole_kernel(info, mine_ref, got_ref, w_ref, out_ref, sum_ref):
    for ref, core in ((mine_ref, info[2]), (got_ref, 1 - info[2])):
        for i, place in enumerate((0, 2, 1, 3)):
            cols = pl.ds(pl.multiple_of(i * 512 + core * 256, 256), 256)
            out_ref[:, cols] = ref[:, place * 256 : place * 256 + 256]
    total = jnp.sum(w_ref[...].astype(f32) * out_ref[...], axis=1, keepdims=True)
    sum_ref[...] = jnp.broadcast_to(total, sum_ref.shape)


def up_whole(info, mine, got, w):
    return call(
        up_whole_kernel,
        "up_whole",
        [block(64, 1024)] * 2 + [block(64, 2048)],
        [(block(64, 2048), of(f32, 64, 2048)), (block(64, 128), of(f32, 64, 128))],
        [],
        0,
        info,
        mine,
        got,
        w,
    )


def qkv_sum_kernel(info, *refs):
    heads_ref, mid_ref, keep_ref, send_ref, out_ref = refs[4:]
    total = summed(refs[:4])
    out_ref[...] = total[:, 768:1280]
    groups = (total[:, :768], total[:, 1280:])
    q, k, v = (jnp.concatenate([g[:, j : j + 256] for g in groups], axis=1) for j in (0, 256, 512))
    weights = heads_ref[...].astype(f32)
    by_row = jnp.sum(weights[:, :768] * groups[0], axis=1, keepdims=True) + jnp.sum(
        weights[:, 768:1536] * groups[1], axis=1, keepdims=True
    )
    both = jnp.broadcast_to(by_row, mid_ref.shape)
    first = info[3] == 0
    keep_ref[:, :512] = jnp.where(first, q, k)
    keep_ref[:, 512:1024] = jnp.where(first, k, v)
    keep_ref[:, 1024:] = jnp.where(first, both, mid_ref[...])
    send_ref[:, :512] = jnp.where(first, v, q)
    send_ref[:, 512:] = jnp.where(first, mid_ref[...], both)


def qkv_sum(info, parts, heads, mid_sums):
    return call(
        qkv_sum_kernel,
        "qkv_sum",
        [block(64, 2048)] * 4 + [block(64, 1664), block(64, 128)],
        [
            (block(64, 1152), of(f32, 64, 1152)),
            (block(64, 640), of(f32, 64, 640)),
            (block(64, 512), of(f32, 64, 512)),
        ],
        [],
        0,
        info,
        *parts,
        heads,
        mid_sums,
    )


def qkv_whole_kernel(info, keep_ref, got_ref, gain_ref, out_ref, gg_ref):
    out_ref[:, :512] = keep_ref[:, :512]
    out_ref[:, 512:1024] = got_ref[:, :512]
    out_ref[:, 1024:] = keep_ref[:, 512:1024]
    gg_ref[...] = (keep_ref[:, 1024:1025] + got_ref[:, 512:513]) / gain_ref[...].astype(f32)


def qkv_whole(info, keep, got, gains):
    return call(
        qkv_whole_kernel,
        "qkv_whole",
        [block(64, 1152), block(64, 640), block(64, 1)],
        [(block(64, 1536), of(f32, 64, 1536)), (block(64, 1), of(f32, 64, 1))],
        [],
        0,
        info,
        keep,
        got,
        gains,
    )


def input_grad_kernel(info, x_ref, e0_ref, e1_ref, gm_ref, g_ref, out_ref):
    n, scale = centred(x_ref[...].astype(f32))
    eg = (e0_ref[...] + e1_ref[...].astype(f32)) * g_ref[:1]
    lean = eg - jnp.mean(eg, axis=-1, keepdims=True) - n * jnp.mean(eg * n, axis=-1, keepdims=True)
    out_ref[...] = gm_ref[...] + scale * lean


def input_grad(info, x, e_own, e_got, gm, gains):
    rows = pl.BlockSpec((256, 1024), lambda i, s: (i, 0))
    return call(
        input_grad_kernel,
        "input_grad",
        [rows] * 4 + [block(2, 1024)],
        [(rows, of(f32, HALF, 1024))],
        [],
        0,
        info,
        x,
        e_own,
        e_got,
        gm,
        gains,
        grid=(2,),
    )[0]


def slot_bias(phones, prompts, targets):
    places = jnp.arange(HALF, dtype=jnp.int32)
    count = phones.shape[0]
    segs, is_phone = [], None
    for lengths in (phones + prompts, targets):
        ends = jnp.stack([sum(lengths[i] for i in range(upto + 1)) for upto in range(count)])
        seg = jnp.sum((places[:, None] >= ends[None, :]).astype(jnp.int32), axis=1)
        segs.append(seg)
        if is_phone is None:
            onehot = seg[:, None] == jnp.arange(count, dtype=jnp.int32)[None, :]
            phone_ends = jnp.sum(jnp.where(onehot, (ends - lengths + phones)[None, :], 0), axis=1)
            is_phone = places < phone_ends
    seg = jnp.concatenate(segs)
    phone = jnp.concatenate([is_phone, jnp.zeros((HALF,), dtype=bool)])
    order = jnp.arange(2 * HALF, dtype=jnp.int32)
    allowed = (seg[:, None] == seg[None, :]) & (
        phone[:, None] | (jnp.logical_not(phone)[None, :] & (order[:, None] <= order[None, :]))
    )
    allowed_t = (seg[:, None] == seg[None, :]) & (
        phone[None, :] | (jnp.logical_not(phone)[:, None] & (order[None, :] <= order[:, None]))
    )
    bias = jnp.where(allowed, 0.0, NEG).astype(f32)
    return bias, jnp.where(allowed_t, 0.0, NEG).astype(f32)


def line_shards(tokens, cotangent, gains, w_qkv, w_out, w_up, w_down, phone_len, prompt_len, target_len):
    r = lax.axis_index("rows")
    side = lax.axis_index("pair")
    core = r % 2
    info = jnp.stack([r // 4, r // 2 % 2, core, side]).astype(jnp.int32)
    x_own = tokens[0]
    cot = cotangent[0]

    out_all = lax.all_gather(w_out, ("pair", "rows"), axis=0, tiled=True).reshape(2, 1024, 512)
    crossed = swap_y(jnp.concatenate([w_qkv[:, 512:1024], jnp.pad(gains, ((0, 0), (0, 127)))], axis=1))
    x_other = swap_y(x_own)
    heads = heads_of(info, w_qkv, crossed, gains)
    pieces = along_line(heads)
    up_keep, up_send = by_core(info, after(w_up, heads))
    up_got = swap_c(up_send)
    bias_t, bias = slot_bias(after(phone_len, up_keep)[0], prompt_len[0], target_len[0])
    up_piece = both_rows(info, up_keep, up_got)
    pieces, x_other, bias, bias_t, up_piece = barrier(pieces, x_other, bias, bias_t, up_piece)
    qkv_line = stacked(info, pieces, "qkv_stack")
    beside = swap_x(qkv_line)
    qkv_line_sib = swap_c(qkv_line)
    up_line = along_line(after(up_piece, qkv_line))
    beside_sib = swap_c(beside)
    up_line = stacked(info, up_line, "up_stack")
    up_x, up_y = swap_x(up_line), swap_y(up_line)

    qkv_pieces = (qkv_line, beside, after(qkv_line_sib, up_line), after(beside_sib, up_line))
    projected, gain_all = project(info, x_own, x_other, qkv_pieces)
    down_line = along_line(after(w_down, projected))
    keep0, send0, lse0 = attend(info, projected, after(bias, out_all), 0)
    got0 = swap_y(send0)
    up_x, up_y = after((up_x, up_y), keep0)
    up_far = swap_x(up_y)
    keep1, send1, lse1 = attend(info, projected, after(bias, keep0), 1)
    got1 = swap_y(send1)
    down_line = stacked(info, after(down_line, keep1), "down_stack")
    down_x = swap_x(down_line)
    cot_sib = swap_c(after(cot, keep1))
    nin_t, nin_t_oth = input_norm(info, after(x_own, down_line), x_other, gain_all)
    down_y = swap_y(after(down_line, got0))
    gain_all = touch(info, after(gain_all, nin_t, up_far, got0))
    got1 = after(got1, gain_all)
    mid, nm_own, att_t, att_t_oth = attention_out(info, x_own, (keep0, keep1), (got0, got1), out_all, gain_all)
    nm_sib = swap_c(nm_own)
    nin_t_sib = swap_c(after(nin_t_oth, nm_own))
    att_t_sib = swap_c(att_t_oth)
    up_pieces = (up_line, up_x, up_y, up_far, up_far)
    down_far = [swap_y(down_x[:2]), swap_x(down_y[2:])]
    nm_sib = after(nm_sib, touch(info, after(gain_all, nm_own, down_x, down_y)))
    act, slope = up(info, nm_own, nm_sib, up_pieces)
    down_pieces = (down_line, down_x, down_y, *down_far)
    mixed_keep, mixed_send, gp = down(info, act, slope, cot, cot_sib, mid, down_pieces)

    gp, nin_t_sib, att_t_sib = barrier(gp, nin_t_sib, att_t_sib)
    mixed_got = swap_c(mixed_send)
    e_keep, e_send = normed_back(info, gp, up_pieces)
    e_got = swap_c(e_send)
    far, down_across, down_beside, down_own = down_grad(info, cot, cot_sib, after(act, e_keep))
    down_far, down_x = swap_x(far), swap_x(down_beside)
    gm, gb, ga_keep, ga_send = middle_back(info, after(e_keep, far), after(e_got, far), cot, mid, gain_all, out_all)
    ga_got = swap_y(ga_send)
    gb_sib = swap_c(gb)
    far, up_across, up_beside, up_own = up_grad(info, nm_own, nm_sib, after(gp, gb))
    down_across = added(info, after(down_across, far), after(down_far, far))
    down_y = swap_y(down_across)
    up_far = swap_x(far)
    gb_sib = after(gb_sib, down_across)
    out_keep, out_send = out_grad(info, att_t, after(gb, down_across), att_t_sib, gb_sib)
    out_got = swap_y(out_send)
    ga_got = after(ga_got, out_keep)
    dproj0 = attend_back(info, projected, after(bias_t, out_keep), lse0, ga_keep, ga_got, 0)
    dproj0_sib = swap_c(dproj0)
    down_x, down_y = after((down_x, down_y), dproj0)
    down_parts = line_parts(info, down_own, down_x, down_y, "down_parts")
    down_shift = [shift_z(down_parts[k], k) for k in range(1, LINE)]
    up_x = swap_x(up_beside)
    mixed = added(info, mixed_keep, after(mixed_got, out_got, down_parts), "mixed")
    dproj0_sib = after(dproj0_sib, mixed)
    first_beside, first_own = qkv_grad(info, nin_t, after(dproj0, mixed), nin_t_sib, dproj0_sib, (out_keep, out_got))
    first_x = swap_x(first_beside)
    up_across = added(info, up_across, after(up_far, first_own))
    up_y = swap_y(up_across)
    dproj1 = attend_back(info, projected, after(bias_t, first_own, up_across), lse1, ga_keep, ga_got, 1)
    dproj1_sib = swap_c(dproj1)
    g_down = down_sum(info, (after(down_parts[0], dproj1), *after(down_shift, dproj1)))
    up_x, up_y = after((up_x, up_y), g_down)
    up_parts = line_parts(info, up_own, up_x, up_y, "up_parts")
    up_shift = [shift_z(up_parts[k], k) for k in range(1, LINE)]
    dproj1_sib = after(dproj1_sib, up_parts)
    second_beside, second_own = qkv_grad(info, nin_t, after(dproj1, up_parts), nin_t_sib, dproj1_sib)
    second_x = swap_x(second_beside)
    e_own, e_send = input_back(info, after(dproj0, second_own), dproj1, qkv_pieces)
    e_got = swap_y(e_send)
    first_x, second_x = after((first_x, second_x), e_own)
    heads_parts = qkv_parts(info, first_own, first_x, second_own, second_x)
    qkv_shift = [shift_z(heads_parts[k], k) for k in range(1, LINE)]
    up_mine, up_send = up_sum(info, (after(up_parts[0], heads_parts), *up_shift))
    up_got = swap_c(up_send)
    grad_tokens = input_grad(info, after(x_own, up_mine), e_own, after(e_got, up_mine), gm, gain_all)
    g_up, mid_sums = up_whole(info, up_mine, after(up_got, grad_tokens), w_up)
    keep, send, g_out = qkv_sum(info, (after(heads_parts[0], mid_sums), *after(qkv_shift, mid_sums)), heads, mid_sums)
    got = swap_y(send)
    g_qkv, grad_gains = qkv_whole(info, keep, got, gains)
    return (mixed[None], grad_tokens[None], grad_gains, g_qkv, g_out, g_up, g_down)


def solution(mesh):
    lined = mesh.shape["rows"] == 4 * LINE and mesh.shape["pair"] == 2
    return jax.shard_map(
        line_shards if lined else shards,
        mesh=mesh,
        in_specs=(
            P("rows", "pair", None),
            P("rows", "pair", None),
            P("rows", "pair"),
            P("rows", "pair"),
            P("rows", "pair"),
            P("rows", "pair"),
            P("rows", "pair"),
            P("rows", None),
            P("rows", None),
            P("rows", None),
        ),
        out_specs=(
            P("rows", "pair", None),
            P("rows", "pair", None),
            P("rows", "pair"),
            P("rows", "pair"),
            P("rows", "pair"),
            P("rows", "pair"),
            P("rows", "pair"),
        ),
        check_vma=False,
    )
```

```python
import functools

import jax
import jax.numpy as jnp
from jax import lax
from jax.experimental import pallas as pl
from jax.experimental.pallas import tpu as pltpu
from jax.sharding import PartitionSpec as P

HEADS = 16
HEAD_DIM = 64


epsilon = 1e-05


def passed_along(value, axis, steps):
    count = lax.axis_size(axis)
    leading, last = (max(0, -steps), min(count, count - steps))
    return lax.ppermute(value, axis, [(source, source + steps) for source in range(leading, last)])


def slot_layout(side_index, phones, prompts, targets, slot_count):
    lengths = jnp.where(side_index == 0, phones + prompts, targets)
    count = lengths.shape[0]
    seg_ends = jnp.stack([sum(lengths[i] for i in range(upto + 1)) for upto in range(count)])
    starts = seg_ends - lengths
    places = jnp.arange(slot_count, dtype=jnp.int32)
    segment = jnp.sum((places[:, None] >= seg_ends[None, :]).astype(jnp.int32), axis=1)
    onehot = (segment[:, None] == jnp.arange(lengths.shape[0], dtype=jnp.int32)[None, :]).astype(
        jnp.int32
    )
    within = places - jnp.sum(onehot * starts[None, :], axis=1)
    phone_here = jnp.sum(onehot * phones[None, :], axis=1)
    is_phone = jnp.logical_and(side_index == 0, within < phone_here)
    ordering = places + side_index * slot_count
    return (segment, is_phone, ordering)


def permitted(query_side, key_side):
    query_seg, query_phone, query_order = query_side
    key_seg, key_phone, key_order = key_side
    same_seg = query_seg[:, None] == key_seg[None, :]
    earlier = key_order[None, :] <= query_order[:, None]
    return same_seg & (key_phone[None, :] | jnp.logical_not(query_phone)[:, None] & earlier)


def normalize(values, gain_row):
    centred = values - jnp.mean(values, axis=-1, keepdims=True)
    spread = jnp.mean(centred * centred, axis=-1, keepdims=True)
    return centred * lax.rsqrt(spread + epsilon) * gain_row


def exact_gelu(values):
    return jax.nn.gelu(values, approximate=False)


def softmax_rows(query_piece, key_piece, allowed):
    scores = jnp.einsum(
        "qhd,khd->hqk", query_piece, key_piece, preferred_element_type=jnp.float32
    ) * HEAD_DIM ** (-0.5)
    scores = jnp.where(allowed[None], scores, -1e30)
    row_max = jnp.max(scores, axis=-1, keepdims=True)
    exponents = jnp.exp(scores - row_max)
    return exponents / jnp.sum(exponents, axis=-1, keepdims=True)


def shards(tokens, cotangent, gains, w_qkv, w_out, w_up, w_down, phone_len, prompt_len, target_len):
    slot_count = tokens.shape[1]
    model_width = tokens.shape[2]
    inputs = tokens[0].astype(jnp.float32)
    side_index = lax.axis_index("pair")
    paired = (
        lax.all_gather(gains, "pair", axis=1, tiled=True),
        lax.all_gather(w_qkv, "pair", axis=1, tiled=True),
        lax.all_gather(w_out, "pair", axis=1, tiled=True),
        lax.all_gather(w_up, "pair", axis=1, tiled=True),
        lax.all_gather(w_down, "pair", axis=1, tiled=True),
    )
    gain_all, qkv_all, out_all, up_all, down_all = (
        lax.all_gather(paired[0], "rows", axis=0, tiled=True),
        lax.all_gather(paired[1], "rows", axis=0, tiled=True),
        lax.all_gather(paired[2], "rows", axis=0, tiled=True),
        lax.all_gather(paired[3], "rows", axis=0, tiled=True),
        lax.all_gather(paired[4], "rows", axis=0, tiled=True),
    )
    gain_first = gain_all[:, 0].astype(jnp.float32)
    gain_second = gain_all[:, 1].astype(jnp.float32)
    phones = phone_len[0]
    prompts = prompt_len[0]
    targets = target_len[0]
    own_layout = slot_layout(side_index, phones, prompts, targets, slot_count)
    far_layout = slot_layout(0, phones, prompts, targets, slot_count)
    key_layout = tuple(
        (
            jnp.concatenate([far_part, own_part])
            for far_part, own_part in zip(far_layout, own_layout)
        )
    )
    far_live = jnp.concatenate(
        [jnp.full((slot_count,), side_index == 1), jnp.ones((slot_count,), dtype=bool)]
    )
    normed_in, norm_first_back = jax.vjp(normalize, inputs, gain_first)
    normed_low = normed_in.astype(jnp.bfloat16)
    projected = jnp.dot(normed_low, qkv_all, preferred_element_type=jnp.float32).astype(
        jnp.bfloat16
    )
    queries = projected[:, :model_width]
    near_pairs = projected[:, model_width:]
    far_pairs = passed_along(near_pairs, "pair", 1)
    key_value = jnp.concatenate([far_pairs, near_pairs], axis=0)
    block_rows = min(512, slot_count)
    per_group = min(4, HEADS)
    group_width = per_group * HEAD_DIM
    groups = HEADS // per_group
    steps_total = slot_count // block_rows * groups
    key_count = 2 * slot_count

    def piece_of(item_index):
        row_start = item_index // groups * block_rows
        col_start = item_index % groups * group_width
        query_piece = lax.dynamic_slice(
            queries, (row_start, col_start), (block_rows, group_width)
        ).reshape(block_rows, per_group, HEAD_DIM)
        key_piece = lax.dynamic_slice(key_value, (0, col_start), (key_count, group_width)).reshape(
            key_count, per_group, HEAD_DIM
        )
        value_piece = lax.dynamic_slice(
            key_value, (0, model_width + col_start), (key_count, group_width)
        ).reshape(key_count, per_group, HEAD_DIM)
        query_layout = tuple((member for member in own_layout))
        allowed = permitted(query_layout, key_layout) & far_live[None, :]
        attn_probs = softmax_rows(query_piece, key_piece, allowed)
        return (row_start, col_start, query_piece, key_piece, value_piece, attn_probs)

    def forward_step(item_index, attended):
        row_start, col_start, query_piece, key_piece, value_piece, attn_probs = piece_of(item_index)
        head_mix = jnp.einsum(
            "hqk,khd->qhd",
            attn_probs.astype(jnp.bfloat16),
            value_piece,
            preferred_element_type=jnp.float32,
        )
        return lax.dynamic_update_slice(
            attended, head_mix.reshape(block_rows, group_width), (row_start, col_start)
        )

    attended = lax.fori_loop(
        0, steps_total, forward_step, jnp.zeros((slot_count, model_width), jnp.float32)
    )
    attended_low = attended.astype(jnp.bfloat16)
    middle = inputs + jnp.dot(attended_low, out_all, preferred_element_type=jnp.float32)
    normed_mid, norm_second_back = jax.vjp(normalize, middle, gain_second)
    normed_mid_low = normed_mid.astype(jnp.bfloat16)
    pre_act = jnp.dot(normed_mid_low, up_all, preferred_element_type=jnp.float32)
    activated, gelu_back = jax.vjp(exact_gelu, pre_act)
    activated_low = activated.astype(jnp.bfloat16)
    result = middle + jnp.dot(activated_low, down_all, preferred_element_type=jnp.float32)
    mixed_out = result.astype(jnp.bfloat16)[None]
    qkv_back, out_back, up_back, down_back = (qkv_all, out_all, up_all, down_all)
    grad_result = cotangent[0]
    grad_down = jnp.dot(activated_low.T, grad_result, preferred_element_type=jnp.float32)
    grad_act = jnp.dot(grad_result, down_back.T, preferred_element_type=jnp.float32)
    grad_pre = gelu_back(grad_act)[0].astype(jnp.bfloat16)
    grad_up = jnp.dot(normed_mid_low.T, grad_pre, preferred_element_type=jnp.float32)
    grad_normed_mid = jnp.dot(grad_pre, up_back.T, preferred_element_type=jnp.float32)
    grad_middle_norm, grad_gain_second = norm_second_back(grad_normed_mid)
    grad_middle = grad_result.astype(jnp.float32) + grad_middle_norm
    grad_branch = grad_middle.astype(jnp.bfloat16)
    grad_out = jnp.dot(attended_low.T, grad_branch, preferred_element_type=jnp.float32)
    grad_attended = jnp.dot(grad_branch, out_back.T, preferred_element_type=jnp.float32).astype(
        jnp.bfloat16
    )

    def backward_step(item_index, running):
        grad_queries, grad_pairs = running
        row_start, col_start, query_piece, key_piece, value_piece, attn_probs = piece_of(item_index)
        grad_piece = lax.dynamic_slice(
            grad_attended, (row_start, col_start), (block_rows, group_width)
        ).reshape(block_rows, per_group, HEAD_DIM)
        grad_probs = jnp.einsum(
            "qhd,khd->hqk", grad_piece, value_piece, preferred_element_type=jnp.float32
        )
        centre = jnp.sum(grad_probs * attn_probs, axis=-1, keepdims=True)
        grad_scores = (attn_probs * (grad_probs - centre)).astype(jnp.bfloat16)
        score_scale = HEAD_DIM ** (-0.5)
        query_grad = (
            jnp.einsum("hqk,khd->qhd", grad_scores, key_piece, preferred_element_type=jnp.float32)
            * score_scale
        )
        key_grad = (
            jnp.einsum("hqk,qhd->khd", grad_scores, query_piece, preferred_element_type=jnp.float32)
            * score_scale
        )
        value_grad = jnp.einsum(
            "hqk,qhd->khd",
            attn_probs.astype(jnp.bfloat16),
            grad_piece,
            preferred_element_type=jnp.float32,
        )
        grad_queries = lax.dynamic_update_slice(
            grad_queries, query_grad.reshape(block_rows, group_width), (row_start, col_start)
        )
        key_old = lax.dynamic_slice(grad_pairs, (0, col_start), (key_count, group_width))
        grad_pairs = lax.dynamic_update_slice(
            grad_pairs, key_old + key_grad.reshape(key_count, group_width), (0, col_start)
        )
        value_old = lax.dynamic_slice(
            grad_pairs, (0, model_width + col_start), (key_count, group_width)
        )
        grad_pairs = lax.dynamic_update_slice(
            grad_pairs,
            value_old + value_grad.reshape(key_count, group_width),
            (0, model_width + col_start),
        )
        return (grad_queries, grad_pairs)

    start_state = (
        jnp.zeros((slot_count, model_width), jnp.float32),
        jnp.zeros((key_count, 2 * model_width), jnp.float32),
    )
    grad_queries, grad_pairs = lax.fori_loop(0, steps_total, backward_step, start_state)
    returned = passed_along(grad_pairs[:slot_count].astype(jnp.bfloat16), "pair", -1).astype(
        jnp.float32
    )
    grad_near = (grad_pairs[slot_count:] + returned).astype(jnp.bfloat16)
    grad_projected = jnp.concatenate([grad_queries.astype(jnp.bfloat16), grad_near], axis=1)
    grad_qkv = jnp.dot(normed_low.T, grad_projected, preferred_element_type=jnp.float32)
    grad_normed_in = jnp.dot(grad_projected, qkv_back.T, preferred_element_type=jnp.float32)
    grad_inputs_norm, grad_gain_first = norm_first_back(grad_normed_in)
    grad_tokens = (grad_middle + grad_inputs_norm)[None]
    grad_gains = jnp.stack([grad_gain_first, grad_gain_second], axis=1)
    strips = (
        lax.psum_scatter(grad_gains, "rows", scatter_dimension=0, tiled=True),
        lax.psum_scatter(grad_qkv.astype(jnp.bfloat16), "rows", scatter_dimension=0, tiled=True),
        lax.psum_scatter(grad_out.astype(jnp.bfloat16), "rows", scatter_dimension=0, tiled=True),
        lax.psum_scatter(grad_up.astype(jnp.bfloat16), "rows", scatter_dimension=0, tiled=True),
        lax.psum_scatter(grad_down.astype(jnp.bfloat16), "rows", scatter_dimension=0, tiled=True),
    )
    owned = (
        lax.psum_scatter(
            strips[0].astype(jnp.bfloat16), "pair", scatter_dimension=1, tiled=True
        ).astype(jnp.float32),
        lax.psum_scatter(
            strips[1].astype(jnp.bfloat16), "pair", scatter_dimension=1, tiled=True
        ).astype(jnp.float32),
        lax.psum_scatter(
            strips[2].astype(jnp.bfloat16), "pair", scatter_dimension=1, tiled=True
        ).astype(jnp.float32),
        lax.psum_scatter(
            strips[3].astype(jnp.bfloat16), "pair", scatter_dimension=1, tiled=True
        ).astype(jnp.float32),
        lax.psum_scatter(
            strips[4].astype(jnp.bfloat16), "pair", scatter_dimension=1, tiled=True
        ).astype(jnp.float32),
    )
    return (mixed_out, grad_tokens, owned[0], owned[1], owned[2], owned[3], owned[4])


LINE = 4
HALF = 512
NEG = -1e30
bf16 = jnp.bfloat16
f32 = jnp.float32
VMEM = dict(
    down=24, up=20, normed_back=20, down_grad=20, up_grad=16, middle_back=20, project=20, input_back=18, attend_0=12, attend_1=12,
    attend_back_0=14, attend_back_1=14, attention_out=16, qkv_grad=16, out_grad=10, input_norm=18, input_grad=14
)


def params(name):
    return pltpu.CompilerParams(vmem_limit_bytes=VMEM.get(name, 10) * 1024 * 1024)


PLACES = dict(attend_1=20, touch=20, attend_back_0=20, down_sum=20, up_parts=20, up_sum=20)


def cost(name):
    return pl.CostEstimate(flops=int(PLACES.get(name, 0.5) * 1.15e9), bytes_accessed=1 << 16, transcendentals=0)


def hbm():
    return pl.BlockSpec(memory_space=pl.ANY)


def block(*shape):
    return pl.BlockSpec(shape, lambda i, s: (0,) * len(shape))


def call(kernel, name, ins, outs, scratch, flops, *args, grid=(1,)):
    out = pl.pallas_call(
        kernel,
        grid_spec=pltpu.PrefetchScalarGridSpec(
            num_scalar_prefetch=1,
            grid=grid,
            in_specs=ins,
            out_specs=[spec for spec, _ in outs],
            scratch_shapes=scratch,
        ),
        out_shape=[shape for _, shape in outs],
        compiler_params=params(name),
        cost_estimate=cost(name),
        name=name,
    )(*args)
    return out


def of(kind, *shape):
    return jax.ShapeDtypeStruct(shape, kind)


def dot(a, b, contract):
    return lax.dot_general(a, b, ((contract[:1], contract[1:]), ((), ())), preferred_element_type=f32)


def row_pairs(target):
    pairs = []
    for r in range(LINE * 4):
        z, x, c = target(r // 4, r // 2 % 2, r % 2)
        pairs.append((r, z % LINE * 4 + x * 2 + c))
    return pairs


def shift_z(v, k):
    return lax.ppermute(v, "rows", row_pairs(lambda z, x, c: (z + k, x, c)))


def swap_x(v):
    return lax.ppermute(v, "rows", row_pairs(lambda z, x, c: (z, 1 - x, c)))


def swap_c(v):
    return lax.ppermute(v, "rows", row_pairs(lambda z, x, c: (z, x, 1 - c)))


def swap_y(v):
    return lax.ppermute(v, "pair", [(0, 1), (1, 0)])


def along_line(shard):
    return [shard] + [shift_z(shard, k) for k in range(1, LINE)]


def barrier(*values):
    return lax.optimization_barrier(values)


def after(value, *others):
    return lax.optimization_barrier((value, others))[0]


def qkv_copies(info, refs, w_ref, sems, start_col, cols):
    out = []
    for dx in range(2):
        for dz in range(LINE):
            chip = lax.rem(info[0] + LINE - dz, LINE) * 2 + lax.rem(info[1] + dx, 2)
            for own in (0, 1):
                core = info[2] if own == 0 else 1 - info[2]
                out.append(
                    pltpu.make_async_copy(
                        refs[own * 2 + dx].at[dz, :, pl.ds(start_col, cols)],
                        w_ref.at[pl.ds(pl.multiple_of(chip * 128 + core * 64, 64), 64), :],
                        sems.at[(dx * LINE + dz) * 2 + own],
                    )
                )
    return out


def by_chip(z, x):
    return z * 2 + x


def by_unit(z, x):
    return z // 2 * 4 + x * 2 + z % 2


def piece_copies(info, refs, w_ref, sems, rows, cols, order):
    line, beside, across, far_a, far_b = refs
    out = [[], []]
    for dy in range(2):
        for dx in range(2):
            for dz in range(LINE):
                chip = order(lax.rem(info[0] + LINE - dz, LINE), lax.rem(info[1] + dx, 2))
                ref, at = ((line, dz), (beside, dz), (across, dz), (far_a, dz) if dz < 2 else (far_b, dz + far_b.shape[0] - LINE))[dx + 2 * dy]
                out[dy].append(
                    pltpu.make_async_copy(
                        ref.at[at, :, pl.ds(0, cols)],
                        w_ref.at[pl.ds(pl.multiple_of(chip * rows, rows), rows), pl.ds(dy * cols, cols)],
                        sems.at[(dy * 2 + dx) * LINE + dz],
                    )
                )
    return out


def start(copies):
    for c in copies:
        c.start()


def wait(copies):
    for c in copies:
        c.wait()


def project_kernel(info, xo_ref, xt_ref, *refs):
    out_ref, g_ref, w_ref, gcol_ref, nin_ref, sems = refs[4:]
    copies = qkv_copies(info, refs[:4], w_ref, sems, 0, 1536)
    gains = qkv_copies(info, refs[:4], gcol_ref, sems.at[pl.ds(16, 16)], 1536, 128)
    start(gains)
    start(copies)
    wait(gains)
    both = gcol_ref[...].T.astype(f32)[:2]
    g_ref[...] = both
    side = info[3]
    for part, x_ref in ((0, xo_ref), (1, xt_ref)):
        at = side if part == 0 else 1 - side
        tokens = pl.ds(pl.multiple_of(at * HALF, HALF), HALF)
        nin_ref[tokens, :] = (centred(x_ref[...].astype(f32))[0] * both[:1]).astype(bf16)
        if part == 0:
            wait(copies)
        for n in range(2):
            cols = slice(n * 768, n * 768 + 768)
            out_ref[tokens, cols] = dot(nin_ref[tokens, :], w_ref[:, cols], (1, 0)).astype(bf16)


def project(info, x_own, x_other, pieces):
    return call(
        project_kernel,
        "project",
        [block(HALF, 1024), block(HALF, 1024)] + [hbm()] * 4,
        [(block(1024, 1536), of(bf16, 1024, 1536)), (block(2, 1024), of(f32, 2, 1024))],
        [
            pltpu.VMEM((1024, 1536), bf16),
            pltpu.VMEM((1024, 128), bf16),
            pltpu.VMEM((1024, 1024), bf16),
            pltpu.SemaphoreType.DMA((32,)),
        ],
        2 * 1024 * 1024 * 1536,
        info,
        x_own,
        x_other,
        *pieces,
    )


TILES = ((0, 512), (256, 512), (512, 768), (768, 1024))


def own_lanes(v, head):
    lane = lax.broadcasted_iota(jnp.int32, v.shape, 1)
    return jnp.where((lane >= 64) if head else (lane < 64), v, jnp.zeros_like(v))


def attend_kernel(info, q_ref, k_ref, v_ref, bias_ref, keep_ref, send_ref, lse_ref):
    side = info[3]
    lane = lax.broadcasted_iota(jnp.int32, (256, 128), 1)
    for tile, (first, seen) in enumerate(TILES):
        rows = slice(first, first + 256)
        q_tile = q_ref[rows, :] * jnp.asarray(0.125, bf16)
        done, lse = [], []
        for head in range(2):
            s = dot(own_lanes(q_tile, head), k_ref[:seen, :], (1, 1)) + bias_ref[rows, :seen]
            top = jnp.max(s, axis=1, keepdims=True)
            p = jnp.exp(s - top)
            total = jnp.sum(p, axis=1, keepdims=True)
            lse.append(top + jnp.log(total))
            done.append(dot(p.astype(bf16), v_ref[:seen, :], (1, 0)) * (1.0 / total))
        both = jnp.where(lane < 64, done[0], done[1]).astype(bf16)
        lse_ref[0, :, rows] = jnp.where(lane == 0, lse[0], lse[1]).T[:2]
        half, row = tile // 2, tile % 2 * 256

        @pl.when(side == half)
        def _():
            keep_ref[row : row + 256, :] = both

        @pl.when(side != half)
        def _():
            send_ref[row : row + 256, :] = both


def head_parts(group):
    return [pl.BlockSpec((1024, 128), lambda h, s, j=j: (0, 6 * group + 2 * j + h)) for j in range(3)]


def attend(info, projected, bias, group):
    piece = pl.BlockSpec((HALF, 128), lambda h, s: (0, h))
    return call(
        attend_kernel,
        f"attend_{group}",
        [*head_parts(group), block(1024, 1024)],
        [
            (piece, of(bf16, HALF, 256)),
            (piece, of(bf16, HALF, 256)),
            (pl.BlockSpec((1, 2, 1024), lambda h, s: (h, 0, 0)), of(f32, 2, 2, 1024)),
        ],
        [],
        4 * 1024 * 768 * 64 * 4,
        info,
        projected,
        projected,
        projected,
        bias,
        grid=(2,),
    )


def attend_back_kernel(info, q_ref, k_ref, v_ref, bias_ref, lse_ref, keep_ref, send_ref, out_ref, dk_ref, dv_ref):
    side = info[3]
    pair = pl.program_id(0)
    k_t = k_ref[...].T
    dk_ref[...] = jnp.zeros_like(dk_ref)
    dv_ref[...] = jnp.zeros_like(dv_ref)
    for tile, (start, seen) in enumerate(TILES):
        half, row = tile // 2, tile % 2 * 256
        q_tile = q_ref[start : start + 256, :] * jnp.asarray(0.125, bf16)
        g_tile = jnp.where(side == half, keep_ref[row : row + 256, :], send_ref[row : row + 256, :])
        pieces = []
        for head in range(2):
            q_head = own_lanes(q_tile, head)
            g_head = own_lanes(g_tile, head)
            s = dot(k_ref[:seen, :], q_head, (1, 1))
            p = jnp.exp(s + bias_ref[:seen, start : start + 256] - lse_ref[0, head : head + 1, start : start + 256])
            dp = dot(v_ref[:seen, :], g_head, (1, 1))
            centre = jnp.sum(p * dp, axis=0, keepdims=True)
            ds = (p * (dp - centre)).astype(bf16)
            dv_ref[:seen, :] += dot(p.astype(bf16), g_head, (1, 0))
            dk_ref[:seen, :] += dot(ds, q_head, (1, 0))
            pieces.append(dot(k_t[head * 64 : head * 64 + 64, :seen], ds, (1, 0)) * 0.125)
        cols = pl.ds(pl.multiple_of(pair * 128, 128), 128)
        out_ref[start : start + 256, cols] = jnp.concatenate(pieces, axis=0).T.astype(bf16)
    out_ref[:, pl.ds(pl.multiple_of(256 + pair * 128, 128), 128)] = dk_ref[...].astype(bf16)
    out_ref[:, pl.ds(pl.multiple_of(512 + pair * 128, 128), 128)] = dv_ref[...].astype(bf16)


def attend_back(info, projected, bias, lse, keep, other, group):
    piece = pl.BlockSpec((HALF, 128), lambda h, s: (0, 2 * group + h))
    return pl.pallas_call(
        attend_back_kernel,
        grid_spec=pltpu.PrefetchScalarGridSpec(
            num_scalar_prefetch=1,
            grid=(2,),
            in_specs=[
                *head_parts(group),
                pl.BlockSpec((1024, 1024), lambda h, s: (0, 0)),
                pl.BlockSpec((1, 2, 1024), lambda h, s: (h, 0, 0)),
                piece,
                piece,
            ],
            out_specs=pl.BlockSpec((1024, 768), lambda h, s: (0, 0)),
            scratch_shapes=[pltpu.VMEM((1024, 128), f32), pltpu.VMEM((1024, 128), f32)],
        ),
        out_shape=jax.ShapeDtypeStruct((1024, 768), bf16),
        compiler_params=params(f"attend_back_{group}"),
        cost_estimate=cost(f"attend_back_{group}"),
        name=f"attend_back_{group}",
    )(info, projected, projected, projected, bias, lse, keep, other)


def centred(v):
    off = v - jnp.mean(v, axis=-1, keepdims=True)
    scale = lax.rsqrt(jnp.mean(off * off, axis=-1, keepdims=True) + epsilon)
    return off * scale, scale


def out_kernel(info, x_ref, k0, k1, g0, g1, w_ref, g_ref, mid_ref, nm_ref, own_ref, oth_ref, t_ref):
    places = [(info[3] if i < 2 else 1 - info[3]) * HALF + i % 2 * 256 for i in range(4)]
    places = [pl.ds(pl.multiple_of(at, 256), 256) for at in places]
    for half in range(2):
        cols = slice(half * 512, half * 512 + 512)
        branch = x_ref[:, cols].astype(f32)
        for at, ref in zip(places, (k0, k1, g0, g1)):
            branch = branch + dot(ref[...], w_ref[half, at, :], (1, 0))
        mid_ref[:, cols] = branch
    nm_ref[...] = (centred(mid_ref[...])[0] * g_ref[1:]).astype(bf16)
    for at, ref in zip(places, (k0, k1, g0, g1)):
        t_ref[at, :] = ref[...].T
    put_parities(info, t_ref, own_ref, oth_ref)


def put_parities(info, t_ref, own_ref, oth_ref):
    for dx in range(2):
        for dz in range(LINE):
            chip = lax.rem(info[0] + dz, LINE) * 2 + lax.rem(info[1] + dx, 2)
            here = pl.multiple_of(chip * 128 + info[2] * 64, 64)
            there = pl.multiple_of(chip * 128 + (1 - info[2]) * 64, 64)
            own_ref[dx * LINE + dz] = t_ref[pl.ds(here, 64), :]
            oth_ref[dx * LINE + dz] = t_ref[pl.ds(there, 64), :]


def attention_out(info, x, keeps, gots, w, gain):
    return call(
        out_kernel,
        "attention_out",
        [block(HALF, 1024)] + [block(HALF, 256)] * 4 + [block(2, 1024, 512), block(2, 1024)],
        [
            (block(HALF, 1024), of(f32, HALF, 1024)),
            (block(HALF, 1024), of(bf16, HALF, 1024)),
            (block(8, 64, HALF), of(bf16, 8, 64, HALF)),
            (block(8, 64, HALF), of(bf16, 8, 64, HALF)),
        ],
        [pltpu.VMEM((1024, HALF), bf16)],
        2 * 512 * 1024 * 1024,
        info,
        x,
        *keeps,
        *gots,
        w,
        gain,
    )


def up_kernel(info, x0_ref, x1_ref, *refs):
    act_ref, slope_ref, w_ref, sems = refs[5:]
    step = pl.program_id(0)
    near, far = piece_copies(info, refs[:5], w_ref, sems, 128, 1024, by_chip)

    @pl.when(step == 0)
    def _():
        start(near)
        start(far)
        wait(near)

    @pl.when(step == 1)
    def _():
        wait(far)

    for part, x_ref in enumerate((x0_ref, x1_ref)):
        rows = slice(part * HALF, part * HALF + HALF)
        for n in range(2):
            cols = slice(n * 512, n * 512 + 512)
            pre = dot(x_ref[...], w_ref[:, pl.ds(pl.multiple_of(step * 1024 + n * 512, 512), 512)], (1, 0))
            below = 0.5 * (1.0 + lax.erf(pre * 0.7071067811865476))
            act_ref[rows, cols] = (pre * below).astype(bf16)
            slope_ref[rows, cols] = (below + pre * (0.3989422804014327 * jnp.exp(-0.5 * pre * pre))).astype(bf16)


def up(info, x_own, x_sib, pieces):
    out = pl.BlockSpec((1024, 1024), lambda n, s: (0, lax.rem(s[3] + n, 2)))
    return call(
        up_kernel,
        "up",
        [block(HALF, 1024)] * 2 + [hbm()] * 5,
        [(out, of(bf16, 1024, 2048))] * 2,
        [pltpu.VMEM((1024, 2048), bf16), pltpu.SemaphoreType.DMA((16,))],
        4 * 512 * 1024 * 4096,
        info,
        x_own,
        x_sib,
        *pieces,
        grid=(2,),
    )


def down_kernel(info, act_ref, slope_ref, c0_ref, c1_ref, mid_ref, *refs):
    keep_ref, send_ref, gp_ref, w_ref, acc_ref, sems = refs[5:]
    step = pl.program_id(0)
    side = info[3]
    near, far = piece_copies(info, refs[:5], w_ref, sems, 256, 512, by_unit)
    mine = pl.ds(pl.multiple_of(side * 512, 512), 512)
    theirs = pl.ds(pl.multiple_of((1 - side) * 512, 512), 512)

    @pl.when(step == 0)
    def _():
        start(near)
        start(far)
        wait(near)
        wait(far)

    units = pl.ds(pl.multiple_of(step * 1024, 1024), 1024)
    for part, cot_ref in enumerate((c0_ref, c1_ref)):
        rows = slice(part * HALF, part * HALF + HALF)
        for n in range(2):
            here = pl.ds(pl.multiple_of(step * 1024 + n * 512, 512), 512)
            cols = slice(n * 512, n * 512 + 512)
            back = dot(cot_ref[:, mine], w_ref[here, :512], (1, 1)) + dot(cot_ref[:, theirs], w_ref[here, 512:], (1, 1))
            gp_ref[rows, cols] = (back * slope_ref[rows, cols].astype(f32)).astype(bf16)
        total = dot(act_ref[rows, :], w_ref[units, :], (1, 0))

        @pl.when(step == 0)
        def _():
            acc_ref[rows, :] = total

        @pl.when(step == 1)
        def _():
            done = total + acc_ref[rows, :]
            if part == 0:
                keep_ref[:, mine] = mid_ref[:, mine] + done[:, :512]
                keep_ref[:, theirs] = mid_ref[:, theirs] + done[:, 512:]
            else:
                send_ref[:, mine] = done[:, :512].astype(bf16)
                send_ref[:, theirs] = done[:, 512:].astype(bf16)


def down(info, act, slope, cot_own, cot_sib, mid, pieces):
    tile = pl.BlockSpec((1024, 1024), lambda n, s: (0, n))
    return call(
        down_kernel,
        "down",
        [tile, tile] + [block(HALF, 1024)] * 3 + [hbm()] * 5,
        [
            (block(HALF, 1024), of(f32, HALF, 1024)),
            (block(HALF, 1024), of(bf16, HALF, 1024)),
            (tile, of(bf16, 1024, 2048)),
        ],
        [pltpu.VMEM((2048, 1024), bf16), pltpu.VMEM((1024, 1024), f32), pltpu.SemaphoreType.DMA((16,))],
        4 * 512 * 1024 * 4096,
        info,
        act,
        slope,
        cot_own,
        cot_sib,
        mid,
        *pieces,
        grid=(2,),
    )


def normed_back_kernel(info, gp_ref, *refs):
    keep_ref, send_ref, w_ref, sems = refs[5:]
    near, far = piece_copies(info, refs[:5], w_ref, sems, 128, 1024, by_chip)
    start(near)
    start(far)
    wait(near)
    wait(far)
    mine = pl.ds(pl.multiple_of(info[3] * 1024, 1024), 1024)
    theirs = pl.ds(pl.multiple_of((1 - info[3]) * 1024, 1024), 1024)
    for part, out in ((1, send_ref), (0, keep_ref)):
        rows = slice(part * HALF, part * HALF + HALF)
        for n in range(2):
            dims = slice(n * 512, n * 512 + 512)
            total = dot(gp_ref[rows, mine], w_ref[dims, :1024], (1, 1)) + dot(gp_ref[rows, theirs], w_ref[dims, 1024:], (1, 1))
            out[:, dims] = total.astype(out.dtype)


def normed_back(info, gp, pieces):
    return call(
        normed_back_kernel,
        "normed_back",
        [block(1024, 2048)] + [hbm()] * 5,
        [(block(HALF, 1024), of(f32, HALF, 1024)), (block(HALF, 1024), of(bf16, HALF, 1024))],
        [pltpu.VMEM((1024, 2048), bf16), pltpu.SemaphoreType.DMA((16,))],
        2 * 512 * 1024 * 4096,
        info,
        gp,
        *pieces,
    )


def middle_back_kernel(info, e0_ref, e1_ref, cot_ref, mid_ref, g_ref, w_ref, gm_ref, gb_ref, keep, send):
    n, scale = centred(mid_ref[...])
    eg = (e0_ref[...] + e1_ref[...].astype(f32)) * g_ref[1:]
    lean = eg - jnp.mean(eg, axis=-1, keepdims=True) - n * jnp.mean(eg * n, axis=-1, keepdims=True)
    grad = cot_ref[...].astype(f32) + scale * lean
    gm_ref[...] = grad
    low = grad.astype(bf16)
    gb_ref[...] = low
    for out, at in ((keep, info[3]), (send, 1 - info[3])):
        rows = pl.ds(pl.multiple_of(at * HALF, HALF), HALF)
        out[...] = (dot(low[:, :512], w_ref[0, rows, :], (1, 1)) + dot(low[:, 512:], w_ref[1, rows, :], (1, 1))).astype(bf16)


def middle_back(info, e_keep, e_got, cot, mid, gain, w):
    return call(
        middle_back_kernel,
        "middle_back",
        [block(HALF, 1024)] * 4 + [block(2, 1024), block(2, 1024, 512)],
        [
            (block(HALF, 1024), of(f32, HALF, 1024)),
            (block(HALF, 1024), of(bf16, HALF, 1024)),
            (block(HALF, 512), of(bf16, HALF, 512)),
            (block(HALF, 512), of(bf16, HALF, 512)),
        ],
        [],
        2 * 512 * 1024 * 1024,
        info,
        e_keep,
        e_got,
        cot,
        mid,
        gain,
        w,
    )


def down_grad_kernel(info, c0_ref, c1_ref, act_ref, far, across, beside, own, t_ref):
    g = pl.program_id(0)

    @pl.when(g == 0)
    def _():
        t_ref[:, :HALF] = c0_ref[...].T
        t_ref[:, HALF:] = c1_ref[...].T

    x = lax.rem(info[1] + 1 - lax.rem(g, 2), 2)
    side = lax.rem(info[3] + 1 - g // 2, 2)
    rows = pl.ds(pl.multiple_of(side * 512, 512), 512)
    for half in range(2):
        units = pl.ds(pl.multiple_of(half * 1024 + x * 512, 512), 512)
        total = dot(t_ref[rows, :], act_ref[:, units], (1, 0)).astype(bf16)
        for j in range(2):
            dz = lax.rem(half * 2 + j - info[0] + LINE, LINE)
            for at, ref in enumerate((far, across, beside, own)):

                @pl.when(g == at)
                def _():
                    ref[dz] = total[:, j * 256 : j * 256 + 256]


def down_grad(info, cot_own, cot_sib, act):
    return call(
        down_grad_kernel,
        "down_grad",
        [block(HALF, 1024), block(HALF, 1024), block(1024, 2048)],
        [(block(LINE, 512, 256), of(bf16, LINE, 512, 256))] * 4,
        [pltpu.VMEM((1024, 1024), bf16)],
        2 * 1024 * 1024 * 2048,
        info,
        cot_own,
        cot_sib,
        act,
        grid=(4,),
    )


def stay(g, first):
    return lax.max(0, lax.min(g - first, 1))


def up_grad_kernel(info, n0_ref, n1_ref, gp_ref, far, across, beside, own, t_ref):
    g = pl.program_id(0)

    @pl.when(g == 0)
    def _():
        for dx in range(2):
            for dz in range(LINE):
                chip = lax.rem(info[0] + dz, LINE) * 2 + lax.rem(info[1] + dx, 2)
                cols = pl.ds(pl.multiple_of(chip * 128, 128), 128)
                rows = slice((dx * LINE + dz) * 128, (dx * LINE + dz) * 128 + 128)
                t_ref[rows, :HALF] = n0_ref[:, cols].T
                t_ref[rows, HALF:] = n1_ref[:, cols].T

    total = dot(t_ref[...], gp_ref[...], (1, 0)).astype(bf16).reshape(8, 128, 512)

    @pl.when(g < 2)
    def _():
        across[...] = total[:4]
        far[...] = total[4:]

    @pl.when(g >= 2)
    def _():
        own[...] = total[:4]
        beside[...] = total[4:]


def up_grad(info, nm_own, nm_sib, gp):
    right = pl.BlockSpec((1024, 512), lambda g, s: (0, lax.rem(s[3] + 1 - g // 2, 2) * 2 + lax.rem(g, 2)))
    return call(
        up_grad_kernel,
        "up_grad",
        [block(HALF, 1024), block(HALF, 1024), right],
        [
            (pl.BlockSpec((LINE, 128, 512), lambda g, s, f=f: (0, 0, stay(g, f))), of(bf16, LINE, 128, 1024))
            for f in (0, 0, 2, 2)
        ],
        [pltpu.VMEM((1024, 1024), bf16)],
        2 * 1024 * 512 * 4096,
        info,
        nm_own,
        nm_sib,
        gp,
        grid=(4,),
    )


def out_grad_kernel(info, l0_ref, r0_ref, l1_ref, r1_ref, keep_ref, send_ref):
    for out, at in ((keep_ref, info[3]), (send_ref, 1 - info[3])):
        cols = pl.ds(pl.multiple_of(at * 512, 512), 512)
        total = dot(l0_ref[...], r0_ref[:, cols], (1, 0)) + dot(l1_ref[...], r1_ref[:, cols], (1, 0))
        out[...] = total.astype(bf16).reshape(8, 64, 512)


def out_grad(info, att_t, gb, att_t_sib, gb_sib):
    return call(
        out_grad_kernel,
        "out_grad",
        [block(512, HALF), block(HALF, 1024)] * 2,
        [(block(8, 64, 512), of(bf16, 8, 64, 512))] * 2,
        [],
        2 * 512 * 1024 * 1024,
        info,
        att_t.reshape(512, HALF),
        gb,
        att_t_sib.reshape(512, HALF),
        gb_sib,
    )


def input_back_kernel(info, d0_ref, d1_ref, *refs):
    keep_ref, send_ref, w_ref, sems = refs[4:]
    copies = qkv_copies(info, refs[:4], w_ref, sems, 0, 1536)
    start(copies)
    wait(copies)
    for part, out in ((1, send_ref), (0, keep_ref)):
        at = info[3] if part == 0 else 1 - info[3]
        slots = pl.ds(pl.multiple_of(at * HALF, HALF), HALF)
        for n in range(2):
            dims = slice(n * 512, n * 512 + 512)
            total = dot(d0_ref[slots, :], w_ref[dims, :768], (1, 1)) + dot(d1_ref[slots, :], w_ref[dims, 768:], (1, 1))
            out[:, dims] = total.astype(out.dtype)


def input_back(info, d0, d1, pieces):
    return call(
        input_back_kernel,
        "input_back",
        [block(1024, 768)] * 2 + [hbm()] * 4,
        [(block(HALF, 1024), of(f32, HALF, 1024)), (block(HALF, 1024), of(bf16, HALF, 1024))],
        [pltpu.VMEM((1024, 1536), bf16), pltpu.SemaphoreType.DMA((16,))],
        2 * 1024 * 1024 * 1536,
        info,
        d0,
        d1,
        *pieces,
    )


def qkv_grad_kernel(info, l0_ref, r0_ref, l1_ref, r1_ref, *refs):
    beside, own = refs[-2:]
    total = dot(l0_ref[...], r0_ref[...], (1, 0)) + dot(l1_ref[...], r1_ref[...], (1, 0))
    total = total.astype(bf16).reshape(8, 64, 768)
    own[:, :, :768] = total[:4]
    beside[:, :, :768] = total[4:]
    if len(refs) == 4:
        both = (refs[0][...].astype(f32) + refs[1][...].astype(f32)).astype(bf16)
        own[:, :, 768:] = both[:4]
        beside[:, :, 768:] = both[4:]


def qkv_grad(info, nin_t, dproj, nin_t_sib, dproj_sib, more=()):
    width = 768 + 512 * bool(more)
    return call(
        qkv_grad_kernel,
        "qkv_grad",
        [block(512, 1024), block(1024, 768)] * 2 + [block(8, 64, 512)] * len(more),
        [(block(4, 64, width), of(bf16, 4, 64, width))] * 2,
        [],
        2 * 2048 * 512 * 768,
        info,
        nin_t.reshape(512, 1024),
        dproj,
        nin_t_sib.reshape(512, 1024),
        dproj_sib,
        *more,
    )


def input_norm_kernel(info, xo_ref, xt_ref, g_ref, own_ref, oth_ref, t_ref):
    side = info[3]
    for part, x_ref in ((0, xo_ref), (1, xt_ref)):
        at = side if part == 0 else 1 - side
        normed = (centred(x_ref[...].astype(f32))[0] * g_ref[:1]).astype(bf16)
        t_ref[:, pl.ds(pl.multiple_of(at * HALF, HALF), HALF)] = normed.T
    put_parities(info, t_ref, own_ref, oth_ref)


def input_norm(info, x_own, x_other, gains):
    return call(
        input_norm_kernel,
        "input_norm",
        [block(HALF, 1024), block(HALF, 1024), block(2, 1024)],
        [(block(8, 64, 1024), of(bf16, 8, 64, 1024))] * 2,
        [pltpu.VMEM((1024, 1024), bf16)],
        20 << 20,
        info,
        x_own,
        x_other,
        gains,
    )


def heads_kernel(info, w_ref, got_ref, gain_ref, out_ref):
    side = info[3] == 0
    first, middle, last = w_ref[:, :512], got_ref[:, :512], w_ref[:, 1024:]
    q = jnp.where(side, first, middle)
    k = jnp.where(side, last, first)
    v = jnp.where(side, middle, last)
    for i in range(2):
        for j, part in enumerate((q, k, v)):
            out_ref[:, i * 768 + j * 256 : i * 768 + j * 256 + 256] = part[:, i * 256 : i * 256 + 256]
    lane = lax.broadcasted_iota(jnp.int32, (w_ref.shape[0], 128), 1)
    mine = jnp.broadcast_to(gain_ref[...].astype(f32), lane.shape)
    theirs = jnp.broadcast_to(got_ref[:, 512:513].astype(f32), lane.shape)
    out_ref[:, 1536:] = jnp.where((lane == 0) == side, mine, theirs).astype(bf16)


def heads_of(info, w, got, gains):
    return call(
        heads_kernel,
        "heads",
        [block(64, 1536), block(64, 640), block(64, 1)],
        [(block(64, 1664), of(bf16, 64, 1664))],
        [],
        1 << 16,
        info,
        w,
        got,
        gains,
    )[0]


def by_core_kernel(info, up_ref, own_ref, oth_ref):
    for ref, core in ((own_ref, info[2]), (oth_ref, 1 - info[2])):
        for i, to in enumerate((0, 2, 1, 3)):
            ref[:, to * 256 : to * 256 + 256] = up_ref[:, pl.ds(pl.multiple_of(i * 512 + core * 256, 256), 256)]


def by_core(info, w_up):
    return call(
        by_core_kernel,
        "by_core",
        [block(64, 2048)],
        [(block(64, 1024), of(bf16, 64, 1024))] * 2,
        [],
        1 << 16,
        info,
        w_up,
    )


def both_rows_kernel(info, own_ref, got_ref, out_ref):
    out_ref[pl.ds(pl.multiple_of(info[2] * 64, 64), 64), :] = own_ref[...]
    out_ref[pl.ds(pl.multiple_of((1 - info[2]) * 64, 64), 64), :] = got_ref[...]


def both_rows(info, own, got):
    return call(
        both_rows_kernel,
        "both_rows",
        [block(64, 1024)] * 2,
        [(block(128, 1024), of(bf16, 128, 1024))],
        [],
        1 << 16,
        info,
        own,
        got,
    )[0]


def added_kernel(info, a_ref, b_ref, out_ref):
    out_ref[...] = (a_ref[...].astype(f32) + b_ref[...].astype(f32)).astype(bf16)


def added(info, a, b, name="added"):
    steps = 2
    spec = pl.BlockSpec((a.shape[0] // steps, *a.shape[1:]), lambda i, s: (i,) + (0,) * (a.ndim - 1))
    return call(added_kernel, name, [spec, spec], [(spec, of(bf16, *a.shape))], [], 0, info, a, b, grid=(steps,))[0]


def line_parts_kernel(info, a_ref, b_ref, c_ref, *outs):
    for k, out in enumerate(outs):
        out[...] = (a_ref[k].astype(f32) + b_ref[k].astype(f32) + c_ref[k].astype(f32)).astype(bf16)


def line_parts(info, own, from_x, from_y, name):
    spec, out = block(*own.shape), block(*own.shape[1:])
    return call(
        line_parts_kernel, name, [spec] * 3, [(out, of(bf16, *own.shape[1:]))] * LINE, [], 0, info, own, from_x, from_y
    )


def qkv_parts_kernel(info, a_ref, ax_ref, b_ref, bx_ref, *outs):
    for k, out in enumerate(outs):
        out[:, :1280] = (a_ref[k].astype(f32) + ax_ref[k].astype(f32)).astype(bf16)
        out[:, 1280:] = (b_ref[k].astype(f32) + bx_ref[k].astype(f32)).astype(bf16)


def qkv_parts(info, a, a_x, b, b_x):
    return call(
        qkv_parts_kernel,
        "qkv_parts",
        [block(4, 64, 1280)] * 2 + [block(4, 64, 768)] * 2,
        [(block(64, 2048), of(bf16, 64, 2048))] * LINE,
        [],
        0,
        info,
        a,
        a_x,
        b,
        b_x,
    )


def stack_kernel(info, *refs):
    for k in range(LINE):
        refs[LINE][k] = refs[k][...]


def stacked(info, parts, name):
    shape = parts[0].shape
    return call(
        stack_kernel, name, [block(*shape)] * LINE, [(block(LINE, *shape), of(bf16, LINE, *shape))], [], 0, info, *parts
    )[0]


def touch_kernel(info, a_ref, out_ref):
    out_ref[...] = a_ref[...]


def touch(info, a):
    return call(touch_kernel, "touch", [block(*a.shape)], [(block(*a.shape), of(a.dtype, *a.shape))], [], 0, info, a)[0]


def summed(refs, *at):
    total = refs[0][at].astype(f32)
    for ref in refs[1:]:
        total = total + ref[at].astype(f32)
    return total


def down_sum_kernel(info, *refs):
    refs[4][...] = summed(refs[:4]).T


def down_sum(info, parts):
    return call(
        down_sum_kernel,
        "down_sum",
        [block(512, 256)] * 4,
        [(block(256, 512), of(f32, 256, 512))],
        [],
        0,
        info,
        *parts,
    )[0]


def up_sum_kernel(info, *refs):
    for out, core in ((refs[4], info[2]), (refs[5], 1 - info[2])):
        out[...] = summed(refs[:4], pl.ds(pl.multiple_of(core * 64, 64), 64))


def up_sum(info, parts):
    return call(
        up_sum_kernel,
        "up_sum",
        [block(128, 1024)] * 4,
        [(block(64, 1024), of(f32, 64, 1024))] * 2,
        [],
        0,
        info,
        *parts,
    )


def up_whole_kernel(info, mine_ref, got_ref, w_ref, out_ref, sum_ref):
    for ref, core in ((mine_ref, info[2]), (got_ref, 1 - info[2])):
        for i, place in enumerate((0, 2, 1, 3)):
            cols = pl.ds(pl.multiple_of(i * 512 + core * 256, 256), 256)
            out_ref[:, cols] = ref[:, place * 256 : place * 256 + 256]
    total = jnp.sum(w_ref[...].astype(f32) * out_ref[...], axis=1, keepdims=True)
    sum_ref[...] = jnp.broadcast_to(total, sum_ref.shape)


def up_whole(info, mine, got, w):
    return call(
        up_whole_kernel,
        "up_whole",
        [block(64, 1024)] * 2 + [block(64, 2048)],
        [(block(64, 2048), of(f32, 64, 2048)), (block(64, 128), of(f32, 64, 128))],
        [],
        0,
        info,
        mine,
        got,
        w,
    )


def qkv_sum_kernel(info, *refs):
    heads_ref, mid_ref, keep_ref, send_ref, out_ref = refs[4:]
    total = summed(refs[:4])
    out_ref[...] = total[:, 768:1280]
    groups = (total[:, :768], total[:, 1280:])
    q, k, v = (jnp.concatenate([g[:, j : j + 256] for g in groups], axis=1) for j in (0, 256, 512))
    weights = heads_ref[...].astype(f32)
    by_row = jnp.sum(weights[:, :768] * groups[0], axis=1, keepdims=True) + jnp.sum(
        weights[:, 768:1536] * groups[1], axis=1, keepdims=True
    )
    both = jnp.broadcast_to(by_row, mid_ref.shape)
    first = info[3] == 0
    keep_ref[:, :512] = jnp.where(first, q, k)
    keep_ref[:, 512:1024] = jnp.where(first, k, v)
    keep_ref[:, 1024:] = jnp.where(first, both, mid_ref[...])
    send_ref[:, :512] = jnp.where(first, v, q)
    send_ref[:, 512:] = jnp.where(first, mid_ref[...], both)


def qkv_sum(info, parts, heads, mid_sums):
    return call(
        qkv_sum_kernel,
        "qkv_sum",
        [block(64, 2048)] * 4 + [block(64, 1664), block(64, 128)],
        [
            (block(64, 1152), of(f32, 64, 1152)),
            (block(64, 640), of(f32, 64, 640)),
            (block(64, 512), of(f32, 64, 512)),
        ],
        [],
        0,
        info,
        *parts,
        heads,
        mid_sums,
    )


def qkv_whole_kernel(info, keep_ref, got_ref, gain_ref, out_ref, gg_ref):
    out_ref[:, :512] = keep_ref[:, :512]
    out_ref[:, 512:1024] = got_ref[:, :512]
    out_ref[:, 1024:] = keep_ref[:, 512:1024]
    gg_ref[...] = (keep_ref[:, 1024:1025] + got_ref[:, 512:513]) / gain_ref[...].astype(f32)


def qkv_whole(info, keep, got, gains):
    return call(
        qkv_whole_kernel,
        "qkv_whole",
        [block(64, 1152), block(64, 640), block(64, 1)],
        [(block(64, 1536), of(f32, 64, 1536)), (block(64, 1), of(f32, 64, 1))],
        [],
        0,
        info,
        keep,
        got,
        gains,
    )


def input_grad_kernel(info, x_ref, e0_ref, e1_ref, gm_ref, g_ref, out_ref):
    n, scale = centred(x_ref[...].astype(f32))
    eg = (e0_ref[...] + e1_ref[...].astype(f32)) * g_ref[:1]
    lean = eg - jnp.mean(eg, axis=-1, keepdims=True) - n * jnp.mean(eg * n, axis=-1, keepdims=True)
    out_ref[...] = gm_ref[...] + scale * lean


def input_grad(info, x, e_own, e_got, gm, gains):
    rows = pl.BlockSpec((256, 1024), lambda i, s: (i, 0))
    return call(
        input_grad_kernel,
        "input_grad",
        [rows] * 4 + [block(2, 1024)],
        [(rows, of(f32, HALF, 1024))],
        [],
        0,
        info,
        x,
        e_own,
        e_got,
        gm,
        gains,
        grid=(2,),
    )[0]


def slot_bias(phones, prompts, targets):
    places = jnp.arange(HALF, dtype=jnp.int32)
    count = phones.shape[0]
    segs, is_phone = [], None
    for lengths in (phones + prompts, targets):
        ends = jnp.stack([sum(lengths[i] for i in range(upto + 1)) for upto in range(count)])
        seg = jnp.sum((places[:, None] >= ends[None, :]).astype(jnp.int32), axis=1)
        segs.append(seg)
        if is_phone is None:
            onehot = seg[:, None] == jnp.arange(count, dtype=jnp.int32)[None, :]
            phone_ends = jnp.sum(jnp.where(onehot, (ends - lengths + phones)[None, :], 0), axis=1)
            is_phone = places < phone_ends
    seg = jnp.concatenate(segs)
    phone = jnp.concatenate([is_phone, jnp.zeros((HALF,), dtype=bool)])
    order = jnp.arange(2 * HALF, dtype=jnp.int32)
    allowed = (seg[:, None] == seg[None, :]) & (
        phone[:, None] | (jnp.logical_not(phone)[None, :] & (order[:, None] <= order[None, :]))
    )
    allowed_t = (seg[:, None] == seg[None, :]) & (
        phone[None, :] | (jnp.logical_not(phone)[:, None] & (order[None, :] <= order[:, None]))
    )
    bias = jnp.where(allowed, 0.0, NEG).astype(f32)
    return bias, jnp.where(allowed_t, 0.0, NEG).astype(f32)


def line_shards(tokens, cotangent, gains, w_qkv, w_out, w_up, w_down, phone_len, prompt_len, target_len):
    r = lax.axis_index("rows")
    side = lax.axis_index("pair")
    core = r % 2
    info = jnp.stack([r // 4, r // 2 % 2, core, side]).astype(jnp.int32)
    x_own = tokens[0]
    cot = cotangent[0]

    out_all = lax.all_gather(w_out, ("pair", "rows"), axis=0, tiled=True).reshape(2, 1024, 512)
    crossed = swap_y(jnp.concatenate([w_qkv[:, 512:1024], jnp.pad(gains, ((0, 0), (0, 127)))], axis=1))
    x_other = swap_y(x_own)
    heads = heads_of(info, w_qkv, crossed, gains)
    pieces = along_line(heads)
    up_keep, up_send = by_core(info, after(w_up, heads))
    up_got = swap_c(up_send)
    bias_t, bias = slot_bias(after(phone_len, up_keep)[0], prompt_len[0], target_len[0])
    up_piece = both_rows(info, up_keep, up_got)
    pieces, x_other, bias, bias_t, up_piece = barrier(pieces, x_other, bias, bias_t, up_piece)
    qkv_line = stacked(info, pieces, "qkv_stack")
    beside = swap_x(qkv_line)
    qkv_line_sib = swap_c(qkv_line)
    up_line = along_line(after(up_piece, qkv_line))
    beside_sib = swap_c(beside)
    heads = touch(info, after(heads, up_line))
    up_line = stacked(info, after(up_line, heads, beside_sib, qkv_line_sib), "up_stack")
    up_x, up_y = swap_x(up_line), swap_y(up_line)

    qkv_pieces = (qkv_line, beside, after(qkv_line_sib, up_line), after(beside_sib, up_line))
    projected, gain_all = project(info, x_own, x_other, qkv_pieces)
    down_line = along_line(after(w_down, projected))
    keep0, send0, lse0 = attend(info, projected, bias, 0)
    got0 = swap_y(send0)
    up_x, up_y = after((up_x, up_y), keep0)
    up_far = swap_x(up_y)
    keep1, send1, lse1 = attend(info, projected, after(bias, keep0), 1)
    got1 = swap_y(send1)
    down_line = stacked(info, after(down_line, keep1), "down_stack")
    down_x = swap_x(down_line)
    cot_sib = swap_c(after(cot, keep1))
    nin_t, nin_t_oth = input_norm(info, after(x_own, down_line), x_other, gain_all)
    down_y = swap_y(after(down_line, got0))
    gain_all = touch(info, after(gain_all, nin_t, up_far, got0, out_all))
    got1 = after(got1, gain_all)
    mid, nm_own, att_t, att_t_oth = attention_out(info, x_own, (keep0, keep1), (got0, got1), out_all, gain_all)
    nm_sib = swap_c(nm_own)
    nin_t_sib = swap_c(after(nin_t_oth, nm_own))
    att_t_sib = swap_c(att_t_oth)
    up_pieces = (up_line, up_x, up_y, up_far, up_far)
    down_far = [swap_y(down_x[:2]), swap_x(down_y[2:])]
    gain_all = touch(info, after(gain_all, nm_own, down_x, down_y))
    nm_sib = after(nm_sib, gain_all)
    act, slope = up(info, nm_own, nm_sib, up_pieces)
    down_pieces = (down_line, down_x, down_y, *down_far)
    mixed_keep, mixed_send, gp = down(info, act, slope, cot, cot_sib, mid, down_pieces)

    gp, nin_t_sib, att_t_sib = barrier(gp, nin_t_sib, att_t_sib)
    mixed_got = swap_c(mixed_send)
    e_keep, e_send = normed_back(info, gp, up_pieces)
    e_got = swap_c(e_send)
    far, down_across, down_beside, down_own = down_grad(info, cot, cot_sib, after(act, e_keep))
    down_far, down_x = swap_x(far), swap_x(down_beside)
    gm, gb, ga_keep, ga_send = middle_back(info, after(e_keep, far), after(e_got, far), cot, mid, gain_all, out_all)
    ga_got = swap_y(ga_send)
    gb_sib = swap_c(gb)
    far, up_across, up_beside, up_own = up_grad(info, nm_own, nm_sib, after(gp, gb))
    down_across = added(info, after(down_across, far), after(down_far, far))
    down_y = swap_y(down_across)
    up_far = swap_x(far)
    gb_sib = after(gb_sib, down_across)
    out_keep, out_send = out_grad(info, att_t, after(gb, down_across), att_t_sib, gb_sib)
    out_got = swap_y(out_send)
    ga_got = after(ga_got, out_keep)
    dproj0 = attend_back(info, projected, after(bias_t, out_keep), lse0, ga_keep, ga_got, 0)
    dproj0_sib = swap_c(dproj0)
    down_x, down_y = after((down_x, down_y), dproj0)
    down_parts = line_parts(info, down_own, down_x, down_y, "down_parts")
    down_shift = [shift_z(down_parts[k], k) for k in range(1, LINE)]
    up_x = swap_x(up_beside)
    gain_all = touch(info, after(gain_all, out_got, down_parts))
    dproj0_sib = after(dproj0_sib, gain_all)
    first_beside, first_own = qkv_grad(info, nin_t, after(dproj0, gain_all), nin_t_sib, dproj0_sib, (out_keep, out_got))
    first_x = swap_x(first_beside)
    up_across = added(info, up_across, after(up_far, first_own))
    up_y = swap_y(up_across)
    dproj1 = attend_back(info, projected, after(bias_t, first_own, up_across), lse1, ga_keep, ga_got, 1)
    dproj1_sib = swap_c(dproj1)
    g_down = down_sum(info, (after(down_parts[0], dproj1), *after(down_shift, dproj1)))
    up_x, up_y = after((up_x, up_y), g_down)
    up_parts = line_parts(info, up_own, up_x, up_y, "up_parts")
    up_shift = [shift_z(up_parts[k], k) for k in range(1, LINE)]
    dproj1_sib = after(dproj1_sib, up_parts)
    second_beside, second_own = qkv_grad(info, nin_t, after(dproj1, up_parts), nin_t_sib, dproj1_sib)
    second_x = swap_x(second_beside)
    e_own, e_send = input_back(info, after(dproj0, second_own), dproj1, qkv_pieces)
    e_got = swap_y(e_send)
    first_x, second_x = after((first_x, second_x), e_own)
    heads_parts = qkv_parts(info, first_own, first_x, second_own, second_x)
    qkv_shift = [shift_z(heads_parts[k], k) for k in range(1, LINE)]
    up_mine, up_send = up_sum(info, (after(up_parts[0], heads_parts), *up_shift))
    up_got = swap_c(up_send)
    mixed = added(info, mixed_keep, after(mixed_got, up_mine), "mixed")
    grad_tokens = input_grad(info, after(x_own, mixed), e_own, after(e_got, mixed), gm, gain_all)
    g_up, mid_sums = up_whole(info, up_mine, after(up_got, grad_tokens), w_up)
    keep, send, g_out = qkv_sum(info, (after(heads_parts[0], mid_sums), *after(qkv_shift, mid_sums)), heads, mid_sums)
    got = swap_y(send)
    g_qkv, grad_gains = qkv_whole(info, keep, got, gains)
    return (mixed[None], grad_tokens[None], grad_gains, g_qkv, g_out, g_up, g_down)


def solution(mesh):
    lined = mesh.shape["rows"] == 4 * LINE and mesh.shape["pair"] == 2
    return jax.shard_map(
        line_shards if lined else shards,
        mesh=mesh,
        in_specs=(
            P("rows", "pair", None),
            P("rows", "pair", None),
            P("rows", "pair"),
            P("rows", "pair"),
            P("rows", "pair"),
            P("rows", "pair"),
            P("rows", "pair"),
            P("rows", None),
            P("rows", None),
            P("rows", None),
        ),
        out_specs=(
            P("rows", "pair", None),
            P("rows", "pair", None),
            P("rows", "pair"),
            P("rows", "pair"),
            P("rows", "pair"),
            P("rows", "pair"),
            P("rows", "pair"),
        ),
        check_vma=False,
    )
```

```python
import functools

import jax
import jax.numpy as jnp
from jax import lax
from jax.experimental import pallas as pl
from jax.experimental.pallas import tpu as pltpu
from jax.sharding import PartitionSpec as P

HEADS = 16
HEAD_DIM = 64


epsilon = 1e-05


def passed_along(value, axis, steps):
    count = lax.axis_size(axis)
    leading, last = (max(0, -steps), min(count, count - steps))
    return lax.ppermute(value, axis, [(source, source + steps) for source in range(leading, last)])


def slot_layout(side_index, phones, prompts, targets, slot_count):
    lengths = jnp.where(side_index == 0, phones + prompts, targets)
    count = lengths.shape[0]
    seg_ends = jnp.stack([sum(lengths[i] for i in range(upto + 1)) for upto in range(count)])
    starts = seg_ends - lengths
    places = jnp.arange(slot_count, dtype=jnp.int32)
    segment = jnp.sum((places[:, None] >= seg_ends[None, :]).astype(jnp.int32), axis=1)
    onehot = (segment[:, None] == jnp.arange(lengths.shape[0], dtype=jnp.int32)[None, :]).astype(
        jnp.int32
    )
    within = places - jnp.sum(onehot * starts[None, :], axis=1)
    phone_here = jnp.sum(onehot * phones[None, :], axis=1)
    is_phone = jnp.logical_and(side_index == 0, within < phone_here)
    ordering = places + side_index * slot_count
    return (segment, is_phone, ordering)


def permitted(query_side, key_side):
    query_seg, query_phone, query_order = query_side
    key_seg, key_phone, key_order = key_side
    same_seg = query_seg[:, None] == key_seg[None, :]
    earlier = key_order[None, :] <= query_order[:, None]
    return same_seg & (key_phone[None, :] | jnp.logical_not(query_phone)[:, None] & earlier)


def normalize(values, gain_row):
    centred = values - jnp.mean(values, axis=-1, keepdims=True)
    spread = jnp.mean(centred * centred, axis=-1, keepdims=True)
    return centred * lax.rsqrt(spread + epsilon) * gain_row


def exact_gelu(values):
    return jax.nn.gelu(values, approximate=False)


def softmax_rows(query_piece, key_piece, allowed):
    scores = jnp.einsum(
        "qhd,khd->hqk", query_piece, key_piece, preferred_element_type=jnp.float32
    ) * HEAD_DIM ** (-0.5)
    scores = jnp.where(allowed[None], scores, -1e30)
    row_max = jnp.max(scores, axis=-1, keepdims=True)
    exponents = jnp.exp(scores - row_max)
    return exponents / jnp.sum(exponents, axis=-1, keepdims=True)


def shards(tokens, cotangent, gains, w_qkv, w_out, w_up, w_down, phone_len, prompt_len, target_len):
    slot_count = tokens.shape[1]
    model_width = tokens.shape[2]
    inputs = tokens[0].astype(jnp.float32)
    side_index = lax.axis_index("pair")
    paired = (
        lax.all_gather(gains, "pair", axis=1, tiled=True),
        lax.all_gather(w_qkv, "pair", axis=1, tiled=True),
        lax.all_gather(w_out, "pair", axis=1, tiled=True),
        lax.all_gather(w_up, "pair", axis=1, tiled=True),
        lax.all_gather(w_down, "pair", axis=1, tiled=True),
    )
    gain_all, qkv_all, out_all, up_all, down_all = (
        lax.all_gather(paired[0], "rows", axis=0, tiled=True),
        lax.all_gather(paired[1], "rows", axis=0, tiled=True),
        lax.all_gather(paired[2], "rows", axis=0, tiled=True),
        lax.all_gather(paired[3], "rows", axis=0, tiled=True),
        lax.all_gather(paired[4], "rows", axis=0, tiled=True),
    )
    gain_first = gain_all[:, 0].astype(jnp.float32)
    gain_second = gain_all[:, 1].astype(jnp.float32)
    phones = phone_len[0]
    prompts = prompt_len[0]
    targets = target_len[0]
    own_layout = slot_layout(side_index, phones, prompts, targets, slot_count)
    far_layout = slot_layout(0, phones, prompts, targets, slot_count)
    key_layout = tuple(
        (
            jnp.concatenate([far_part, own_part])
            for far_part, own_part in zip(far_layout, own_layout)
        )
    )
    far_live = jnp.concatenate(
        [jnp.full((slot_count,), side_index == 1), jnp.ones((slot_count,), dtype=bool)]
    )
    normed_in, norm_first_back = jax.vjp(normalize, inputs, gain_first)
    normed_low = normed_in.astype(jnp.bfloat16)
    projected = jnp.dot(normed_low, qkv_all, preferred_element_type=jnp.float32).astype(
        jnp.bfloat16
    )
    queries = projected[:, :model_width]
    near_pairs = projected[:, model_width:]
    far_pairs = passed_along(near_pairs, "pair", 1)
    key_value = jnp.concatenate([far_pairs, near_pairs], axis=0)
    block_rows = min(512, slot_count)
    per_group = min(4, HEADS)
    group_width = per_group * HEAD_DIM
    groups = HEADS // per_group
    steps_total = slot_count // block_rows * groups
    key_count = 2 * slot_count

    def piece_of(item_index):
        row_start = item_index // groups * block_rows
        col_start = item_index % groups * group_width
        query_piece = lax.dynamic_slice(
            queries, (row_start, col_start), (block_rows, group_width)
        ).reshape(block_rows, per_group, HEAD_DIM)
        key_piece = lax.dynamic_slice(key_value, (0, col_start), (key_count, group_width)).reshape(
            key_count, per_group, HEAD_DIM
        )
        value_piece = lax.dynamic_slice(
            key_value, (0, model_width + col_start), (key_count, group_width)
        ).reshape(key_count, per_group, HEAD_DIM)
        query_layout = tuple((member for member in own_layout))
        allowed = permitted(query_layout, key_layout) & far_live[None, :]
        attn_probs = softmax_rows(query_piece, key_piece, allowed)
        return (row_start, col_start, query_piece, key_piece, value_piece, attn_probs)

    def forward_step(item_index, attended):
        row_start, col_start, query_piece, key_piece, value_piece, attn_probs = piece_of(item_index)
        head_mix = jnp.einsum(
            "hqk,khd->qhd",
            attn_probs.astype(jnp.bfloat16),
            value_piece,
            preferred_element_type=jnp.float32,
        )
        return lax.dynamic_update_slice(
            attended, head_mix.reshape(block_rows, group_width), (row_start, col_start)
        )

    attended = lax.fori_loop(
        0, steps_total, forward_step, jnp.zeros((slot_count, model_width), jnp.float32)
    )
    attended_low = attended.astype(jnp.bfloat16)
    middle = inputs + jnp.dot(attended_low, out_all, preferred_element_type=jnp.float32)
    normed_mid, norm_second_back = jax.vjp(normalize, middle, gain_second)
    normed_mid_low = normed_mid.astype(jnp.bfloat16)
    pre_act = jnp.dot(normed_mid_low, up_all, preferred_element_type=jnp.float32)
    activated, gelu_back = jax.vjp(exact_gelu, pre_act)
    activated_low = activated.astype(jnp.bfloat16)
    result = middle + jnp.dot(activated_low, down_all, preferred_element_type=jnp.float32)
    mixed_out = result.astype(jnp.bfloat16)[None]
    qkv_back, out_back, up_back, down_back = (qkv_all, out_all, up_all, down_all)
    grad_result = cotangent[0]
    grad_down = jnp.dot(activated_low.T, grad_result, preferred_element_type=jnp.float32)
    grad_act = jnp.dot(grad_result, down_back.T, preferred_element_type=jnp.float32)
    grad_pre = gelu_back(grad_act)[0].astype(jnp.bfloat16)
    grad_up = jnp.dot(normed_mid_low.T, grad_pre, preferred_element_type=jnp.float32)
    grad_normed_mid = jnp.dot(grad_pre, up_back.T, preferred_element_type=jnp.float32)
    grad_middle_norm, grad_gain_second = norm_second_back(grad_normed_mid)
    grad_middle = grad_result.astype(jnp.float32) + grad_middle_norm
    grad_branch = grad_middle.astype(jnp.bfloat16)
    grad_out = jnp.dot(attended_low.T, grad_branch, preferred_element_type=jnp.float32)
    grad_attended = jnp.dot(grad_branch, out_back.T, preferred_element_type=jnp.float32).astype(
        jnp.bfloat16
    )

    def backward_step(item_index, running):
        grad_queries, grad_pairs = running
        row_start, col_start, query_piece, key_piece, value_piece, attn_probs = piece_of(item_index)
        grad_piece = lax.dynamic_slice(
            grad_attended, (row_start, col_start), (block_rows, group_width)
        ).reshape(block_rows, per_group, HEAD_DIM)
        grad_probs = jnp.einsum(
            "qhd,khd->hqk", grad_piece, value_piece, preferred_element_type=jnp.float32
        )
        centre = jnp.sum(grad_probs * attn_probs, axis=-1, keepdims=True)
        grad_scores = (attn_probs * (grad_probs - centre)).astype(jnp.bfloat16)
        score_scale = HEAD_DIM ** (-0.5)
        query_grad = (
            jnp.einsum("hqk,khd->qhd", grad_scores, key_piece, preferred_element_type=jnp.float32)
            * score_scale
        )
        key_grad = (
            jnp.einsum("hqk,qhd->khd", grad_scores, query_piece, preferred_element_type=jnp.float32)
            * score_scale
        )
        value_grad = jnp.einsum(
            "hqk,qhd->khd",
            attn_probs.astype(jnp.bfloat16),
            grad_piece,
            preferred_element_type=jnp.float32,
        )
        grad_queries = lax.dynamic_update_slice(
            grad_queries, query_grad.reshape(block_rows, group_width), (row_start, col_start)
        )
        key_old = lax.dynamic_slice(grad_pairs, (0, col_start), (key_count, group_width))
        grad_pairs = lax.dynamic_update_slice(
            grad_pairs, key_old + key_grad.reshape(key_count, group_width), (0, col_start)
        )
        value_old = lax.dynamic_slice(
            grad_pairs, (0, model_width + col_start), (key_count, group_width)
        )
        grad_pairs = lax.dynamic_update_slice(
            grad_pairs,
            value_old + value_grad.reshape(key_count, group_width),
            (0, model_width + col_start),
        )
        return (grad_queries, grad_pairs)

    start_state = (
        jnp.zeros((slot_count, model_width), jnp.float32),
        jnp.zeros((key_count, 2 * model_width), jnp.float32),
    )
    grad_queries, grad_pairs = lax.fori_loop(0, steps_total, backward_step, start_state)
    returned = passed_along(grad_pairs[:slot_count].astype(jnp.bfloat16), "pair", -1).astype(
        jnp.float32
    )
    grad_near = (grad_pairs[slot_count:] + returned).astype(jnp.bfloat16)
    grad_projected = jnp.concatenate([grad_queries.astype(jnp.bfloat16), grad_near], axis=1)
    grad_qkv = jnp.dot(normed_low.T, grad_projected, preferred_element_type=jnp.float32)
    grad_normed_in = jnp.dot(grad_projected, qkv_back.T, preferred_element_type=jnp.float32)
    grad_inputs_norm, grad_gain_first = norm_first_back(grad_normed_in)
    grad_tokens = (grad_middle + grad_inputs_norm)[None]
    grad_gains = jnp.stack([grad_gain_first, grad_gain_second], axis=1)
    strips = (
        lax.psum_scatter(grad_gains, "rows", scatter_dimension=0, tiled=True),
        lax.psum_scatter(grad_qkv.astype(jnp.bfloat16), "rows", scatter_dimension=0, tiled=True),
        lax.psum_scatter(grad_out.astype(jnp.bfloat16), "rows", scatter_dimension=0, tiled=True),
        lax.psum_scatter(grad_up.astype(jnp.bfloat16), "rows", scatter_dimension=0, tiled=True),
        lax.psum_scatter(grad_down.astype(jnp.bfloat16), "rows", scatter_dimension=0, tiled=True),
    )
    owned = (
        lax.psum_scatter(
            strips[0].astype(jnp.bfloat16), "pair", scatter_dimension=1, tiled=True
        ).astype(jnp.float32),
        lax.psum_scatter(
            strips[1].astype(jnp.bfloat16), "pair", scatter_dimension=1, tiled=True
        ).astype(jnp.float32),
        lax.psum_scatter(
            strips[2].astype(jnp.bfloat16), "pair", scatter_dimension=1, tiled=True
        ).astype(jnp.float32),
        lax.psum_scatter(
            strips[3].astype(jnp.bfloat16), "pair", scatter_dimension=1, tiled=True
        ).astype(jnp.float32),
        lax.psum_scatter(
            strips[4].astype(jnp.bfloat16), "pair", scatter_dimension=1, tiled=True
        ).astype(jnp.float32),
    )
    return (mixed_out, grad_tokens, owned[0], owned[1], owned[2], owned[3], owned[4])


LINE = 4
HALF = 512
NEG = -1e30
bf16 = jnp.bfloat16
f32 = jnp.float32
VMEM = dict(
    down=24, up=20, normed_back=20, down_grad=20, up_grad=16, middle_back=20, project=20, input_back=18, attend_0=12, attend_1=12,
    attend_back_0=14, attend_back_1=14, attention_out=16, qkv_grad=16, out_grad=10, input_norm=18, input_grad=14
)


def params(name):
    return pltpu.CompilerParams(vmem_limit_bytes=VMEM.get(name, 10) * 1024 * 1024)


PLACES = dict(attend_1=20, touch=20, attend_back_0=20, down_sum=20, up_parts=20, up_sum=20)


def cost(name):
    return pl.CostEstimate(flops=int(PLACES.get(name, 0.5) * 1.15e9), bytes_accessed=1 << 16, transcendentals=0)


def hbm():
    return pl.BlockSpec(memory_space=pl.ANY)


def block(*shape):
    return pl.BlockSpec(shape, lambda i, s: (0,) * len(shape))


def call(kernel, name, ins, outs, scratch, flops, *args, grid=(1,)):
    out = pl.pallas_call(
        kernel,
        grid_spec=pltpu.PrefetchScalarGridSpec(
            num_scalar_prefetch=1,
            grid=grid,
            in_specs=ins,
            out_specs=[spec for spec, _ in outs],
            scratch_shapes=scratch,
        ),
        out_shape=[shape for _, shape in outs],
        compiler_params=params(name),
        cost_estimate=cost(name),
        name=name,
    )(*args)
    return out


def of(kind, *shape):
    return jax.ShapeDtypeStruct(shape, kind)


def dot(a, b, contract):
    return lax.dot_general(a, b, ((contract[:1], contract[1:]), ((), ())), preferred_element_type=f32)


def row_pairs(target):
    pairs = []
    for r in range(LINE * 4):
        z, x, c = target(r // 4, r // 2 % 2, r % 2)
        pairs.append((r, z % LINE * 4 + x * 2 + c))
    return pairs


def shift_z(v, k):
    return lax.ppermute(v, "rows", row_pairs(lambda z, x, c: (z + k, x, c)))


def swap_x(v):
    return lax.ppermute(v, "rows", row_pairs(lambda z, x, c: (z, 1 - x, c)))


def swap_c(v):
    return lax.ppermute(v, "rows", row_pairs(lambda z, x, c: (z, x, 1 - c)))


def swap_y(v):
    return lax.ppermute(v, "pair", [(0, 1), (1, 0)])


def along_line(shard):
    return [shard] + [shift_z(shard, k) for k in range(1, LINE)]


def barrier(*values):
    return lax.optimization_barrier(values)


def after(value, *others):
    return lax.optimization_barrier((value, others))[0]


def qkv_copies(info, refs, w_ref, sems, start_col, cols):
    out = []
    for dx in range(2):
        for dz in range(LINE):
            chip = lax.rem(info[0] + LINE - dz, LINE) * 2 + lax.rem(info[1] + dx, 2)
            for own in (0, 1):
                core = info[2] if own == 0 else 1 - info[2]
                out.append(
                    pltpu.make_async_copy(
                        refs[own * 2 + dx].at[dz, :, pl.ds(start_col, cols)],
                        w_ref.at[pl.ds(pl.multiple_of(chip * 128 + core * 64, 64), 64), :],
                        sems.at[(dx * LINE + dz) * 2 + own],
                    )
                )
    return out


def by_chip(z, x):
    return z * 2 + x


def by_unit(z, x):
    return z // 2 * 4 + x * 2 + z % 2


def piece_copies(info, refs, w_ref, sems, rows, cols, order):
    line, beside, across, far_a, far_b = refs
    out = [[], []]
    for dy in range(2):
        for dx in range(2):
            for dz in range(LINE):
                chip = order(lax.rem(info[0] + LINE - dz, LINE), lax.rem(info[1] + dx, 2))
                ref, at = ((line, dz), (beside, dz), (across, dz), (far_a, dz) if dz < 2 else (far_b, dz + far_b.shape[0] - LINE))[dx + 2 * dy]
                out[dy].append(
                    pltpu.make_async_copy(
                        ref.at[at, :, pl.ds(0, cols)],
                        w_ref.at[pl.ds(pl.multiple_of(chip * rows, rows), rows), pl.ds(dy * cols, cols)],
                        sems.at[(dy * 2 + dx) * LINE + dz],
                    )
                )
    return out


def start(copies):
    for c in copies:
        c.start()


def wait(copies):
    for c in copies:
        c.wait()


def project_kernel(info, xo_ref, xt_ref, *refs):
    out_ref, g_ref, w_ref, gcol_ref, nin_ref, sems = refs[4:]
    copies = qkv_copies(info, refs[:4], w_ref, sems, 0, 1536)
    gains = qkv_copies(info, refs[:4], gcol_ref, sems.at[pl.ds(16, 16)], 1536, 128)
    start(gains)
    start(copies)
    wait(gains)
    both = gcol_ref[...].T.astype(f32)[:2]
    g_ref[...] = both
    side = info[3]
    for part, x_ref in ((0, xo_ref), (1, xt_ref)):
        at = side if part == 0 else 1 - side
        tokens = pl.ds(pl.multiple_of(at * HALF, HALF), HALF)
        nin_ref[tokens, :] = (centred(x_ref[...].astype(f32))[0] * both[:1]).astype(bf16)
        if part == 0:
            wait(copies)
        for n in range(2):
            cols = slice(n * 768, n * 768 + 768)
            out_ref[tokens, cols] = dot(nin_ref[tokens, :], w_ref[:, cols], (1, 0)).astype(bf16)


def project(info, x_own, x_other, pieces):
    return call(
        project_kernel,
        "project",
        [block(HALF, 1024), block(HALF, 1024)] + [hbm()] * 4,
        [(block(1024, 1536), of(bf16, 1024, 1536)), (block(2, 1024), of(f32, 2, 1024))],
        [
            pltpu.VMEM((1024, 1536), bf16),
            pltpu.VMEM((1024, 128), bf16),
            pltpu.VMEM((1024, 1024), bf16),
            pltpu.SemaphoreType.DMA((32,)),
        ],
        2 * 1024 * 1024 * 1536,
        info,
        x_own,
        x_other,
        *pieces,
    )


TILES = ((0, 512), (256, 512), (512, 768), (768, 1024))


def own_lanes(v, head):
    lane = lax.broadcasted_iota(jnp.int32, v.shape, 1)
    return jnp.where((lane >= 64) if head else (lane < 64), v, jnp.zeros_like(v))


def attend_kernel(info, q_ref, k_ref, v_ref, bias_ref, keep_ref, send_ref, lse_ref):
    side = info[3]
    lane = lax.broadcasted_iota(jnp.int32, (256, 128), 1)
    for tile, (first, seen) in enumerate(TILES):
        rows = slice(first, first + 256)
        q_tile = q_ref[rows, :] * jnp.asarray(0.125, bf16)
        done, lse = [], []
        for head in range(2):
            s = dot(own_lanes(q_tile, head), k_ref[:seen, :], (1, 1)) + bias_ref[rows, :seen]
            top = jnp.max(s, axis=1, keepdims=True)
            p = jnp.exp(s - top)
            total = jnp.sum(p, axis=1, keepdims=True)
            lse.append(top + jnp.log(total))
            done.append(dot(p.astype(bf16), v_ref[:seen, :], (1, 0)) * (1.0 / total))
        both = jnp.where(lane < 64, done[0], done[1]).astype(bf16)
        lse_ref[0, :, rows] = jnp.where(lane == 0, lse[0], lse[1]).T[:2]
        half, row = tile // 2, tile % 2 * 256

        @pl.when(side == half)
        def _():
            keep_ref[row : row + 256, :] = both

        @pl.when(side != half)
        def _():
            send_ref[row : row + 256, :] = both


def head_parts(group):
    return [pl.BlockSpec((1024, 128), lambda h, s, j=j: (0, 6 * group + 2 * j + h)) for j in range(3)]


def attend(info, projected, bias, group):
    piece = pl.BlockSpec((HALF, 128), lambda h, s: (0, h))
    return call(
        attend_kernel,
        f"attend_{group}",
        [*head_parts(group), block(1024, 1024)],
        [
            (piece, of(bf16, HALF, 256)),
            (piece, of(bf16, HALF, 256)),
            (pl.BlockSpec((1, 2, 1024), lambda h, s: (h, 0, 0)), of(f32, 2, 2, 1024)),
        ],
        [],
        4 * 1024 * 768 * 64 * 4,
        info,
        projected,
        projected,
        projected,
        bias,
        grid=(2,),
    )


def attend_back_kernel(info, q_ref, k_ref, v_ref, bias_ref, lse_ref, keep_ref, send_ref, out_ref, dk_ref, dv_ref):
    side = info[3]
    pair = pl.program_id(0)
    k_t = k_ref[...].T
    dk_ref[...] = jnp.zeros_like(dk_ref)
    dv_ref[...] = jnp.zeros_like(dv_ref)
    for tile, (start, seen) in enumerate(TILES):
        half, row = tile // 2, tile % 2 * 256
        q_tile = q_ref[start : start + 256, :] * jnp.asarray(0.125, bf16)
        g_tile = jnp.where(side == half, keep_ref[row : row + 256, :], send_ref[row : row + 256, :])
        pieces = []
        for head in range(2):
            q_head = own_lanes(q_tile, head)
            g_head = own_lanes(g_tile, head)
            s = dot(k_ref[:seen, :], q_head, (1, 1))
            p = jnp.exp(s + bias_ref[:seen, start : start + 256] - lse_ref[0, head : head + 1, start : start + 256])
            dp = dot(v_ref[:seen, :], g_head, (1, 1))
            centre = jnp.sum(p * dp, axis=0, keepdims=True)
            ds = (p * (dp - centre)).astype(bf16)
            dv_ref[:seen, :] += dot(p.astype(bf16), g_head, (1, 0))
            dk_ref[:seen, :] += dot(ds, q_head, (1, 0))
            pieces.append(dot(k_t[head * 64 : head * 64 + 64, :seen], ds, (1, 0)) * 0.125)
        cols = pl.ds(pl.multiple_of(pair * 128, 128), 128)
        out_ref[start : start + 256, cols] = jnp.concatenate(pieces, axis=0).T.astype(bf16)
    out_ref[:, pl.ds(pl.multiple_of(256 + pair * 128, 128), 128)] = dk_ref[...].astype(bf16)
    out_ref[:, pl.ds(pl.multiple_of(512 + pair * 128, 128), 128)] = dv_ref[...].astype(bf16)


def attend_back(info, projected, bias, lse, keep, other, group):
    piece = pl.BlockSpec((HALF, 128), lambda h, s: (0, 2 * group + h))
    return pl.pallas_call(
        attend_back_kernel,
        grid_spec=pltpu.PrefetchScalarGridSpec(
            num_scalar_prefetch=1,
            grid=(2,),
            in_specs=[
                *head_parts(group),
                pl.BlockSpec((1024, 1024), lambda h, s: (0, 0)),
                pl.BlockSpec((1, 2, 1024), lambda h, s: (h, 0, 0)),
                piece,
                piece,
            ],
            out_specs=pl.BlockSpec((1024, 768), lambda h, s: (0, 0)),
            scratch_shapes=[pltpu.VMEM((1024, 128), f32), pltpu.VMEM((1024, 128), f32)],
        ),
        out_shape=jax.ShapeDtypeStruct((1024, 768), bf16),
        compiler_params=params(f"attend_back_{group}"),
        cost_estimate=cost(f"attend_back_{group}"),
        name=f"attend_back_{group}",
    )(info, projected, projected, projected, bias, lse, keep, other)


def centred(v):
    off = v - jnp.mean(v, axis=-1, keepdims=True)
    scale = lax.rsqrt(jnp.mean(off * off, axis=-1, keepdims=True) + epsilon)
    return off * scale, scale


def out_kernel(info, x_ref, k0, k1, g0, g1, w_ref, g_ref, mid_ref, nm_ref, own_ref, oth_ref, t_ref):
    places = [(info[3] if i < 2 else 1 - info[3]) * HALF + i % 2 * 256 for i in range(4)]
    places = [pl.ds(pl.multiple_of(at, 256), 256) for at in places]
    for half in range(2):
        cols = slice(half * 512, half * 512 + 512)
        branch = x_ref[:, cols].astype(f32)
        for at, ref in zip(places, (k0, k1, g0, g1)):
            branch = branch + dot(ref[...], w_ref[half, at, :], (1, 0))
        mid_ref[:, cols] = branch
    nm_ref[...] = (centred(mid_ref[...])[0] * g_ref[1:]).astype(bf16)
    for at, ref in zip(places, (k0, k1, g0, g1)):
        t_ref[at, :] = ref[...].T
    put_parities(info, t_ref, own_ref, oth_ref)


def put_parities(info, t_ref, own_ref, oth_ref):
    for dx in range(2):
        for dz in range(LINE):
            chip = lax.rem(info[0] + dz, LINE) * 2 + lax.rem(info[1] + dx, 2)
            here = pl.multiple_of(chip * 128 + info[2] * 64, 64)
            there = pl.multiple_of(chip * 128 + (1 - info[2]) * 64, 64)
            own_ref[dx * LINE + dz] = t_ref[pl.ds(here, 64), :]
            oth_ref[dx * LINE + dz] = t_ref[pl.ds(there, 64), :]


def attention_out(info, x, keeps, gots, w, gain):
    return call(
        out_kernel,
        "attention_out",
        [block(HALF, 1024)] + [block(HALF, 256)] * 4 + [block(2, 1024, 512), block(2, 1024)],
        [
            (block(HALF, 1024), of(f32, HALF, 1024)),
            (block(HALF, 1024), of(bf16, HALF, 1024)),
            (block(8, 64, HALF), of(bf16, 8, 64, HALF)),
            (block(8, 64, HALF), of(bf16, 8, 64, HALF)),
        ],
        [pltpu.VMEM((1024, HALF), bf16)],
        2 * 512 * 1024 * 1024,
        info,
        x,
        *keeps,
        *gots,
        w,
        gain,
    )


def up_kernel(info, x0_ref, x1_ref, *refs):
    act_ref, slope_ref, w_ref, sems = refs[5:]
    step = pl.program_id(0)
    near, far = piece_copies(info, refs[:5], w_ref, sems, 128, 1024, by_chip)

    @pl.when(step == 0)
    def _():
        start(near)
        start(far)
        wait(near)

    @pl.when(step == 1)
    def _():
        wait(far)

    for part, x_ref in enumerate((x0_ref, x1_ref)):
        rows = slice(part * HALF, part * HALF + HALF)
        for n in range(2):
            cols = slice(n * 512, n * 512 + 512)
            pre = dot(x_ref[...], w_ref[:, pl.ds(pl.multiple_of(step * 1024 + n * 512, 512), 512)], (1, 0))
            below = 0.5 * (1.0 + lax.erf(pre * 0.7071067811865476))
            act_ref[rows, cols] = (pre * below).astype(bf16)
            slope_ref[rows, cols] = (below + pre * (0.3989422804014327 * jnp.exp(-0.5 * pre * pre))).astype(bf16)


def up(info, x_own, x_sib, pieces):
    out = pl.BlockSpec((1024, 1024), lambda n, s: (0, lax.rem(s[3] + n, 2)))
    return call(
        up_kernel,
        "up",
        [block(HALF, 1024)] * 2 + [hbm()] * 5,
        [(out, of(bf16, 1024, 2048))] * 2,
        [pltpu.VMEM((1024, 2048), bf16), pltpu.SemaphoreType.DMA((16,))],
        4 * 512 * 1024 * 4096,
        info,
        x_own,
        x_sib,
        *pieces,
        grid=(2,),
    )


def down_kernel(info, act_ref, slope_ref, c0_ref, c1_ref, mid_ref, *refs):
    keep_ref, send_ref, gp_ref, w_ref, acc_ref, sems = refs[5:]
    step = pl.program_id(0)
    side = info[3]
    near, far = piece_copies(info, refs[:5], w_ref, sems, 256, 512, by_unit)
    mine = pl.ds(pl.multiple_of(side * 512, 512), 512)
    theirs = pl.ds(pl.multiple_of((1 - side) * 512, 512), 512)

    @pl.when(step == 0)
    def _():
        start(near)
        start(far)
        wait(near)
        wait(far)

    units = pl.ds(pl.multiple_of(step * 1024, 1024), 1024)
    for part, cot_ref in enumerate((c0_ref, c1_ref)):
        rows = slice(part * HALF, part * HALF + HALF)
        for n in range(2):
            here = pl.ds(pl.multiple_of(step * 1024 + n * 512, 512), 512)
            cols = slice(n * 512, n * 512 + 512)
            back = dot(cot_ref[:, mine], w_ref[here, :512], (1, 1)) + dot(cot_ref[:, theirs], w_ref[here, 512:], (1, 1))
            gp_ref[rows, cols] = (back * slope_ref[rows, cols].astype(f32)).astype(bf16)
        total = dot(act_ref[rows, :], w_ref[units, :], (1, 0))

        @pl.when(step == 0)
        def _():
            acc_ref[rows, :] = total

        @pl.when(step == 1)
        def _():
            done = total + acc_ref[rows, :]
            if part == 0:
                keep_ref[:, mine] = mid_ref[:, mine] + done[:, :512]
                keep_ref[:, theirs] = mid_ref[:, theirs] + done[:, 512:]
            else:
                send_ref[:, mine] = done[:, :512].astype(bf16)
                send_ref[:, theirs] = done[:, 512:].astype(bf16)


def down(info, act, slope, cot_own, cot_sib, mid, pieces):
    tile = pl.BlockSpec((1024, 1024), lambda n, s: (0, n))
    return call(
        down_kernel,
        "down",
        [tile, tile] + [block(HALF, 1024)] * 3 + [hbm()] * 5,
        [
            (block(HALF, 1024), of(f32, HALF, 1024)),
            (block(HALF, 1024), of(bf16, HALF, 1024)),
            (tile, of(bf16, 1024, 2048)),
        ],
        [pltpu.VMEM((2048, 1024), bf16), pltpu.VMEM((1024, 1024), f32), pltpu.SemaphoreType.DMA((16,))],
        4 * 512 * 1024 * 4096,
        info,
        act,
        slope,
        cot_own,
        cot_sib,
        mid,
        *pieces,
        grid=(2,),
    )


def normed_back_kernel(info, gp_ref, *refs):
    keep_ref, send_ref, w_ref, sems = refs[5:]
    near, far = piece_copies(info, refs[:5], w_ref, sems, 128, 1024, by_chip)
    start(near)
    start(far)
    wait(near)
    wait(far)
    mine = pl.ds(pl.multiple_of(info[3] * 1024, 1024), 1024)
    theirs = pl.ds(pl.multiple_of((1 - info[3]) * 1024, 1024), 1024)
    for part, out in ((1, send_ref), (0, keep_ref)):
        rows = slice(part * HALF, part * HALF + HALF)
        for n in range(2):
            dims = slice(n * 512, n * 512 + 512)
            total = dot(gp_ref[rows, mine], w_ref[dims, :1024], (1, 1)) + dot(gp_ref[rows, theirs], w_ref[dims, 1024:], (1, 1))
            out[:, dims] = total.astype(out.dtype)


def normed_back(info, gp, pieces):
    return call(
        normed_back_kernel,
        "normed_back",
        [block(1024, 2048)] + [hbm()] * 5,
        [(block(HALF, 1024), of(f32, HALF, 1024)), (block(HALF, 1024), of(bf16, HALF, 1024))],
        [pltpu.VMEM((1024, 2048), bf16), pltpu.SemaphoreType.DMA((16,))],
        2 * 512 * 1024 * 4096,
        info,
        gp,
        *pieces,
    )


def middle_back_kernel(info, e0_ref, e1_ref, cot_ref, mid_ref, g_ref, w_ref, gm_ref, gb_ref, keep, send):
    n, scale = centred(mid_ref[...])
    eg = (e0_ref[...] + e1_ref[...].astype(f32)) * g_ref[1:]
    lean = eg - jnp.mean(eg, axis=-1, keepdims=True) - n * jnp.mean(eg * n, axis=-1, keepdims=True)
    grad = cot_ref[...].astype(f32) + scale * lean
    gm_ref[...] = grad
    low = grad.astype(bf16)
    gb_ref[...] = low
    for out, at in ((keep, info[3]), (send, 1 - info[3])):
        rows = pl.ds(pl.multiple_of(at * HALF, HALF), HALF)
        out[...] = (dot(low[:, :512], w_ref[0, rows, :], (1, 1)) + dot(low[:, 512:], w_ref[1, rows, :], (1, 1))).astype(bf16)


def middle_back(info, e_keep, e_got, cot, mid, gain, w):
    return call(
        middle_back_kernel,
        "middle_back",
        [block(HALF, 1024)] * 4 + [block(2, 1024), block(2, 1024, 512)],
        [
            (block(HALF, 1024), of(f32, HALF, 1024)),
            (block(HALF, 1024), of(bf16, HALF, 1024)),
            (block(HALF, 512), of(bf16, HALF, 512)),
            (block(HALF, 512), of(bf16, HALF, 512)),
        ],
        [],
        2 * 512 * 1024 * 1024,
        info,
        e_keep,
        e_got,
        cot,
        mid,
        gain,
        w,
    )


def down_grad_kernel(info, c0_ref, c1_ref, act_ref, far, across, beside, own, t_ref):
    g = pl.program_id(0)

    @pl.when(g == 0)
    def _():
        t_ref[:, :HALF] = c0_ref[...].T
        t_ref[:, HALF:] = c1_ref[...].T

    x = lax.rem(info[1] + 1 - lax.rem(g, 2), 2)
    side = lax.rem(info[3] + 1 - g // 2, 2)
    rows = pl.ds(pl.multiple_of(side * 512, 512), 512)
    for half in range(2):
        units = pl.ds(pl.multiple_of(half * 1024 + x * 512, 512), 512)
        total = dot(t_ref[rows, :], act_ref[:, units], (1, 0)).astype(bf16)
        for j in range(2):
            dz = lax.rem(half * 2 + j - info[0] + LINE, LINE)
            for at, ref in enumerate((far, across, beside, own)):

                @pl.when(g == at)
                def _():
                    ref[dz] = total[:, j * 256 : j * 256 + 256]


def down_grad(info, cot_own, cot_sib, act):
    return call(
        down_grad_kernel,
        "down_grad",
        [block(HALF, 1024), block(HALF, 1024), block(1024, 2048)],
        [(block(LINE, 512, 256), of(bf16, LINE, 512, 256))] * 4,
        [pltpu.VMEM((1024, 1024), bf16)],
        2 * 1024 * 1024 * 2048,
        info,
        cot_own,
        cot_sib,
        act,
        grid=(4,),
    )


def stay(g, first):
    return lax.max(0, lax.min(g - first, 1))


def up_grad_kernel(info, n0_ref, n1_ref, gp_ref, far, across, beside, own, t_ref):
    g = pl.program_id(0)

    @pl.when(g == 0)
    def _():
        for dx in range(2):
            for dz in range(LINE):
                chip = lax.rem(info[0] + dz, LINE) * 2 + lax.rem(info[1] + dx, 2)
                cols = pl.ds(pl.multiple_of(chip * 128, 128), 128)
                rows = slice((dx * LINE + dz) * 128, (dx * LINE + dz) * 128 + 128)
                t_ref[rows, :HALF] = n0_ref[:, cols].T
                t_ref[rows, HALF:] = n1_ref[:, cols].T

    total = dot(t_ref[...], gp_ref[...], (1, 0)).astype(bf16).reshape(8, 128, 512)

    @pl.when(g < 2)
    def _():
        across[...] = total[:4]
        far[...] = total[4:]

    @pl.when(g >= 2)
    def _():
        own[...] = total[:4]
        beside[...] = total[4:]


def up_grad(info, nm_own, nm_sib, gp):
    right = pl.BlockSpec((1024, 512), lambda g, s: (0, lax.rem(s[3] + 1 - g // 2, 2) * 2 + lax.rem(g, 2)))
    return call(
        up_grad_kernel,
        "up_grad",
        [block(HALF, 1024), block(HALF, 1024), right],
        [
            (pl.BlockSpec((LINE, 128, 512), lambda g, s, f=f: (0, 0, stay(g, f))), of(bf16, LINE, 128, 1024))
            for f in (0, 0, 2, 2)
        ],
        [pltpu.VMEM((1024, 1024), bf16)],
        2 * 1024 * 512 * 4096,
        info,
        nm_own,
        nm_sib,
        gp,
        grid=(4,),
    )


def out_grad_kernel(info, l0_ref, r0_ref, l1_ref, r1_ref, keep_ref, send_ref):
    for out, at in ((keep_ref, info[3]), (send_ref, 1 - info[3])):
        cols = pl.ds(pl.multiple_of(at * 512, 512), 512)
        total = dot(l0_ref[...], r0_ref[:, cols], (1, 0)) + dot(l1_ref[...], r1_ref[:, cols], (1, 0))
        out[...] = total.astype(bf16).reshape(8, 64, 512)


def out_grad(info, att_t, gb, att_t_sib, gb_sib):
    return call(
        out_grad_kernel,
        "out_grad",
        [block(512, HALF), block(HALF, 1024)] * 2,
        [(block(8, 64, 512), of(bf16, 8, 64, 512))] * 2,
        [],
        2 * 512 * 1024 * 1024,
        info,
        att_t.reshape(512, HALF),
        gb,
        att_t_sib.reshape(512, HALF),
        gb_sib,
    )


def input_back_kernel(info, d0_ref, d1_ref, *refs):
    keep_ref, send_ref, w_ref, sems = refs[4:]
    copies = qkv_copies(info, refs[:4], w_ref, sems, 0, 1536)
    start(copies)
    wait(copies)
    for part, out in ((1, send_ref), (0, keep_ref)):
        at = info[3] if part == 0 else 1 - info[3]
        slots = pl.ds(pl.multiple_of(at * HALF, HALF), HALF)
        for n in range(2):
            dims = slice(n * 512, n * 512 + 512)
            total = dot(d0_ref[slots, :], w_ref[dims, :768], (1, 1)) + dot(d1_ref[slots, :], w_ref[dims, 768:], (1, 1))
            out[:, dims] = total.astype(out.dtype)


def input_back(info, d0, d1, pieces):
    return call(
        input_back_kernel,
        "input_back",
        [block(1024, 768)] * 2 + [hbm()] * 4,
        [(block(HALF, 1024), of(f32, HALF, 1024)), (block(HALF, 1024), of(bf16, HALF, 1024))],
        [pltpu.VMEM((1024, 1536), bf16), pltpu.SemaphoreType.DMA((16,))],
        2 * 1024 * 1024 * 1536,
        info,
        d0,
        d1,
        *pieces,
    )


def qkv_grad_kernel(info, l0_ref, r0_ref, l1_ref, r1_ref, *refs):
    beside, own = refs[-2:]
    total = dot(l0_ref[...], r0_ref[...], (1, 0)) + dot(l1_ref[...], r1_ref[...], (1, 0))
    total = total.astype(bf16).reshape(8, 64, 768)
    own[:, :, :768] = total[:4]
    beside[:, :, :768] = total[4:]
    if len(refs) == 4:
        both = (refs[0][...].astype(f32) + refs[1][...].astype(f32)).astype(bf16)
        own[:, :, 768:] = both[:4]
        beside[:, :, 768:] = both[4:]


def qkv_grad(info, nin_t, dproj, nin_t_sib, dproj_sib, more=()):
    width = 768 + 512 * bool(more)
    return call(
        qkv_grad_kernel,
        "qkv_grad",
        [block(512, 1024), block(1024, 768)] * 2 + [block(8, 64, 512)] * len(more),
        [(block(4, 64, width), of(bf16, 4, 64, width))] * 2,
        [],
        2 * 2048 * 512 * 768,
        info,
        nin_t.reshape(512, 1024),
        dproj,
        nin_t_sib.reshape(512, 1024),
        dproj_sib,
        *more,
    )


def input_norm_kernel(info, xo_ref, xt_ref, g_ref, own_ref, oth_ref, t_ref):
    side = info[3]
    for part, x_ref in ((0, xo_ref), (1, xt_ref)):
        at = side if part == 0 else 1 - side
        normed = (centred(x_ref[...].astype(f32))[0] * g_ref[:1]).astype(bf16)
        t_ref[:, pl.ds(pl.multiple_of(at * HALF, HALF), HALF)] = normed.T
    put_parities(info, t_ref, own_ref, oth_ref)


def input_norm(info, x_own, x_other, gains):
    return call(
        input_norm_kernel,
        "input_norm",
        [block(HALF, 1024), block(HALF, 1024), block(2, 1024)],
        [(block(8, 64, 1024), of(bf16, 8, 64, 1024))] * 2,
        [pltpu.VMEM((1024, 1024), bf16)],
        20 << 20,
        info,
        x_own,
        x_other,
        gains,
    )


def heads_kernel(info, w_ref, got_ref, gain_ref, out_ref):
    side = info[3] == 0
    first, middle, last = w_ref[:, :512], got_ref[:, :512], w_ref[:, 1024:]
    q = jnp.where(side, first, middle)
    k = jnp.where(side, last, first)
    v = jnp.where(side, middle, last)
    for i in range(2):
        for j, part in enumerate((q, k, v)):
            out_ref[:, i * 768 + j * 256 : i * 768 + j * 256 + 256] = part[:, i * 256 : i * 256 + 256]
    lane = lax.broadcasted_iota(jnp.int32, (w_ref.shape[0], 128), 1)
    mine = jnp.broadcast_to(gain_ref[...].astype(f32), lane.shape)
    theirs = jnp.broadcast_to(got_ref[:, 512:513].astype(f32), lane.shape)
    out_ref[:, 1536:] = jnp.where((lane == 0) == side, mine, theirs).astype(bf16)


def heads_of(info, w, got, gains):
    return call(
        heads_kernel,
        "heads",
        [block(64, 1536), block(64, 640), block(64, 1)],
        [(block(64, 1664), of(bf16, 64, 1664))],
        [],
        1 << 16,
        info,
        w,
        got,
        gains,
    )[0]


def by_core_kernel(info, up_ref, own_ref, oth_ref):
    for ref, core in ((own_ref, info[2]), (oth_ref, 1 - info[2])):
        for i, to in enumerate((0, 2, 1, 3)):
            ref[:, to * 256 : to * 256 + 256] = up_ref[:, pl.ds(pl.multiple_of(i * 512 + core * 256, 256), 256)]


def by_core(info, w_up):
    return call(
        by_core_kernel,
        "by_core",
        [block(64, 2048)],
        [(block(64, 1024), of(bf16, 64, 1024))] * 2,
        [],
        1 << 16,
        info,
        w_up,
    )


def both_rows_kernel(info, own_ref, got_ref, out_ref):
    out_ref[pl.ds(pl.multiple_of(info[2] * 64, 64), 64), :] = own_ref[...]
    out_ref[pl.ds(pl.multiple_of((1 - info[2]) * 64, 64), 64), :] = got_ref[...]


def both_rows(info, own, got):
    return call(
        both_rows_kernel,
        "both_rows",
        [block(64, 1024)] * 2,
        [(block(128, 1024), of(bf16, 128, 1024))],
        [],
        1 << 16,
        info,
        own,
        got,
    )[0]


def added_kernel(info, a_ref, b_ref, out_ref):
    out_ref[...] = (a_ref[...].astype(f32) + b_ref[...].astype(f32)).astype(bf16)


def added(info, a, b, name="added"):
    steps = 2
    spec = pl.BlockSpec((a.shape[0] // steps, *a.shape[1:]), lambda i, s: (i,) + (0,) * (a.ndim - 1))
    return call(added_kernel, name, [spec, spec], [(spec, of(bf16, *a.shape))], [], 0, info, a, b, grid=(steps,))[0]


def line_parts_kernel(info, a_ref, b_ref, c_ref, *outs):
    for k, out in enumerate(outs):
        out[...] = (a_ref[k].astype(f32) + b_ref[k].astype(f32) + c_ref[k].astype(f32)).astype(bf16)


def line_parts(info, own, from_x, from_y, name):
    spec, out = block(*own.shape), block(*own.shape[1:])
    return call(
        line_parts_kernel, name, [spec] * 3, [(out, of(bf16, *own.shape[1:]))] * LINE, [], 0, info, own, from_x, from_y
    )


def qkv_parts_kernel(info, a_ref, ax_ref, b_ref, bx_ref, *outs):
    for k, out in enumerate(outs):
        out[:, :1280] = (a_ref[k].astype(f32) + ax_ref[k].astype(f32)).astype(bf16)
        out[:, 1280:] = (b_ref[k].astype(f32) + bx_ref[k].astype(f32)).astype(bf16)


def qkv_parts(info, a, a_x, b, b_x):
    return call(
        qkv_parts_kernel,
        "qkv_parts",
        [block(4, 64, 1280)] * 2 + [block(4, 64, 768)] * 2,
        [(block(64, 2048), of(bf16, 64, 2048))] * LINE,
        [],
        0,
        info,
        a,
        a_x,
        b,
        b_x,
    )


def stack_kernel(info, *refs):
    for k in range(LINE):
        refs[LINE][k] = refs[k][...]


def stacked(info, parts, name):
    shape = parts[0].shape
    return call(
        stack_kernel, name, [block(*shape)] * LINE, [(block(LINE, *shape), of(bf16, LINE, *shape))], [], 0, info, *parts
    )[0]


def touch_kernel(info, a_ref, out_ref):
    out_ref[...] = a_ref[...]


def touch(info, a):
    return call(touch_kernel, "touch", [block(*a.shape)], [(block(*a.shape), of(a.dtype, *a.shape))], [], 0, info, a)[0]


def summed(refs, *at):
    total = refs[0][at].astype(f32)
    for ref in refs[1:]:
        total = total + ref[at].astype(f32)
    return total


def down_sum_kernel(info, *refs):
    refs[4][...] = summed(refs[:4]).T


def down_sum(info, parts):
    return call(
        down_sum_kernel,
        "down_sum",
        [block(512, 256)] * 4,
        [(block(256, 512), of(f32, 256, 512))],
        [],
        0,
        info,
        *parts,
    )[0]


def up_sum_kernel(info, *refs):
    for out, core in ((refs[4], info[2]), (refs[5], 1 - info[2])):
        out[...] = summed(refs[:4], pl.ds(pl.multiple_of(core * 64, 64), 64))


def up_sum(info, parts):
    return call(
        up_sum_kernel,
        "up_sum",
        [block(128, 1024)] * 4,
        [(block(64, 1024), of(f32, 64, 1024))] * 2,
        [],
        0,
        info,
        *parts,
    )


def up_whole_kernel(info, mine_ref, got_ref, w_ref, in_ref, out_ref, own_ref, send_ref):
    for ref, core in ((mine_ref, info[2]), (got_ref, 1 - info[2])):
        for i, place in enumerate((0, 2, 1, 3)):
            cols = pl.ds(pl.multiple_of(i * 512 + core * 256, 256), 256)
            out_ref[:, cols] = ref[:, place * 256 : place * 256 + 256]
    total = jnp.sum(w_ref[...].astype(f32) * out_ref[...], axis=1, keepdims=True)
    mid = jnp.broadcast_to(total, in_ref.shape)
    first = info[3] == 0
    own_ref[...] = jnp.where(first, in_ref[...], mid)
    send_ref[...] = jnp.where(first, mid, in_ref[...])


def up_whole(info, mine, got, w, in_sums):
    return call(
        up_whole_kernel,
        "up_whole",
        [block(64, 1024)] * 2 + [block(64, 2048), block(64, 128)],
        [(block(64, 2048), of(f32, 64, 2048))] + [(block(64, 128), of(f32, 64, 128))] * 2,
        [],
        0,
        info,
        mine,
        got,
        w,
        in_sums,
    )


def qkv_sum_kernel(info, *refs):
    heads_ref, keep_ref, send_ref, sum_ref, out_ref = refs[4:]
    total = summed(refs[:4])
    out_ref[...] = total[:, 768:1280]
    groups = (total[:, :768], total[:, 1280:])
    q, k, v = (jnp.concatenate([g[:, j : j + 256] for g in groups], axis=1) for j in (0, 256, 512))
    weights = heads_ref[...].astype(f32)
    by_row = jnp.sum(weights[:, :768] * groups[0], axis=1, keepdims=True) + jnp.sum(
        weights[:, 768:1536] * groups[1], axis=1, keepdims=True
    )
    sum_ref[...] = jnp.broadcast_to(by_row, sum_ref.shape)
    first = info[3] == 0
    keep_ref[:, :512] = jnp.where(first, q, k)
    keep_ref[:, 512:] = jnp.where(first, k, v)
    send_ref[...] = jnp.where(first, v, q)


def qkv_sum(info, parts, heads):
    return call(
        qkv_sum_kernel,
        "qkv_sum",
        [block(64, 2048)] * 4 + [block(64, 1664)],
        [(block(64, n), of(f32, 64, n)) for n in (1024, 512, 128, 512)],
        [],
        0,
        info,
        *parts,
        heads,
    )


def qkv_whole_kernel(info, keep_ref, got_ref, own_ref, other_ref, gain_ref, out_ref, gg_ref):
    out_ref[:, :512] = keep_ref[:, :512]
    out_ref[:, 512:1024] = got_ref[...]
    out_ref[:, 1024:] = keep_ref[:, 512:]
    gg_ref[...] = (own_ref[:, :1] + other_ref[:, :1]) / gain_ref[...].astype(f32)


def qkv_whole(info, keep, got, own_sums, other_sums, gains):
    return call(
        qkv_whole_kernel,
        "qkv_whole",
        [block(64, 1024), block(64, 512), block(64, 128), block(64, 128), block(64, 1)],
        [(block(64, 1536), of(f32, 64, 1536)), (block(64, 1), of(f32, 64, 1))],
        [],
        0,
        info,
        keep,
        got,
        own_sums,
        other_sums,
        gains,
    )


def input_grad_kernel(info, x_ref, e0_ref, e1_ref, gm_ref, g_ref, out_ref):
    n, scale = centred(x_ref[...].astype(f32))
    eg = (e0_ref[...] + e1_ref[...].astype(f32)) * g_ref[:1]
    lean = eg - jnp.mean(eg, axis=-1, keepdims=True) - n * jnp.mean(eg * n, axis=-1, keepdims=True)
    out_ref[...] = gm_ref[...] + scale * lean


def input_grad(info, x, e_own, e_got, gm, gains):
    rows = pl.BlockSpec((256, 1024), lambda i, s: (i, 0))
    return call(
        input_grad_kernel,
        "input_grad",
        [rows] * 4 + [block(2, 1024)],
        [(rows, of(f32, HALF, 1024))],
        [],
        0,
        info,
        x,
        e_own,
        e_got,
        gm,
        gains,
        grid=(2,),
    )[0]


def slot_bias(phones, prompts, targets):
    places = jnp.arange(HALF, dtype=jnp.int32)
    count = phones.shape[0]
    segs, is_phone = [], None
    for lengths in (phones + prompts, targets):
        ends = jnp.stack([sum(lengths[i] for i in range(upto + 1)) for upto in range(count)])
        seg = jnp.sum((places[:, None] >= ends[None, :]).astype(jnp.int32), axis=1)
        segs.append(seg)
        if is_phone is None:
            onehot = seg[:, None] == jnp.arange(count, dtype=jnp.int32)[None, :]
            phone_ends = jnp.sum(jnp.where(onehot, (ends - lengths + phones)[None, :], 0), axis=1)
            is_phone = places < phone_ends
    seg = jnp.concatenate(segs)
    phone = jnp.concatenate([is_phone, jnp.zeros((HALF,), dtype=bool)])
    order = jnp.arange(2 * HALF, dtype=jnp.int32)
    allowed = (seg[:, None] == seg[None, :]) & (
        phone[:, None] | (jnp.logical_not(phone)[None, :] & (order[:, None] <= order[None, :]))
    )
    allowed_t = (seg[:, None] == seg[None, :]) & (
        phone[None, :] | (jnp.logical_not(phone)[:, None] & (order[None, :] <= order[:, None]))
    )
    bias = jnp.where(allowed, 0.0, NEG).astype(f32)
    return bias, jnp.where(allowed_t, 0.0, NEG).astype(f32)


def line_shards(tokens, cotangent, gains, w_qkv, w_out, w_up, w_down, phone_len, prompt_len, target_len):
    r = lax.axis_index("rows")
    side = lax.axis_index("pair")
    core = r % 2
    info = jnp.stack([r // 4, r // 2 % 2, core, side]).astype(jnp.int32)
    x_own = tokens[0]
    cot = cotangent[0]

    out_all = lax.all_gather(w_out, ("pair", "rows"), axis=0, tiled=True).reshape(2, 1024, 512)
    crossed = swap_y(jnp.concatenate([w_qkv[:, 512:1024], jnp.pad(gains, ((0, 0), (0, 127)))], axis=1))
    x_other = swap_y(x_own)
    heads = heads_of(info, w_qkv, crossed, gains)
    pieces = along_line(heads)
    up_keep, up_send = by_core(info, after(w_up, heads))
    up_got = swap_c(up_send)
    bias_t, bias = slot_bias(after(phone_len, up_keep)[0], prompt_len[0], target_len[0])
    up_piece = both_rows(info, up_keep, up_got)
    pieces, x_other, bias, bias_t, up_piece = barrier(pieces, x_other, bias, bias_t, up_piece)
    qkv_line = stacked(info, pieces, "qkv_stack")
    beside = swap_x(qkv_line)
    qkv_line_sib = swap_c(qkv_line)
    up_line = along_line(after(up_piece, qkv_line))
    beside_sib = swap_c(beside)
    heads = touch(info, after(heads, up_line))
    up_line = stacked(info, after(up_line, heads, beside_sib, qkv_line_sib), "up_stack")
    up_x, up_y = swap_x(up_line), swap_y(up_line)

    qkv_pieces = (qkv_line, beside, after(qkv_line_sib, up_line), after(beside_sib, up_line))
    projected, gain_all = project(info, x_own, x_other, qkv_pieces)
    down_line = along_line(after(w_down, projected))
    keep0, send0, lse0 = attend(info, projected, bias, 0)
    got0 = swap_y(send0)
    up_x, up_y = after((up_x, up_y), keep0)
    up_far = swap_x(up_y)
    keep1, send1, lse1 = attend(info, projected, after(bias, keep0), 1)
    got1 = swap_y(send1)
    down_line = stacked(info, after(down_line, keep1), "down_stack")
    down_x = swap_x(down_line)
    cot_sib = swap_c(after(cot, keep1))
    nin_t, nin_t_oth = input_norm(info, after(x_own, down_line), x_other, gain_all)
    down_y = swap_y(after(down_line, got0))
    gain_all = touch(info, after(gain_all, nin_t, up_far, got0, out_all))
    got1 = after(got1, gain_all)
    mid, nm_own, att_t, att_t_oth = attention_out(info, x_own, (keep0, keep1), (got0, got1), out_all, gain_all)
    nm_sib = swap_c(nm_own)
    nin_t_sib = swap_c(after(nin_t_oth, nm_own))
    att_t_sib = swap_c(att_t_oth)
    up_pieces = (up_line, up_x, up_y, up_far, up_far)
    down_far = [swap_y(down_x[:2]), swap_x(down_y[2:])]
    gain_all = touch(info, after(gain_all, nm_own, down_x, down_y))
    nm_sib = after(nm_sib, gain_all)
    act, slope = up(info, nm_own, nm_sib, up_pieces)
    down_pieces = (down_line, down_x, down_y, *down_far)
    mixed_keep, mixed_send, gp = down(info, act, slope, cot, cot_sib, mid, down_pieces)

    gp, nin_t_sib, att_t_sib = barrier(gp, nin_t_sib, att_t_sib)
    mixed_got = swap_c(mixed_send)
    e_keep, e_send = normed_back(info, gp, up_pieces)
    e_got = swap_c(e_send)
    far, down_across, down_beside, down_own = down_grad(info, cot, cot_sib, after(act, e_keep))
    down_far, down_x = swap_x(far), swap_x(down_beside)
    gm, gb, ga_keep, ga_send = middle_back(info, after(e_keep, far), after(e_got, far), cot, mid, gain_all, out_all)
    ga_got = swap_y(ga_send)
    gb_sib = swap_c(gb)
    far, up_across, up_beside, up_own = up_grad(info, nm_own, nm_sib, after(gp, gb))
    down_across = added(info, after(down_across, far), after(down_far, far))
    down_y = swap_y(down_across)
    up_far = swap_x(far)
    gb_sib = after(gb_sib, down_across)
    out_keep, out_send = out_grad(info, att_t, after(gb, down_across), att_t_sib, gb_sib)
    out_got = swap_y(out_send)
    ga_got = after(ga_got, out_keep)
    dproj0 = attend_back(info, projected, after(bias_t, out_keep), lse0, ga_keep, ga_got, 0)
    dproj0_sib = swap_c(dproj0)
    down_x, down_y = after((down_x, down_y), dproj0)
    down_parts = line_parts(info, down_own, down_x, down_y, "down_parts")
    down_shift = [shift_z(down_parts[k], k) for k in range(1, LINE)]
    up_x = swap_x(up_beside)
    gain_all = touch(info, after(gain_all, out_got, down_parts))
    dproj0_sib = after(dproj0_sib, gain_all)
    first_beside, first_own = qkv_grad(info, nin_t, after(dproj0, gain_all), nin_t_sib, dproj0_sib, (out_keep, out_got))
    first_x = swap_x(first_beside)
    up_across = added(info, up_across, after(up_far, first_own))
    up_y = swap_y(up_across)
    dproj1 = attend_back(info, projected, after(bias_t, first_own, up_across), lse1, ga_keep, ga_got, 1)
    dproj1_sib = swap_c(dproj1)
    g_down = down_sum(info, (after(down_parts[0], dproj1), *after(down_shift, dproj1)))
    up_x, up_y = after((up_x, up_y), g_down)
    up_parts = line_parts(info, up_own, up_x, up_y, "up_parts")
    up_shift = [shift_z(up_parts[k], k) for k in range(1, LINE)]
    dproj1_sib = after(dproj1_sib, up_parts)
    second_beside, second_own = qkv_grad(info, nin_t, after(dproj1, up_parts), nin_t_sib, dproj1_sib)
    second_x = swap_x(second_beside)
    e_own, e_send = input_back(info, after(dproj0, second_own), dproj1, qkv_pieces)
    e_got = swap_y(e_send)
    first_x, second_x = after((first_x, second_x), e_own)
    heads_parts = qkv_parts(info, first_own, first_x, second_own, second_x)
    qkv_shift = [shift_z(heads_parts[k], k) for k in range(1, LINE)]
    up_mine, up_send = up_sum(info, (after(up_parts[0], heads_parts), *up_shift))
    up_got = swap_c(up_send)
    mixed = added(info, mixed_keep, after(mixed_got, up_mine), "mixed")
    grad_tokens = input_grad(info, after(x_own, mixed), e_own, after(e_got, mixed), gm, gain_all)
    keep, send, in_sums, g_out = qkv_sum(info, (after(heads_parts[0], grad_tokens), *after(qkv_shift, grad_tokens)), heads)
    got = swap_y(send)
    g_up, gain_own, gain_send = up_whole(info, up_mine, after(up_got, keep), w_up, in_sums)
    gain_got = swap_y(gain_send)
    g_qkv, grad_gains = qkv_whole(info, keep, after(got, g_up), gain_own, gain_got, gains)
    return (mixed[None], grad_tokens[None], grad_gains, g_qkv, g_out, g_up, g_down)


def solution(mesh):
    lined = mesh.shape["rows"] == 4 * LINE and mesh.shape["pair"] == 2
    return jax.shard_map(
        line_shards if lined else shards,
        mesh=mesh,
        in_specs=(
            P("rows", "pair", None),
            P("rows", "pair", None),
            P("rows", "pair"),
            P("rows", "pair"),
            P("rows", "pair"),
            P("rows", "pair"),
            P("rows", "pair"),
            P("rows", None),
            P("rows", None),
            P("rows", None),
        ),
        out_specs=(
            P("rows", "pair", None),
            P("rows", "pair", None),
            P("rows", "pair"),
            P("rows", "pair"),
            P("rows", "pair"),
            P("rows", "pair"),
            P("rows", "pair"),
        ),
        check_vma=False,
    )
```

```python
import functools

import jax
import jax.numpy as jnp
from jax import lax
from jax.experimental import pallas as pl
from jax.experimental.pallas import tpu as pltpu
from jax.sharding import PartitionSpec as P

HEADS = 16
HEAD_DIM = 64


epsilon = 1e-05


def passed_along(value, axis, steps):
    count = lax.axis_size(axis)
    leading, last = (max(0, -steps), min(count, count - steps))
    return lax.ppermute(value, axis, [(source, source + steps) for source in range(leading, last)])


def slot_layout(side_index, phones, prompts, targets, slot_count):
    lengths = jnp.where(side_index == 0, phones + prompts, targets)
    count = lengths.shape[0]
    seg_ends = jnp.stack([sum(lengths[i] for i in range(upto + 1)) for upto in range(count)])
    starts = seg_ends - lengths
    places = jnp.arange(slot_count, dtype=jnp.int32)
    segment = jnp.sum((places[:, None] >= seg_ends[None, :]).astype(jnp.int32), axis=1)
    onehot = (segment[:, None] == jnp.arange(lengths.shape[0], dtype=jnp.int32)[None, :]).astype(
        jnp.int32
    )
    within = places - jnp.sum(onehot * starts[None, :], axis=1)
    phone_here = jnp.sum(onehot * phones[None, :], axis=1)
    is_phone = jnp.logical_and(side_index == 0, within < phone_here)
    ordering = places + side_index * slot_count
    return (segment, is_phone, ordering)


def permitted(query_side, key_side):
    query_seg, query_phone, query_order = query_side
    key_seg, key_phone, key_order = key_side
    same_seg = query_seg[:, None] == key_seg[None, :]
    earlier = key_order[None, :] <= query_order[:, None]
    return same_seg & (key_phone[None, :] | jnp.logical_not(query_phone)[:, None] & earlier)


def normalize(values, gain_row):
    centred = values - jnp.mean(values, axis=-1, keepdims=True)
    spread = jnp.mean(centred * centred, axis=-1, keepdims=True)
    return centred * lax.rsqrt(spread + epsilon) * gain_row


def exact_gelu(values):
    return jax.nn.gelu(values, approximate=False)


def softmax_rows(query_piece, key_piece, allowed):
    scores = jnp.einsum(
        "qhd,khd->hqk", query_piece, key_piece, preferred_element_type=jnp.float32
    ) * HEAD_DIM ** (-0.5)
    scores = jnp.where(allowed[None], scores, -1e30)
    row_max = jnp.max(scores, axis=-1, keepdims=True)
    exponents = jnp.exp(scores - row_max)
    return exponents / jnp.sum(exponents, axis=-1, keepdims=True)


def shards(tokens, cotangent, gains, w_qkv, w_out, w_up, w_down, phone_len, prompt_len, target_len):
    slot_count = tokens.shape[1]
    model_width = tokens.shape[2]
    inputs = tokens[0].astype(jnp.float32)
    side_index = lax.axis_index("pair")
    paired = (
        lax.all_gather(gains, "pair", axis=1, tiled=True),
        lax.all_gather(w_qkv, "pair", axis=1, tiled=True),
        lax.all_gather(w_out, "pair", axis=1, tiled=True),
        lax.all_gather(w_up, "pair", axis=1, tiled=True),
        lax.all_gather(w_down, "pair", axis=1, tiled=True),
    )
    gain_all, qkv_all, out_all, up_all, down_all = (
        lax.all_gather(paired[0], "rows", axis=0, tiled=True),
        lax.all_gather(paired[1], "rows", axis=0, tiled=True),
        lax.all_gather(paired[2], "rows", axis=0, tiled=True),
        lax.all_gather(paired[3], "rows", axis=0, tiled=True),
        lax.all_gather(paired[4], "rows", axis=0, tiled=True),
    )
    gain_first = gain_all[:, 0].astype(jnp.float32)
    gain_second = gain_all[:, 1].astype(jnp.float32)
    phones = phone_len[0]
    prompts = prompt_len[0]
    targets = target_len[0]
    own_layout = slot_layout(side_index, phones, prompts, targets, slot_count)
    far_layout = slot_layout(0, phones, prompts, targets, slot_count)
    key_layout = tuple(
        (
            jnp.concatenate([far_part, own_part])
            for far_part, own_part in zip(far_layout, own_layout)
        )
    )
    far_live = jnp.concatenate(
        [jnp.full((slot_count,), side_index == 1), jnp.ones((slot_count,), dtype=bool)]
    )
    normed_in, norm_first_back = jax.vjp(normalize, inputs, gain_first)
    normed_low = normed_in.astype(jnp.bfloat16)
    projected = jnp.dot(normed_low, qkv_all, preferred_element_type=jnp.float32).astype(
        jnp.bfloat16
    )
    queries = projected[:, :model_width]
    near_pairs = projected[:, model_width:]
    far_pairs = passed_along(near_pairs, "pair", 1)
    key_value = jnp.concatenate([far_pairs, near_pairs], axis=0)
    block_rows = min(512, slot_count)
    per_group = min(4, HEADS)
    group_width = per_group * HEAD_DIM
    groups = HEADS // per_group
    steps_total = slot_count // block_rows * groups
    key_count = 2 * slot_count

    def piece_of(item_index):
        row_start = item_index // groups * block_rows
        col_start = item_index % groups * group_width
        query_piece = lax.dynamic_slice(
            queries, (row_start, col_start), (block_rows, group_width)
        ).reshape(block_rows, per_group, HEAD_DIM)
        key_piece = lax.dynamic_slice(key_value, (0, col_start), (key_count, group_width)).reshape(
            key_count, per_group, HEAD_DIM
        )
        value_piece = lax.dynamic_slice(
            key_value, (0, model_width + col_start), (key_count, group_width)
        ).reshape(key_count, per_group, HEAD_DIM)
        query_layout = tuple((member for member in own_layout))
        allowed = permitted(query_layout, key_layout) & far_live[None, :]
        attn_probs = softmax_rows(query_piece, key_piece, allowed)
        return (row_start, col_start, query_piece, key_piece, value_piece, attn_probs)

    def forward_step(item_index, attended):
        row_start, col_start, query_piece, key_piece, value_piece, attn_probs = piece_of(item_index)
        head_mix = jnp.einsum(
            "hqk,khd->qhd",
            attn_probs.astype(jnp.bfloat16),
            value_piece,
            preferred_element_type=jnp.float32,
        )
        return lax.dynamic_update_slice(
            attended, head_mix.reshape(block_rows, group_width), (row_start, col_start)
        )

    attended = lax.fori_loop(
        0, steps_total, forward_step, jnp.zeros((slot_count, model_width), jnp.float32)
    )
    attended_low = attended.astype(jnp.bfloat16)
    middle = inputs + jnp.dot(attended_low, out_all, preferred_element_type=jnp.float32)
    normed_mid, norm_second_back = jax.vjp(normalize, middle, gain_second)
    normed_mid_low = normed_mid.astype(jnp.bfloat16)
    pre_act = jnp.dot(normed_mid_low, up_all, preferred_element_type=jnp.float32)
    activated, gelu_back = jax.vjp(exact_gelu, pre_act)
    activated_low = activated.astype(jnp.bfloat16)
    result = middle + jnp.dot(activated_low, down_all, preferred_element_type=jnp.float32)
    mixed_out = result.astype(jnp.bfloat16)[None]
    qkv_back, out_back, up_back, down_back = (qkv_all, out_all, up_all, down_all)
    grad_result = cotangent[0]
    grad_down = jnp.dot(activated_low.T, grad_result, preferred_element_type=jnp.float32)
    grad_act = jnp.dot(grad_result, down_back.T, preferred_element_type=jnp.float32)
    grad_pre = gelu_back(grad_act)[0].astype(jnp.bfloat16)
    grad_up = jnp.dot(normed_mid_low.T, grad_pre, preferred_element_type=jnp.float32)
    grad_normed_mid = jnp.dot(grad_pre, up_back.T, preferred_element_type=jnp.float32)
    grad_middle_norm, grad_gain_second = norm_second_back(grad_normed_mid)
    grad_middle = grad_result.astype(jnp.float32) + grad_middle_norm
    grad_branch = grad_middle.astype(jnp.bfloat16)
    grad_out = jnp.dot(attended_low.T, grad_branch, preferred_element_type=jnp.float32)
    grad_attended = jnp.dot(grad_branch, out_back.T, preferred_element_type=jnp.float32).astype(
        jnp.bfloat16
    )

    def backward_step(item_index, running):
        grad_queries, grad_pairs = running
        row_start, col_start, query_piece, key_piece, value_piece, attn_probs = piece_of(item_index)
        grad_piece = lax.dynamic_slice(
            grad_attended, (row_start, col_start), (block_rows, group_width)
        ).reshape(block_rows, per_group, HEAD_DIM)
        grad_probs = jnp.einsum(
            "qhd,khd->hqk", grad_piece, value_piece, preferred_element_type=jnp.float32
        )
        centre = jnp.sum(grad_probs * attn_probs, axis=-1, keepdims=True)
        grad_scores = (attn_probs * (grad_probs - centre)).astype(jnp.bfloat16)
        score_scale = HEAD_DIM ** (-0.5)
        query_grad = (
            jnp.einsum("hqk,khd->qhd", grad_scores, key_piece, preferred_element_type=jnp.float32)
            * score_scale
        )
        key_grad = (
            jnp.einsum("hqk,qhd->khd", grad_scores, query_piece, preferred_element_type=jnp.float32)
            * score_scale
        )
        value_grad = jnp.einsum(
            "hqk,qhd->khd",
            attn_probs.astype(jnp.bfloat16),
            grad_piece,
            preferred_element_type=jnp.float32,
        )
        grad_queries = lax.dynamic_update_slice(
            grad_queries, query_grad.reshape(block_rows, group_width), (row_start, col_start)
        )
        key_old = lax.dynamic_slice(grad_pairs, (0, col_start), (key_count, group_width))
        grad_pairs = lax.dynamic_update_slice(
            grad_pairs, key_old + key_grad.reshape(key_count, group_width), (0, col_start)
        )
        value_old = lax.dynamic_slice(
            grad_pairs, (0, model_width + col_start), (key_count, group_width)
        )
        grad_pairs = lax.dynamic_update_slice(
            grad_pairs,
            value_old + value_grad.reshape(key_count, group_width),
            (0, model_width + col_start),
        )
        return (grad_queries, grad_pairs)

    start_state = (
        jnp.zeros((slot_count, model_width), jnp.float32),
        jnp.zeros((key_count, 2 * model_width), jnp.float32),
    )
    grad_queries, grad_pairs = lax.fori_loop(0, steps_total, backward_step, start_state)
    returned = passed_along(grad_pairs[:slot_count].astype(jnp.bfloat16), "pair", -1).astype(
        jnp.float32
    )
    grad_near = (grad_pairs[slot_count:] + returned).astype(jnp.bfloat16)
    grad_projected = jnp.concatenate([grad_queries.astype(jnp.bfloat16), grad_near], axis=1)
    grad_qkv = jnp.dot(normed_low.T, grad_projected, preferred_element_type=jnp.float32)
    grad_normed_in = jnp.dot(grad_projected, qkv_back.T, preferred_element_type=jnp.float32)
    grad_inputs_norm, grad_gain_first = norm_first_back(grad_normed_in)
    grad_tokens = (grad_middle + grad_inputs_norm)[None]
    grad_gains = jnp.stack([grad_gain_first, grad_gain_second], axis=1)
    strips = (
        lax.psum_scatter(grad_gains, "rows", scatter_dimension=0, tiled=True),
        lax.psum_scatter(grad_qkv.astype(jnp.bfloat16), "rows", scatter_dimension=0, tiled=True),
        lax.psum_scatter(grad_out.astype(jnp.bfloat16), "rows", scatter_dimension=0, tiled=True),
        lax.psum_scatter(grad_up.astype(jnp.bfloat16), "rows", scatter_dimension=0, tiled=True),
        lax.psum_scatter(grad_down.astype(jnp.bfloat16), "rows", scatter_dimension=0, tiled=True),
    )
    owned = (
        lax.psum_scatter(
            strips[0].astype(jnp.bfloat16), "pair", scatter_dimension=1, tiled=True
        ).astype(jnp.float32),
        lax.psum_scatter(
            strips[1].astype(jnp.bfloat16), "pair", scatter_dimension=1, tiled=True
        ).astype(jnp.float32),
        lax.psum_scatter(
            strips[2].astype(jnp.bfloat16), "pair", scatter_dimension=1, tiled=True
        ).astype(jnp.float32),
        lax.psum_scatter(
            strips[3].astype(jnp.bfloat16), "pair", scatter_dimension=1, tiled=True
        ).astype(jnp.float32),
        lax.psum_scatter(
            strips[4].astype(jnp.bfloat16), "pair", scatter_dimension=1, tiled=True
        ).astype(jnp.float32),
    )
    return (mixed_out, grad_tokens, owned[0], owned[1], owned[2], owned[3], owned[4])


LINE = 4
HALF = 512
NEG = -1e30
bf16 = jnp.bfloat16
f32 = jnp.float32
VMEM = dict(
    down=24, up=20, normed_back=20, down_grad=20, up_grad=16, middle_back=20, project=20, input_back=18, attend_0=12, attend_1=12,
    attend_back_0=14, attend_back_1=14, attention_out=16, qkv_grad=16, out_grad=10, input_norm=18, input_grad=14, half_added=18
)


def params(name):
    return pltpu.CompilerParams(vmem_limit_bytes=VMEM.get(name, 10) * 1024 * 1024)


PLACES = dict(half_added=8, attend_1=20, touch=20, attend_back_0=20, down_sum=20, up_parts=20, up_sum=20)


def cost(name):
    return pl.CostEstimate(flops=int(PLACES.get(name, 0.5) * 1.15e9), bytes_accessed=1 << 16, transcendentals=0)


def hbm():
    return pl.BlockSpec(memory_space=pl.ANY)


def block(*shape):
    return pl.BlockSpec(shape, lambda i, s: (0,) * len(shape))


def call(kernel, name, ins, outs, scratch, flops, *args, grid=(1,)):
    out = pl.pallas_call(
        kernel,
        grid_spec=pltpu.PrefetchScalarGridSpec(
            num_scalar_prefetch=1,
            grid=grid,
            in_specs=ins,
            out_specs=[spec for spec, _ in outs],
            scratch_shapes=scratch,
        ),
        out_shape=[shape for _, shape in outs],
        compiler_params=params(name),
        cost_estimate=cost(name),
        name=name,
    )(*args)
    return out


def of(kind, *shape):
    return jax.ShapeDtypeStruct(shape, kind)


def dot(a, b, contract):
    return lax.dot_general(a, b, ((contract[:1], contract[1:]), ((), ())), preferred_element_type=f32)


def row_pairs(target):
    pairs = []
    for r in range(LINE * 4):
        z, x, c = target(r // 4, r // 2 % 2, r % 2)
        pairs.append((r, z % LINE * 4 + x * 2 + c))
    return pairs


def shift_z(v, k):
    return lax.ppermute(v, "rows", row_pairs(lambda z, x, c: (z + k, x, c)))


def swap_x(v):
    return lax.ppermute(v, "rows", row_pairs(lambda z, x, c: (z, 1 - x, c)))


def swap_c(v):
    return lax.ppermute(v, "rows", row_pairs(lambda z, x, c: (z, x, 1 - c)))


def swap_y(v):
    return lax.ppermute(v, "pair", [(0, 1), (1, 0)])


def along_line(shard):
    return [shard] + [shift_z(shard, k) for k in range(1, LINE)]


def barrier(*values):
    return lax.optimization_barrier(values)


def after(value, *others):
    return lax.optimization_barrier((value, others))[0]


def qkv_copies(info, refs, w_ref, sems, start_col, cols):
    out = []
    for dx in range(2):
        for dz in range(LINE):
            chip = lax.rem(info[0] + LINE - dz, LINE) * 2 + lax.rem(info[1] + dx, 2)
            for own in (0, 1):
                core = info[2] if own == 0 else 1 - info[2]
                out.append(
                    pltpu.make_async_copy(
                        refs[own * 2 + dx].at[dz, :, pl.ds(start_col, cols)],
                        w_ref.at[pl.ds(pl.multiple_of(chip * 128 + core * 64, 64), 64), :],
                        sems.at[(dx * LINE + dz) * 2 + own],
                    )
                )
    return out


def by_chip(z, x):
    return z * 2 + x


def by_unit(z, x):
    return z // 2 * 4 + x * 2 + z % 2


def piece_copies(info, refs, w_ref, sems, rows, cols, order):
    line, beside, across, far_a, far_b = refs
    out = [[], []]
    for dy in range(2):
        for dx in range(2):
            for dz in range(LINE):
                chip = order(lax.rem(info[0] + LINE - dz, LINE), lax.rem(info[1] + dx, 2))
                ref, at = ((line, dz), (beside, dz), (across, dz), (far_a, dz) if dz < 2 else (far_b, dz + far_b.shape[0] - LINE))[dx + 2 * dy]
                out[dy].append(
                    pltpu.make_async_copy(
                        ref.at[at, :, pl.ds(0, cols)],
                        w_ref.at[pl.ds(pl.multiple_of(chip * rows, rows), rows), pl.ds(dy * cols, cols)],
                        sems.at[(dy * 2 + dx) * LINE + dz],
                    )
                )
    return out


def start(copies):
    for c in copies:
        c.start()


def wait(copies):
    for c in copies:
        c.wait()


def project_kernel(info, xo_ref, xt_ref, *refs):
    out_ref, g_ref, w_ref, gcol_ref, nin_ref, sems = refs[4:]
    copies = qkv_copies(info, refs[:4], w_ref, sems, 0, 1536)
    gains = qkv_copies(info, refs[:4], gcol_ref, sems.at[pl.ds(16, 16)], 1536, 128)
    start(gains)
    start(copies)
    wait(gains)
    both = gcol_ref[...].T.astype(f32)[:2]
    g_ref[...] = both
    side = info[3]
    for part, x_ref in ((0, xo_ref), (1, xt_ref)):
        at = side if part == 0 else 1 - side
        tokens = pl.ds(pl.multiple_of(at * HALF, HALF), HALF)
        nin_ref[tokens, :] = (centred(x_ref[...].astype(f32))[0] * both[:1]).astype(bf16)
        if part == 0:
            wait(copies)
        for n in range(2):
            cols = slice(n * 768, n * 768 + 768)
            out_ref[tokens, cols] = dot(nin_ref[tokens, :], w_ref[:, cols], (1, 0)).astype(bf16)


def project(info, x_own, x_other, pieces):
    return call(
        project_kernel,
        "project",
        [block(HALF, 1024), block(HALF, 1024)] + [hbm()] * 4,
        [(block(1024, 1536), of(bf16, 1024, 1536)), (block(2, 1024), of(f32, 2, 1024))],
        [
            pltpu.VMEM((1024, 1536), bf16),
            pltpu.VMEM((1024, 128), bf16),
            pltpu.VMEM((1024, 1024), bf16),
            pltpu.SemaphoreType.DMA((32,)),
        ],
        2 * 1024 * 1024 * 1536,
        info,
        x_own,
        x_other,
        *pieces,
    )


TILES = ((0, 512), (256, 512), (512, 768), (768, 1024))


def own_lanes(v, head):
    lane = lax.broadcasted_iota(jnp.int32, v.shape, 1)
    return jnp.where((lane >= 64) if head else (lane < 64), v, jnp.zeros_like(v))


def attend_kernel(info, q_ref, k_ref, v_ref, bias_ref, keep_ref, send_ref, lse_ref):
    side = info[3]
    lane = lax.broadcasted_iota(jnp.int32, (256, 128), 1)
    for tile, (first, seen) in enumerate(TILES):
        rows = slice(first, first + 256)
        q_tile = q_ref[rows, :] * jnp.asarray(0.125, bf16)
        done, lse = [], []
        for head in range(2):
            s = dot(own_lanes(q_tile, head), k_ref[:seen, :], (1, 1)) + bias_ref[rows, :seen]
            top = jnp.max(s, axis=1, keepdims=True)
            p = jnp.exp(s - top)
            total = jnp.sum(p, axis=1, keepdims=True)
            lse.append(top + jnp.log(total))
            done.append(dot(p.astype(bf16), v_ref[:seen, :], (1, 0)) * (1.0 / total))
        both = jnp.where(lane < 64, done[0], done[1]).astype(bf16)
        lse_ref[0, :, rows] = jnp.where(lane == 0, lse[0], lse[1]).T[:2]
        half, row = tile // 2, tile % 2 * 256

        @pl.when(side == half)
        def _():
            keep_ref[row : row + 256, :] = both

        @pl.when(side != half)
        def _():
            send_ref[row : row + 256, :] = both


def head_parts(group):
    return [pl.BlockSpec((1024, 128), lambda h, s, j=j: (0, 6 * group + 2 * j + h)) for j in range(3)]


def attend(info, projected, bias, group):
    piece = pl.BlockSpec((HALF, 128), lambda h, s: (0, h))
    return call(
        attend_kernel,
        f"attend_{group}",
        [*head_parts(group), block(1024, 1024)],
        [
            (piece, of(bf16, HALF, 256)),
            (piece, of(bf16, HALF, 256)),
            (pl.BlockSpec((1, 2, 1024), lambda h, s: (h, 0, 0)), of(f32, 2, 2, 1024)),
        ],
        [],
        4 * 1024 * 768 * 64 * 4,
        info,
        projected,
        projected,
        projected,
        bias,
        grid=(2,),
    )


def attend_back_kernel(info, q_ref, k_ref, v_ref, bias_ref, lse_ref, keep_ref, send_ref, out_ref, dk_ref, dv_ref):
    side = info[3]
    pair = pl.program_id(0)
    k_t = k_ref[...].T
    dk_ref[...] = jnp.zeros_like(dk_ref)
    dv_ref[...] = jnp.zeros_like(dv_ref)
    for tile, (start, seen) in enumerate(TILES):
        half, row = tile // 2, tile % 2 * 256
        q_tile = q_ref[start : start + 256, :] * jnp.asarray(0.125, bf16)
        g_tile = jnp.where(side == half, keep_ref[row : row + 256, :], send_ref[row : row + 256, :])
        pieces = []
        for head in range(2):
            q_head = own_lanes(q_tile, head)
            g_head = own_lanes(g_tile, head)
            s = dot(k_ref[:seen, :], q_head, (1, 1))
            p = jnp.exp(s + bias_ref[:seen, start : start + 256] - lse_ref[0, head : head + 1, start : start + 256])
            dp = dot(v_ref[:seen, :], g_head, (1, 1))
            centre = jnp.sum(p * dp, axis=0, keepdims=True)
            ds = (p * (dp - centre)).astype(bf16)
            dv_ref[:seen, :] += dot(p.astype(bf16), g_head, (1, 0))
            dk_ref[:seen, :] += dot(ds, q_head, (1, 0))
            pieces.append(dot(k_t[head * 64 : head * 64 + 64, :seen], ds, (1, 0)) * 0.125)
        cols = pl.ds(pl.multiple_of(pair * 128, 128), 128)
        out_ref[start : start + 256, cols] = jnp.concatenate(pieces, axis=0).T.astype(bf16)
    out_ref[:, pl.ds(pl.multiple_of(256 + pair * 128, 128), 128)] = dk_ref[...].astype(bf16)
    out_ref[:, pl.ds(pl.multiple_of(512 + pair * 128, 128), 128)] = dv_ref[...].astype(bf16)


def attend_back(info, projected, bias, lse, keep, other, group):
    piece = pl.BlockSpec((HALF, 128), lambda h, s: (0, 2 * group + h))
    return pl.pallas_call(
        attend_back_kernel,
        grid_spec=pltpu.PrefetchScalarGridSpec(
            num_scalar_prefetch=1,
            grid=(2,),
            in_specs=[
                *head_parts(group),
                pl.BlockSpec((1024, 1024), lambda h, s: (0, 0)),
                pl.BlockSpec((1, 2, 1024), lambda h, s: (h, 0, 0)),
                piece,
                piece,
            ],
            out_specs=pl.BlockSpec((1024, 768), lambda h, s: (0, 0)),
            scratch_shapes=[pltpu.VMEM((1024, 128), f32), pltpu.VMEM((1024, 128), f32)],
        ),
        out_shape=jax.ShapeDtypeStruct((1024, 768), bf16),
        compiler_params=params(f"attend_back_{group}"),
        cost_estimate=cost(f"attend_back_{group}"),
        name=f"attend_back_{group}",
    )(info, projected, projected, projected, bias, lse, keep, other)


def centred(v):
    off = v - jnp.mean(v, axis=-1, keepdims=True)
    scale = lax.rsqrt(jnp.mean(off * off, axis=-1, keepdims=True) + epsilon)
    return off * scale, scale


def out_kernel(info, x_ref, k0, k1, g0, g1, w_ref, g_ref, mid_ref, nm_ref, own_ref, oth_ref, t_ref):
    places = [(info[3] if i < 2 else 1 - info[3]) * HALF + i % 2 * 256 for i in range(4)]
    places = [pl.ds(pl.multiple_of(at, 256), 256) for at in places]
    for half in range(2):
        cols = slice(half * 512, half * 512 + 512)
        branch = x_ref[:, cols].astype(f32)
        for at, ref in zip(places, (k0, k1, g0, g1)):
            branch = branch + dot(ref[...], w_ref[half, at, :], (1, 0))
        mid_ref[:, cols] = branch
    nm_ref[...] = (centred(mid_ref[...])[0] * g_ref[1:]).astype(bf16)
    for at, ref in zip(places, (k0, k1, g0, g1)):
        t_ref[at, :] = ref[...].T
    put_parities(info, t_ref, own_ref, oth_ref)


def put_parities(info, t_ref, own_ref, oth_ref):
    for dx in range(2):
        for dz in range(LINE):
            chip = lax.rem(info[0] + dz, LINE) * 2 + lax.rem(info[1] + dx, 2)
            here = pl.multiple_of(chip * 128 + info[2] * 64, 64)
            there = pl.multiple_of(chip * 128 + (1 - info[2]) * 64, 64)
            own_ref[dx * LINE + dz] = t_ref[pl.ds(here, 64), :]
            oth_ref[dx * LINE + dz] = t_ref[pl.ds(there, 64), :]


def attention_out(info, x, keeps, gots, w, gain):
    return call(
        out_kernel,
        "attention_out",
        [block(HALF, 1024)] + [block(HALF, 256)] * 4 + [block(2, 1024, 512), block(2, 1024)],
        [
            (block(HALF, 1024), of(f32, HALF, 1024)),
            (block(HALF, 1024), of(bf16, HALF, 1024)),
            (block(8, 64, HALF), of(bf16, 8, 64, HALF)),
            (block(8, 64, HALF), of(bf16, 8, 64, HALF)),
        ],
        [pltpu.VMEM((1024, HALF), bf16)],
        2 * 512 * 1024 * 1024,
        info,
        x,
        *keeps,
        *gots,
        w,
        gain,
    )


def up_kernel(info, x0_ref, x1_ref, *refs):
    act_ref, slope_ref, w_ref, sems = refs[5:]
    step = pl.program_id(0)
    near, far = piece_copies(info, refs[:5], w_ref, sems, 128, 1024, by_chip)

    @pl.when(step == 0)
    def _():
        start(near)
        start(far)
        wait(near)

    @pl.when(step == 1)
    def _():
        wait(far)

    for part, x_ref in enumerate((x0_ref, x1_ref)):
        rows = slice(part * HALF, part * HALF + HALF)
        for n in range(2):
            cols = slice(n * 512, n * 512 + 512)
            pre = dot(x_ref[...], w_ref[:, pl.ds(pl.multiple_of(step * 1024 + n * 512, 512), 512)], (1, 0))
            below = 0.5 * (1.0 + lax.erf(pre * 0.7071067811865476))
            act_ref[rows, cols] = (pre * below).astype(bf16)
            slope_ref[rows, cols] = (below + pre * (0.3989422804014327 * jnp.exp(-0.5 * pre * pre))).astype(bf16)


def up(info, x_own, x_sib, pieces):
    out = pl.BlockSpec((1024, 1024), lambda n, s: (0, lax.rem(s[3] + n, 2)))
    return call(
        up_kernel,
        "up",
        [block(HALF, 1024)] * 2 + [hbm()] * 5,
        [(out, of(bf16, 1024, 2048))] * 2,
        [pltpu.VMEM((1024, 2048), bf16), pltpu.SemaphoreType.DMA((16,))],
        4 * 512 * 1024 * 4096,
        info,
        x_own,
        x_sib,
        *pieces,
        grid=(2,),
    )


def down_kernel(info, act_ref, slope_ref, c0_ref, c1_ref, mid_ref, *refs):
    keep_ref, send_ref, gp_ref, w_ref, acc_ref, sems = refs[5:]
    step = pl.program_id(0)
    side = info[3]
    near, far = piece_copies(info, refs[:5], w_ref, sems, 256, 512, by_unit)
    mine = pl.ds(pl.multiple_of(side * 512, 512), 512)
    theirs = pl.ds(pl.multiple_of((1 - side) * 512, 512), 512)

    @pl.when(step == 0)
    def _():
        start(near)
        start(far)
        wait(near)
        wait(far)

    units = pl.ds(pl.multiple_of(step * 1024, 1024), 1024)
    for part, cot_ref in enumerate((c0_ref, c1_ref)):
        rows = slice(part * HALF, part * HALF + HALF)
        for n in range(2):
            here = pl.ds(pl.multiple_of(step * 1024 + n * 512, 512), 512)
            cols = slice(n * 512, n * 512 + 512)
            back = dot(cot_ref[:, mine], w_ref[here, :512], (1, 1)) + dot(cot_ref[:, theirs], w_ref[here, 512:], (1, 1))
            gp_ref[rows, cols] = (back * slope_ref[rows, cols].astype(f32)).astype(bf16)
        total = dot(act_ref[rows, :], w_ref[units, :], (1, 0))

        @pl.when(step == 0)
        def _():
            acc_ref[rows, :] = total

        @pl.when(step == 1)
        def _():
            done = total + acc_ref[rows, :]
            if part == 0:
                keep_ref[:, mine] = mid_ref[:, mine] + done[:, :512]
                keep_ref[:, theirs] = mid_ref[:, theirs] + done[:, 512:]
            else:
                send_ref[:, mine] = done[:, :512].astype(bf16)
                send_ref[:, theirs] = done[:, 512:].astype(bf16)


def down(info, act, slope, cot_own, cot_sib, mid, pieces):
    tile = pl.BlockSpec((1024, 1024), lambda n, s: (0, n))
    return call(
        down_kernel,
        "down",
        [tile, tile] + [block(HALF, 1024)] * 3 + [hbm()] * 5,
        [
            (block(HALF, 1024), of(f32, HALF, 1024)),
            (block(HALF, 1024), of(bf16, HALF, 1024)),
            (tile, of(bf16, 1024, 2048)),
        ],
        [pltpu.VMEM((2048, 1024), bf16), pltpu.VMEM((1024, 1024), f32), pltpu.SemaphoreType.DMA((16,))],
        4 * 512 * 1024 * 4096,
        info,
        act,
        slope,
        cot_own,
        cot_sib,
        mid,
        *pieces,
        grid=(2,),
    )


def normed_back_kernel(info, gp_ref, *refs):
    keep_ref, send_ref, w_ref, sems = refs[5:]
    near, far = piece_copies(info, refs[:5], w_ref, sems, 128, 1024, by_chip)
    start(near)
    start(far)
    wait(near)
    wait(far)
    mine = pl.ds(pl.multiple_of(info[3] * 1024, 1024), 1024)
    theirs = pl.ds(pl.multiple_of((1 - info[3]) * 1024, 1024), 1024)
    for part, out in ((1, send_ref), (0, keep_ref)):
        rows = slice(part * HALF, part * HALF + HALF)
        for n in range(2):
            dims = slice(n * 512, n * 512 + 512)
            total = dot(gp_ref[rows, mine], w_ref[dims, :1024], (1, 1)) + dot(gp_ref[rows, theirs], w_ref[dims, 1024:], (1, 1))
            out[:, dims] = total.astype(out.dtype)


def normed_back(info, gp, pieces):
    return call(
        normed_back_kernel,
        "normed_back",
        [block(1024, 2048)] + [hbm()] * 5,
        [(block(HALF, 1024), of(f32, HALF, 1024)), (block(HALF, 1024), of(bf16, HALF, 1024))],
        [pltpu.VMEM((1024, 2048), bf16), pltpu.SemaphoreType.DMA((16,))],
        2 * 512 * 1024 * 4096,
        info,
        gp,
        *pieces,
    )


def middle_back_kernel(info, e0_ref, e1_ref, cot_ref, mid_ref, g_ref, w_ref, gm_ref, gb_ref, keep, send):
    n, scale = centred(mid_ref[...])
    eg = (e0_ref[...] + e1_ref[...].astype(f32)) * g_ref[1:]
    lean = eg - jnp.mean(eg, axis=-1, keepdims=True) - n * jnp.mean(eg * n, axis=-1, keepdims=True)
    grad = cot_ref[...].astype(f32) + scale * lean
    gm_ref[...] = grad
    low = grad.astype(bf16)
    gb_ref[...] = low
    for out, at in ((keep, info[3]), (send, 1 - info[3])):
        rows = pl.ds(pl.multiple_of(at * HALF, HALF), HALF)
        out[...] = (dot(low[:, :512], w_ref[0, rows, :], (1, 1)) + dot(low[:, 512:], w_ref[1, rows, :], (1, 1))).astype(bf16)


def middle_back(info, e_keep, e_got, cot, mid, gain, w):
    return call(
        middle_back_kernel,
        "middle_back",
        [block(HALF, 1024)] * 4 + [block(2, 1024), block(2, 1024, 512)],
        [
            (block(HALF, 1024), of(f32, HALF, 1024)),
            (block(HALF, 1024), of(bf16, HALF, 1024)),
            (block(HALF, 512), of(bf16, HALF, 512)),
            (block(HALF, 512), of(bf16, HALF, 512)),
        ],
        [],
        2 * 512 * 1024 * 1024,
        info,
        e_keep,
        e_got,
        cot,
        mid,
        gain,
        w,
    )


def down_grad_kernel(info, c0_ref, c1_ref, act_ref, far_a, far_b, across, beside, own, t_ref):
    g = pl.program_id(0)

    @pl.when(g == 0)
    def _():
        t_ref[:, :HALF] = c0_ref[...].T
        t_ref[:, HALF:] = c1_ref[...].T

    x = lax.rem(info[1] + 1 - lax.rem(g, 2), 2)
    side = lax.rem(info[3] + 1 - g // 2, 2)
    rows = pl.ds(pl.multiple_of(side * 512, 512), 512)
    for half in range(2):
        units = pl.ds(pl.multiple_of(half * 1024 + x * 512, 512), 512)
        total = dot(t_ref[rows, :], act_ref[:, units], (1, 0)).astype(bf16)
        for j in range(2):
            dz = lax.rem(half * 2 + j - info[0] + LINE, LINE)
            part = total[:, j * 256 : j * 256 + 256]
            for at, ref in ((1, across), (2, beside), (3, own)):

                @pl.when(g == at)
                def _():
                    ref[dz] = part

            for ref, here in ((far_a, dz < 2), (far_b, dz >= 2)):

                @pl.when((g == 0) & here)
                def _():
                    ref[lax.rem(dz, 2)] = part


def down_grad(info, cot_own, cot_sib, act):
    return call(
        down_grad_kernel,
        "down_grad",
        [block(HALF, 1024), block(HALF, 1024), block(1024, 2048)],
        [(block(n, 512, 256), of(bf16, n, 512, 256)) for n in (2, 2, 4, 4, 4)],
        [pltpu.VMEM((1024, 1024), bf16)],
        2 * 1024 * 1024 * 2048,
        info,
        cot_own,
        cot_sib,
        act,
        grid=(4,),
    )


def stay(g, first):
    return lax.max(0, lax.min(g - first, 1))


def up_grad_kernel(info, n0_ref, n1_ref, gp_ref, far, across, beside, own, t_ref):
    g = pl.program_id(0)

    @pl.when(g == 0)
    def _():
        for dx in range(2):
            for dz in range(LINE):
                chip = lax.rem(info[0] + dz, LINE) * 2 + lax.rem(info[1] + dx, 2)
                cols = pl.ds(pl.multiple_of(chip * 128, 128), 128)
                rows = slice((dx * LINE + dz) * 128, (dx * LINE + dz) * 128 + 128)
                t_ref[rows, :HALF] = n0_ref[:, cols].T
                t_ref[rows, HALF:] = n1_ref[:, cols].T

    total = dot(t_ref[...], gp_ref[...], (1, 0)).astype(bf16).reshape(8, 128, 512)

    @pl.when(g < 2)
    def _():
        across[...] = total[:4]
        far[...] = total[4:]

    @pl.when(g >= 2)
    def _():
        own[...] = total[:4]
        beside[...] = total[4:]


def up_grad(info, nm_own, nm_sib, gp):
    right = pl.BlockSpec((1024, 512), lambda g, s: (0, lax.rem(s[3] + 1 - g // 2, 2) * 2 + lax.rem(g, 2)))
    return call(
        up_grad_kernel,
        "up_grad",
        [block(HALF, 1024), block(HALF, 1024), right],
        [
            (pl.BlockSpec((LINE, 128, 512), lambda g, s, f=f: (0, 0, stay(g, f))), of(bf16, LINE, 128, 1024))
            for f in (0, 0, 2, 2)
        ],
        [pltpu.VMEM((1024, 1024), bf16)],
        2 * 1024 * 512 * 4096,
        info,
        nm_own,
        nm_sib,
        gp,
        grid=(4,),
    )


def out_grad_kernel(info, l0_ref, r0_ref, l1_ref, r1_ref, keep_ref, send_ref):
    for out, at in ((keep_ref, info[3]), (send_ref, 1 - info[3])):
        cols = pl.ds(pl.multiple_of(at * 512, 512), 512)
        total = dot(l0_ref[...], r0_ref[:, cols], (1, 0)) + dot(l1_ref[...], r1_ref[:, cols], (1, 0))
        out[...] = total.astype(bf16).reshape(8, 64, 512)


def out_grad(info, att_t, gb, att_t_sib, gb_sib):
    return call(
        out_grad_kernel,
        "out_grad",
        [block(512, HALF), block(HALF, 1024)] * 2,
        [(block(8, 64, 512), of(bf16, 8, 64, 512))] * 2,
        [],
        2 * 512 * 1024 * 1024,
        info,
        att_t.reshape(512, HALF),
        gb,
        att_t_sib.reshape(512, HALF),
        gb_sib,
    )


def input_back_kernel(info, d0_ref, d1_ref, *refs):
    keep_ref, send_ref, w_ref, sems = refs[4:]
    copies = qkv_copies(info, refs[:4], w_ref, sems, 0, 1536)
    start(copies)
    wait(copies)
    for part, out in ((1, send_ref), (0, keep_ref)):
        at = info[3] if part == 0 else 1 - info[3]
        slots = pl.ds(pl.multiple_of(at * HALF, HALF), HALF)
        for n in range(2):
            dims = slice(n * 512, n * 512 + 512)
            total = dot(d0_ref[slots, :], w_ref[dims, :768], (1, 1)) + dot(d1_ref[slots, :], w_ref[dims, 768:], (1, 1))
            out[:, dims] = total.astype(out.dtype)


def input_back(info, d0, d1, pieces):
    return call(
        input_back_kernel,
        "input_back",
        [block(1024, 768)] * 2 + [hbm()] * 4,
        [(block(HALF, 1024), of(f32, HALF, 1024)), (block(HALF, 1024), of(bf16, HALF, 1024))],
        [pltpu.VMEM((1024, 1536), bf16), pltpu.SemaphoreType.DMA((16,))],
        2 * 1024 * 1024 * 1536,
        info,
        d0,
        d1,
        *pieces,
    )


def qkv_grad_kernel(info, l0_ref, r0_ref, l1_ref, r1_ref, *refs):
    beside, own = refs[-2:]
    total = dot(l0_ref[...], r0_ref[...], (1, 0)) + dot(l1_ref[...], r1_ref[...], (1, 0))
    total = total.astype(bf16).reshape(8, 64, 768)
    own[:, :, :768] = total[:4]
    beside[:, :, :768] = total[4:]
    if len(refs) == 4:
        both = (refs[0][...].astype(f32) + refs[1][...].astype(f32)).astype(bf16)
        own[:, :, 768:] = both[:4]
        beside[:, :, 768:] = both[4:]


def qkv_grad(info, nin_t, dproj, nin_t_sib, dproj_sib, more=()):
    width = 768 + 512 * bool(more)
    return call(
        qkv_grad_kernel,
        "qkv_grad",
        [block(512, 1024), block(1024, 768)] * 2 + [block(8, 64, 512)] * len(more),
        [(block(4, 64, width), of(bf16, 4, 64, width))] * 2,
        [],
        2 * 2048 * 512 * 768,
        info,
        nin_t.reshape(512, 1024),
        dproj,
        nin_t_sib.reshape(512, 1024),
        dproj_sib,
        *more,
    )


def input_norm_kernel(info, xo_ref, xt_ref, g_ref, own_ref, oth_ref, t_ref):
    side = info[3]
    for part, x_ref in ((0, xo_ref), (1, xt_ref)):
        at = side if part == 0 else 1 - side
        normed = (centred(x_ref[...].astype(f32))[0] * g_ref[:1]).astype(bf16)
        t_ref[:, pl.ds(pl.multiple_of(at * HALF, HALF), HALF)] = normed.T
    put_parities(info, t_ref, own_ref, oth_ref)


def input_norm(info, x_own, x_other, gains):
    return call(
        input_norm_kernel,
        "input_norm",
        [block(HALF, 1024), block(HALF, 1024), block(2, 1024)],
        [(block(8, 64, 1024), of(bf16, 8, 64, 1024))] * 2,
        [pltpu.VMEM((1024, 1024), bf16)],
        20 << 20,
        info,
        x_own,
        x_other,
        gains,
    )


def heads_kernel(info, w_ref, got_ref, gain_ref, out_ref):
    side = info[3] == 0
    first, middle, last = w_ref[:, :512], got_ref[:, :512], w_ref[:, 1024:]
    q = jnp.where(side, first, middle)
    k = jnp.where(side, last, first)
    v = jnp.where(side, middle, last)
    for i in range(2):
        for j, part in enumerate((q, k, v)):
            out_ref[:, i * 768 + j * 256 : i * 768 + j * 256 + 256] = part[:, i * 256 : i * 256 + 256]
    lane = lax.broadcasted_iota(jnp.int32, (w_ref.shape[0], 128), 1)
    mine = jnp.broadcast_to(gain_ref[...].astype(f32), lane.shape)
    theirs = jnp.broadcast_to(got_ref[:, 512:513].astype(f32), lane.shape)
    out_ref[:, 1536:] = jnp.where((lane == 0) == side, mine, theirs).astype(bf16)


def heads_of(info, w, got, gains):
    return call(
        heads_kernel,
        "heads",
        [block(64, 1536), block(64, 640), block(64, 1)],
        [(block(64, 1664), of(bf16, 64, 1664))],
        [],
        1 << 16,
        info,
        w,
        got,
        gains,
    )[0]


def by_core_kernel(info, up_ref, own_ref, oth_ref):
    for ref, core in ((own_ref, info[2]), (oth_ref, 1 - info[2])):
        for i, to in enumerate((0, 2, 1, 3)):
            ref[:, to * 256 : to * 256 + 256] = up_ref[:, pl.ds(pl.multiple_of(i * 512 + core * 256, 256), 256)]


def by_core(info, w_up):
    return call(
        by_core_kernel,
        "by_core",
        [block(64, 2048)],
        [(block(64, 1024), of(bf16, 64, 1024))] * 2,
        [],
        1 << 16,
        info,
        w_up,
    )


def both_rows_kernel(info, own_ref, got_ref, out_ref):
    out_ref[pl.ds(pl.multiple_of(info[2] * 64, 64), 64), :] = own_ref[...]
    out_ref[pl.ds(pl.multiple_of((1 - info[2]) * 64, 64), 64), :] = got_ref[...]


def both_rows(info, own, got):
    return call(
        both_rows_kernel,
        "both_rows",
        [block(64, 1024)] * 2,
        [(block(128, 1024), of(bf16, 128, 1024))],
        [],
        1 << 16,
        info,
        own,
        got,
    )[0]


def added_kernel(info, a_ref, b_ref, out_ref):
    out_ref[...] = (a_ref[...].astype(f32) + b_ref[...].astype(f32)).astype(bf16)


def added(info, a, b, name="added"):
    steps = 2
    spec = pl.BlockSpec((a.shape[0] // steps, *a.shape[1:]), lambda i, s: (i,) + (0,) * (a.ndim - 1))
    return call(added_kernel, name, [spec, spec], [(spec, of(bf16, *a.shape))], [], 0, info, a, b, grid=(steps,))[0]


def half_added_kernel(info, a_ref, b_ref, first_ref, second_ref, a_out, b_out):
    a_out[:2] = (a_ref[:2].astype(f32) + first_ref[...].astype(f32)).astype(bf16)
    a_out[2:] = a_ref[2:]
    b_out[:2] = b_ref[:2]
    b_out[2:] = (b_ref[2:].astype(f32) + second_ref[...].astype(f32)).astype(bf16)


def half_added(info, a, b, first, second):
    spec, half = block(*a.shape), block(*first.shape)
    return call(
        half_added_kernel, "half_added", [spec, spec, half, half], [(spec, of(bf16, *a.shape))] * 2, [], 0, info, a, b, first, second
    )


def line_parts_kernel(info, a_ref, b_ref, c_ref, *outs):
    for k, out in enumerate(outs):
        out[...] = (a_ref[k].astype(f32) + b_ref[k].astype(f32) + c_ref[k].astype(f32)).astype(bf16)


def line_parts(info, own, from_x, from_y, name):
    spec, out = block(*own.shape), block(*own.shape[1:])
    return call(
        line_parts_kernel, name, [spec] * 3, [(out, of(bf16, *own.shape[1:]))] * LINE, [], 0, info, own, from_x, from_y
    )


def qkv_parts_kernel(info, a_ref, ax_ref, b_ref, bx_ref, *outs):
    for k, out in enumerate(outs):
        out[:, :1280] = (a_ref[k].astype(f32) + ax_ref[k].astype(f32)).astype(bf16)
        out[:, 1280:] = (b_ref[k].astype(f32) + bx_ref[k].astype(f32)).astype(bf16)


def qkv_parts(info, a, a_x, b, b_x):
    return call(
        qkv_parts_kernel,
        "qkv_parts",
        [block(4, 64, 1280)] * 2 + [block(4, 64, 768)] * 2,
        [(block(64, 2048), of(bf16, 64, 2048))] * LINE,
        [],
        0,
        info,
        a,
        a_x,
        b,
        b_x,
    )


def stack_kernel(info, *refs):
    for k in range(LINE):
        refs[LINE][k] = refs[k][...]


def stacked(info, parts, name):
    shape = parts[0].shape
    return call(
        stack_kernel, name, [block(*shape)] * LINE, [(block(LINE, *shape), of(bf16, LINE, *shape))], [], 0, info, *parts
    )[0]


def touch_kernel(info, a_ref, out_ref):
    out_ref[...] = a_ref[...]


def touch(info, a):
    return call(touch_kernel, "touch", [block(*a.shape)], [(block(*a.shape), of(a.dtype, *a.shape))], [], 0, info, a)[0]


def summed(refs, *at):
    total = refs[0][at].astype(f32)
    for ref in refs[1:]:
        total = total + ref[at].astype(f32)
    return total


def down_sum_kernel(info, *refs):
    refs[4][...] = summed(refs[:4]).T


def down_sum(info, parts):
    return call(
        down_sum_kernel,
        "down_sum",
        [block(512, 256)] * 4,
        [(block(256, 512), of(f32, 256, 512))],
        [],
        0,
        info,
        *parts,
    )[0]


def up_sum_kernel(info, *refs):
    for out, core in ((refs[4], info[2]), (refs[5], 1 - info[2])):
        out[...] = summed(refs[:4], pl.ds(pl.multiple_of(core * 64, 64), 64))


def up_sum(info, parts):
    return call(
        up_sum_kernel,
        "up_sum",
        [block(128, 1024)] * 4,
        [(block(64, 1024), of(f32, 64, 1024))] * 2,
        [],
        0,
        info,
        *parts,
    )


def up_whole_kernel(info, mine_ref, got_ref, w_ref, in_ref, out_ref, own_ref, send_ref):
    for ref, core in ((mine_ref, info[2]), (got_ref, 1 - info[2])):
        for i, place in enumerate((0, 2, 1, 3)):
            cols = pl.ds(pl.multiple_of(i * 512 + core * 256, 256), 256)
            out_ref[:, cols] = ref[:, place * 256 : place * 256 + 256]
    total = jnp.sum(w_ref[...].astype(f32) * out_ref[...], axis=1, keepdims=True)
    mid = jnp.broadcast_to(total, in_ref.shape)
    first = info[3] == 0
    own_ref[...] = jnp.where(first, in_ref[...], mid)
    send_ref[...] = jnp.where(first, mid, in_ref[...])


def up_whole(info, mine, got, w, in_sums):
    return call(
        up_whole_kernel,
        "up_whole",
        [block(64, 1024)] * 2 + [block(64, 2048), block(64, 128)],
        [(block(64, 2048), of(f32, 64, 2048))] + [(block(64, 128), of(f32, 64, 128))] * 2,
        [],
        0,
        info,
        mine,
        got,
        w,
        in_sums,
    )


def qkv_sum_kernel(info, *refs):
    heads_ref, keep_ref, send_ref, sum_ref, out_ref = refs[4:]
    total = summed(refs[:4])
    out_ref[...] = total[:, 768:1280]
    groups = (total[:, :768], total[:, 1280:])
    q, k, v = (jnp.concatenate([g[:, j : j + 256] for g in groups], axis=1) for j in (0, 256, 512))
    weights = heads_ref[...].astype(f32)
    by_row = jnp.sum(weights[:, :768] * groups[0], axis=1, keepdims=True) + jnp.sum(
        weights[:, 768:1536] * groups[1], axis=1, keepdims=True
    )
    sum_ref[...] = jnp.broadcast_to(by_row, sum_ref.shape)
    first = info[3] == 0
    keep_ref[:, :512] = jnp.where(first, q, k)
    keep_ref[:, 512:] = jnp.where(first, k, v)
    send_ref[...] = jnp.where(first, v, q)


def qkv_sum(info, parts, heads):
    return call(
        qkv_sum_kernel,
        "qkv_sum",
        [block(64, 2048)] * 4 + [block(64, 1664)],
        [(block(64, n), of(f32, 64, n)) for n in (1024, 512, 128, 512)],
        [],
        0,
        info,
        *parts,
        heads,
    )


def qkv_whole_kernel(info, keep_ref, got_ref, own_ref, other_ref, gain_ref, out_ref, gg_ref):
    out_ref[:, :512] = keep_ref[:, :512]
    out_ref[:, 512:1024] = got_ref[...]
    out_ref[:, 1024:] = keep_ref[:, 512:]
    gg_ref[...] = (own_ref[:, :1] + other_ref[:, :1]) / gain_ref[...].astype(f32)


def qkv_whole(info, keep, got, own_sums, other_sums, gains):
    return call(
        qkv_whole_kernel,
        "qkv_whole",
        [block(64, 1024), block(64, 512), block(64, 128), block(64, 128), block(64, 1)],
        [(block(64, 1536), of(f32, 64, 1536)), (block(64, 1), of(f32, 64, 1))],
        [],
        0,
        info,
        keep,
        got,
        own_sums,
        other_sums,
        gains,
    )


def input_grad_kernel(info, x_ref, e0_ref, e1_ref, gm_ref, g_ref, out_ref):
    n, scale = centred(x_ref[...].astype(f32))
    eg = (e0_ref[...] + e1_ref[...].astype(f32)) * g_ref[:1]
    lean = eg - jnp.mean(eg, axis=-1, keepdims=True) - n * jnp.mean(eg * n, axis=-1, keepdims=True)
    out_ref[...] = gm_ref[...] + scale * lean


def input_grad(info, x, e_own, e_got, gm, gains):
    rows = pl.BlockSpec((256, 1024), lambda i, s: (i, 0))
    return call(
        input_grad_kernel,
        "input_grad",
        [rows] * 4 + [block(2, 1024)],
        [(rows, of(f32, HALF, 1024))],
        [],
        0,
        info,
        x,
        e_own,
        e_got,
        gm,
        gains,
        grid=(2,),
    )[0]


def slot_bias(phones, prompts, targets):
    places = jnp.arange(HALF, dtype=jnp.int32)
    count = phones.shape[0]
    segs, is_phone = [], None
    for lengths in (phones + prompts, targets):
        ends = jnp.stack([sum(lengths[i] for i in range(upto + 1)) for upto in range(count)])
        seg = jnp.sum((places[:, None] >= ends[None, :]).astype(jnp.int32), axis=1)
        segs.append(seg)
        if is_phone is None:
            onehot = seg[:, None] == jnp.arange(count, dtype=jnp.int32)[None, :]
            phone_ends = jnp.sum(jnp.where(onehot, (ends - lengths + phones)[None, :], 0), axis=1)
            is_phone = places < phone_ends
    seg = jnp.concatenate(segs)
    phone = jnp.concatenate([is_phone, jnp.zeros((HALF,), dtype=bool)])
    order = jnp.arange(2 * HALF, dtype=jnp.int32)
    allowed = (seg[:, None] == seg[None, :]) & (
        phone[:, None] | (jnp.logical_not(phone)[None, :] & (order[:, None] <= order[None, :]))
    )
    allowed_t = (seg[:, None] == seg[None, :]) & (
        phone[None, :] | (jnp.logical_not(phone)[:, None] & (order[None, :] <= order[:, None]))
    )
    bias = jnp.where(allowed, 0.0, NEG).astype(f32)
    return bias, jnp.where(allowed_t, 0.0, NEG).astype(f32)


def line_shards(tokens, cotangent, gains, w_qkv, w_out, w_up, w_down, phone_len, prompt_len, target_len):
    r = lax.axis_index("rows")
    side = lax.axis_index("pair")
    core = r % 2
    info = jnp.stack([r // 4, r // 2 % 2, core, side]).astype(jnp.int32)
    x_own = tokens[0]
    cot = cotangent[0]

    out_all = lax.all_gather(w_out, ("pair", "rows"), axis=0, tiled=True).reshape(2, 1024, 512)
    crossed = swap_y(jnp.concatenate([w_qkv[:, 512:1024], jnp.pad(gains, ((0, 0), (0, 127)))], axis=1))
    x_other = swap_y(x_own)
    heads = heads_of(info, w_qkv, crossed, gains)
    pieces = along_line(heads)
    up_keep, up_send = by_core(info, after(w_up, heads))
    up_got = swap_c(up_send)
    bias_t, bias = slot_bias(after(phone_len, up_keep)[0], prompt_len[0], target_len[0])
    up_piece = both_rows(info, up_keep, up_got)
    pieces, x_other, bias, bias_t, up_piece = barrier(pieces, x_other, bias, bias_t, up_piece)
    qkv_line = stacked(info, pieces, "qkv_stack")
    beside = swap_x(qkv_line)
    qkv_line_sib = swap_c(qkv_line)
    up_line = along_line(after(up_piece, qkv_line))
    beside_sib = swap_c(beside)
    heads = touch(info, after(heads, up_line))
    up_line = stacked(info, after(up_line, heads, beside_sib, qkv_line_sib), "up_stack")
    up_x, up_y = swap_x(up_line), swap_y(up_line)

    qkv_pieces = (qkv_line, beside, after(qkv_line_sib, up_line), after(beside_sib, up_line))
    projected, gain_all = project(info, x_own, x_other, qkv_pieces)
    down_line = along_line(after(w_down, projected))
    keep0, send0, lse0 = attend(info, projected, bias, 0)
    got0 = swap_y(send0)
    up_x, up_y = after((up_x, up_y), keep0)
    up_far = swap_x(up_y)
    keep1, send1, lse1 = attend(info, projected, after(bias, keep0), 1)
    got1 = swap_y(send1)
    down_line = stacked(info, after(down_line, keep1), "down_stack")
    down_x = swap_x(down_line)
    cot_sib = swap_c(after(cot, keep1))
    nin_t, nin_t_oth = input_norm(info, after(x_own, down_line), x_other, gain_all)
    down_y = swap_y(after(down_line, got0))
    gain_all = touch(info, after(gain_all, nin_t, up_far, got0, out_all))
    got1 = after(got1, gain_all)
    mid, nm_own, att_t, att_t_oth = attention_out(info, x_own, (keep0, keep1), (got0, got1), out_all, gain_all)
    nm_sib = swap_c(nm_own)
    nin_t_sib = swap_c(after(nin_t_oth, nm_own))
    att_t_sib = swap_c(att_t_oth)
    up_pieces = (up_line, up_x, up_y, up_far, up_far)
    down_far = [swap_y(down_x[:2]), swap_x(down_y[2:])]
    gain_all = touch(info, after(gain_all, nm_own, down_x, down_y))
    nm_sib = after(nm_sib, gain_all)
    act, slope = up(info, nm_own, nm_sib, up_pieces)
    down_pieces = (down_line, down_x, down_y, *down_far)
    mixed_keep, mixed_send, gp = down(info, act, slope, cot, cot_sib, mid, down_pieces)

    gp, nin_t_sib, att_t_sib = barrier(gp, nin_t_sib, att_t_sib)
    mixed_got = swap_c(mixed_send)
    e_keep, e_send = normed_back(info, gp, up_pieces)
    e_got = swap_c(e_send)
    far, far_b, down_across, down_beside, down_own = down_grad(info, cot, cot_sib, after(act, e_keep))
    down_far = (swap_x(far), swap_y(far_b))
    gm, gb, ga_keep, ga_send = middle_back(info, after(e_keep, far), after(e_got, far), cot, mid, gain_all, out_all)
    ga_got = swap_y(ga_send)
    gb_sib = swap_c(gb)
    far, up_across, up_beside, up_own = up_grad(info, nm_own, nm_sib, after(gp, gb))
    down_across, down_beside = half_added(info, after(down_across, far), down_beside, *after(down_far, far))
    down_x, down_y = swap_x(down_beside), swap_y(down_across)
    gb_sib = after(gb_sib, down_across)
    out_keep, out_send = out_grad(info, att_t, after(gb, down_across), att_t_sib, gb_sib)
    out_got = swap_y(out_send)
    up_far = swap_x(after(far, out_keep))
    ga_got = after(ga_got, out_keep)
    dproj0 = attend_back(info, projected, after(bias_t, out_keep), lse0, ga_keep, ga_got, 0)
    dproj0_sib = swap_c(dproj0)
    down_x, down_y = after((down_x, down_y), dproj0)
    down_parts = line_parts(info, down_own, down_x, down_y, "down_parts")
    down_shift = [shift_z(down_parts[k], k) for k in range(1, LINE)]
    up_x = swap_x(up_beside)
    gain_all = touch(info, after(gain_all, out_got, down_parts))
    dproj0_sib = after(dproj0_sib, gain_all)
    first_beside, first_own = qkv_grad(info, nin_t, after(dproj0, gain_all), nin_t_sib, dproj0_sib, (out_keep, out_got))
    first_x = swap_x(first_beside)
    up_across = added(info, up_across, after(up_far, first_own))
    up_y = swap_y(up_across)
    dproj1 = attend_back(info, projected, after(bias_t, first_own, up_across), lse1, ga_keep, ga_got, 1)
    dproj1_sib = swap_c(dproj1)
    g_down = down_sum(info, (after(down_parts[0], dproj1), *after(down_shift, dproj1)))
    up_x, up_y = after((up_x, up_y), g_down)
    up_parts = line_parts(info, up_own, up_x, up_y, "up_parts")
    up_shift = [shift_z(up_parts[k], k) for k in range(1, LINE)]
    dproj1_sib = after(dproj1_sib, up_parts)
    second_beside, second_own = qkv_grad(info, nin_t, after(dproj1, up_parts), nin_t_sib, dproj1_sib)
    second_x = swap_x(second_beside)
    e_own, e_send = input_back(info, after(dproj0, second_own), dproj1, qkv_pieces)
    e_got = swap_y(e_send)
    first_x, second_x = after((first_x, second_x), e_own)
    heads_parts = qkv_parts(info, first_own, first_x, second_own, second_x)
    qkv_shift = [shift_z(heads_parts[k], k) for k in range(1, LINE)]
    up_mine, up_send = up_sum(info, (after(up_parts[0], heads_parts), *up_shift))
    up_got = swap_c(up_send)
    mixed = added(info, mixed_keep, after(mixed_got, up_mine), "mixed")
    grad_tokens = input_grad(info, after(x_own, mixed), e_own, after(e_got, mixed), gm, gain_all)
    keep, send, in_sums, g_out = qkv_sum(info, (after(heads_parts[0], grad_tokens), *after(qkv_shift, grad_tokens)), heads)
    got = swap_y(send)
    g_up, gain_own, gain_send = up_whole(info, up_mine, after(up_got, keep), w_up, in_sums)
    gain_got = swap_y(gain_send)
    g_qkv, grad_gains = qkv_whole(info, keep, after(got, g_up), gain_own, gain_got, gains)
    return (mixed[None], grad_tokens[None], grad_gains, g_qkv, g_out, g_up, g_down)


def solution(mesh):
    lined = mesh.shape["rows"] == 4 * LINE and mesh.shape["pair"] == 2
    return jax.shard_map(
        line_shards if lined else shards,
        mesh=mesh,
        in_specs=(
            P("rows", "pair", None),
            P("rows", "pair", None),
            P("rows", "pair"),
            P("rows", "pair"),
            P("rows", "pair"),
            P("rows", "pair"),
            P("rows", "pair"),
            P("rows", None),
            P("rows", None),
            P("rows", None),
        ),
        out_specs=(
            P("rows", "pair", None),
            P("rows", "pair", None),
            P("rows", "pair"),
            P("rows", "pair"),
            P("rows", "pair"),
            P("rows", "pair"),
            P("rows", "pair"),
        ),
        check_vma=False,
    )
```

```python
import functools

import jax
import jax.numpy as jnp
from jax import lax
from jax.experimental import pallas as pl
from jax.experimental.pallas import tpu as pltpu
from jax.sharding import PartitionSpec as P

HEADS = 16
HEAD_DIM = 64


epsilon = 1e-05


def passed_along(value, axis, steps):
    count = lax.axis_size(axis)
    leading, last = (max(0, -steps), min(count, count - steps))
    return lax.ppermute(value, axis, [(source, source + steps) for source in range(leading, last)])


def slot_layout(side_index, phones, prompts, targets, slot_count):
    lengths = jnp.where(side_index == 0, phones + prompts, targets)
    count = lengths.shape[0]
    seg_ends = jnp.stack([sum(lengths[i] for i in range(upto + 1)) for upto in range(count)])
    starts = seg_ends - lengths
    places = jnp.arange(slot_count, dtype=jnp.int32)
    segment = jnp.sum((places[:, None] >= seg_ends[None, :]).astype(jnp.int32), axis=1)
    onehot = (segment[:, None] == jnp.arange(lengths.shape[0], dtype=jnp.int32)[None, :]).astype(
        jnp.int32
    )
    within = places - jnp.sum(onehot * starts[None, :], axis=1)
    phone_here = jnp.sum(onehot * phones[None, :], axis=1)
    is_phone = jnp.logical_and(side_index == 0, within < phone_here)
    ordering = places + side_index * slot_count
    return (segment, is_phone, ordering)


def permitted(query_side, key_side):
    query_seg, query_phone, query_order = query_side
    key_seg, key_phone, key_order = key_side
    same_seg = query_seg[:, None] == key_seg[None, :]
    earlier = key_order[None, :] <= query_order[:, None]
    return same_seg & (key_phone[None, :] | jnp.logical_not(query_phone)[:, None] & earlier)


def normalize(values, gain_row):
    centred = values - jnp.mean(values, axis=-1, keepdims=True)
    spread = jnp.mean(centred * centred, axis=-1, keepdims=True)
    return centred * lax.rsqrt(spread + epsilon) * gain_row


def exact_gelu(values):
    return jax.nn.gelu(values, approximate=False)


def softmax_rows(query_piece, key_piece, allowed):
    scores = jnp.einsum(
        "qhd,khd->hqk", query_piece, key_piece, preferred_element_type=jnp.float32
    ) * HEAD_DIM ** (-0.5)
    scores = jnp.where(allowed[None], scores, -1e30)
    row_max = jnp.max(scores, axis=-1, keepdims=True)
    exponents = jnp.exp(scores - row_max)
    return exponents / jnp.sum(exponents, axis=-1, keepdims=True)


def shards(tokens, cotangent, gains, w_qkv, w_out, w_up, w_down, phone_len, prompt_len, target_len):
    slot_count = tokens.shape[1]
    model_width = tokens.shape[2]
    inputs = tokens[0].astype(jnp.float32)
    side_index = lax.axis_index("pair")
    paired = (
        lax.all_gather(gains, "pair", axis=1, tiled=True),
        lax.all_gather(w_qkv, "pair", axis=1, tiled=True),
        lax.all_gather(w_out, "pair", axis=1, tiled=True),
        lax.all_gather(w_up, "pair", axis=1, tiled=True),
        lax.all_gather(w_down, "pair", axis=1, tiled=True),
    )
    gain_all, qkv_all, out_all, up_all, down_all = (
        lax.all_gather(paired[0], "rows", axis=0, tiled=True),
        lax.all_gather(paired[1], "rows", axis=0, tiled=True),
        lax.all_gather(paired[2], "rows", axis=0, tiled=True),
        lax.all_gather(paired[3], "rows", axis=0, tiled=True),
        lax.all_gather(paired[4], "rows", axis=0, tiled=True),
    )
    gain_first = gain_all[:, 0].astype(jnp.float32)
    gain_second = gain_all[:, 1].astype(jnp.float32)
    phones = phone_len[0]
    prompts = prompt_len[0]
    targets = target_len[0]
    own_layout = slot_layout(side_index, phones, prompts, targets, slot_count)
    far_layout = slot_layout(0, phones, prompts, targets, slot_count)
    key_layout = tuple(
        (
            jnp.concatenate([far_part, own_part])
            for far_part, own_part in zip(far_layout, own_layout)
        )
    )
    far_live = jnp.concatenate(
        [jnp.full((slot_count,), side_index == 1), jnp.ones((slot_count,), dtype=bool)]
    )
    normed_in, norm_first_back = jax.vjp(normalize, inputs, gain_first)
    normed_low = normed_in.astype(jnp.bfloat16)
    projected = jnp.dot(normed_low, qkv_all, preferred_element_type=jnp.float32).astype(
        jnp.bfloat16
    )
    queries = projected[:, :model_width]
    near_pairs = projected[:, model_width:]
    far_pairs = passed_along(near_pairs, "pair", 1)
    key_value = jnp.concatenate([far_pairs, near_pairs], axis=0)
    block_rows = min(512, slot_count)
    per_group = min(4, HEADS)
    group_width = per_group * HEAD_DIM
    groups = HEADS // per_group
    steps_total = slot_count // block_rows * groups
    key_count = 2 * slot_count

    def piece_of(item_index):
        row_start = item_index // groups * block_rows
        col_start = item_index % groups * group_width
        query_piece = lax.dynamic_slice(
            queries, (row_start, col_start), (block_rows, group_width)
        ).reshape(block_rows, per_group, HEAD_DIM)
        key_piece = lax.dynamic_slice(key_value, (0, col_start), (key_count, group_width)).reshape(
            key_count, per_group, HEAD_DIM
        )
        value_piece = lax.dynamic_slice(
            key_value, (0, model_width + col_start), (key_count, group_width)
        ).reshape(key_count, per_group, HEAD_DIM)
        query_layout = tuple((member for member in own_layout))
        allowed = permitted(query_layout, key_layout) & far_live[None, :]
        attn_probs = softmax_rows(query_piece, key_piece, allowed)
        return (row_start, col_start, query_piece, key_piece, value_piece, attn_probs)

    def forward_step(item_index, attended):
        row_start, col_start, query_piece, key_piece, value_piece, attn_probs = piece_of(item_index)
        head_mix = jnp.einsum(
            "hqk,khd->qhd",
            attn_probs.astype(jnp.bfloat16),
            value_piece,
            preferred_element_type=jnp.float32,
        )
        return lax.dynamic_update_slice(
            attended, head_mix.reshape(block_rows, group_width), (row_start, col_start)
        )

    attended = lax.fori_loop(
        0, steps_total, forward_step, jnp.zeros((slot_count, model_width), jnp.float32)
    )
    attended_low = attended.astype(jnp.bfloat16)
    middle = inputs + jnp.dot(attended_low, out_all, preferred_element_type=jnp.float32)
    normed_mid, norm_second_back = jax.vjp(normalize, middle, gain_second)
    normed_mid_low = normed_mid.astype(jnp.bfloat16)
    pre_act = jnp.dot(normed_mid_low, up_all, preferred_element_type=jnp.float32)
    activated, gelu_back = jax.vjp(exact_gelu, pre_act)
    activated_low = activated.astype(jnp.bfloat16)
    result = middle + jnp.dot(activated_low, down_all, preferred_element_type=jnp.float32)
    mixed_out = result.astype(jnp.bfloat16)[None]
    qkv_back, out_back, up_back, down_back = (qkv_all, out_all, up_all, down_all)
    grad_result = cotangent[0]
    grad_down = jnp.dot(activated_low.T, grad_result, preferred_element_type=jnp.float32)
    grad_act = jnp.dot(grad_result, down_back.T, preferred_element_type=jnp.float32)
    grad_pre = gelu_back(grad_act)[0].astype(jnp.bfloat16)
    grad_up = jnp.dot(normed_mid_low.T, grad_pre, preferred_element_type=jnp.float32)
    grad_normed_mid = jnp.dot(grad_pre, up_back.T, preferred_element_type=jnp.float32)
    grad_middle_norm, grad_gain_second = norm_second_back(grad_normed_mid)
    grad_middle = grad_result.astype(jnp.float32) + grad_middle_norm
    grad_branch = grad_middle.astype(jnp.bfloat16)
    grad_out = jnp.dot(attended_low.T, grad_branch, preferred_element_type=jnp.float32)
    grad_attended = jnp.dot(grad_branch, out_back.T, preferred_element_type=jnp.float32).astype(
        jnp.bfloat16
    )

    def backward_step(item_index, running):
        grad_queries, grad_pairs = running
        row_start, col_start, query_piece, key_piece, value_piece, attn_probs = piece_of(item_index)
        grad_piece = lax.dynamic_slice(
            grad_attended, (row_start, col_start), (block_rows, group_width)
        ).reshape(block_rows, per_group, HEAD_DIM)
        grad_probs = jnp.einsum(
            "qhd,khd->hqk", grad_piece, value_piece, preferred_element_type=jnp.float32
        )
        centre = jnp.sum(grad_probs * attn_probs, axis=-1, keepdims=True)
        grad_scores = (attn_probs * (grad_probs - centre)).astype(jnp.bfloat16)
        score_scale = HEAD_DIM ** (-0.5)
        query_grad = (
            jnp.einsum("hqk,khd->qhd", grad_scores, key_piece, preferred_element_type=jnp.float32)
            * score_scale
        )
        key_grad = (
            jnp.einsum("hqk,qhd->khd", grad_scores, query_piece, preferred_element_type=jnp.float32)
            * score_scale
        )
        value_grad = jnp.einsum(
            "hqk,qhd->khd",
            attn_probs.astype(jnp.bfloat16),
            grad_piece,
            preferred_element_type=jnp.float32,
        )
        grad_queries = lax.dynamic_update_slice(
            grad_queries, query_grad.reshape(block_rows, group_width), (row_start, col_start)
        )
        key_old = lax.dynamic_slice(grad_pairs, (0, col_start), (key_count, group_width))
        grad_pairs = lax.dynamic_update_slice(
            grad_pairs, key_old + key_grad.reshape(key_count, group_width), (0, col_start)
        )
        value_old = lax.dynamic_slice(
            grad_pairs, (0, model_width + col_start), (key_count, group_width)
        )
        grad_pairs = lax.dynamic_update_slice(
            grad_pairs,
            value_old + value_grad.reshape(key_count, group_width),
            (0, model_width + col_start),
        )
        return (grad_queries, grad_pairs)

    start_state = (
        jnp.zeros((slot_count, model_width), jnp.float32),
        jnp.zeros((key_count, 2 * model_width), jnp.float32),
    )
    grad_queries, grad_pairs = lax.fori_loop(0, steps_total, backward_step, start_state)
    returned = passed_along(grad_pairs[:slot_count].astype(jnp.bfloat16), "pair", -1).astype(
        jnp.float32
    )
    grad_near = (grad_pairs[slot_count:] + returned).astype(jnp.bfloat16)
    grad_projected = jnp.concatenate([grad_queries.astype(jnp.bfloat16), grad_near], axis=1)
    grad_qkv = jnp.dot(normed_low.T, grad_projected, preferred_element_type=jnp.float32)
    grad_normed_in = jnp.dot(grad_projected, qkv_back.T, preferred_element_type=jnp.float32)
    grad_inputs_norm, grad_gain_first = norm_first_back(grad_normed_in)
    grad_tokens = (grad_middle + grad_inputs_norm)[None]
    grad_gains = jnp.stack([grad_gain_first, grad_gain_second], axis=1)
    strips = (
        lax.psum_scatter(grad_gains, "rows", scatter_dimension=0, tiled=True),
        lax.psum_scatter(grad_qkv.astype(jnp.bfloat16), "rows", scatter_dimension=0, tiled=True),
        lax.psum_scatter(grad_out.astype(jnp.bfloat16), "rows", scatter_dimension=0, tiled=True),
        lax.psum_scatter(grad_up.astype(jnp.bfloat16), "rows", scatter_dimension=0, tiled=True),
        lax.psum_scatter(grad_down.astype(jnp.bfloat16), "rows", scatter_dimension=0, tiled=True),
    )
    owned = (
        lax.psum_scatter(
            strips[0].astype(jnp.bfloat16), "pair", scatter_dimension=1, tiled=True
        ).astype(jnp.float32),
        lax.psum_scatter(
            strips[1].astype(jnp.bfloat16), "pair", scatter_dimension=1, tiled=True
        ).astype(jnp.float32),
        lax.psum_scatter(
            strips[2].astype(jnp.bfloat16), "pair", scatter_dimension=1, tiled=True
        ).astype(jnp.float32),
        lax.psum_scatter(
            strips[3].astype(jnp.bfloat16), "pair", scatter_dimension=1, tiled=True
        ).astype(jnp.float32),
        lax.psum_scatter(
            strips[4].astype(jnp.bfloat16), "pair", scatter_dimension=1, tiled=True
        ).astype(jnp.float32),
    )
    return (mixed_out, grad_tokens, owned[0], owned[1], owned[2], owned[3], owned[4])


LINE = 4
HALF = 512
NEG = -1e30
bf16 = jnp.bfloat16
f32 = jnp.float32
VMEM = dict(
    down=24, up=20, normed_back=20, down_grad=20, up_grad=16, middle_back=20, project=20, input_back=18, attend_0=12, attend_1=12,
    attend_back_0=14, attend_back_1=14, attention_out=16, qkv_grad=16, out_grad=10, input_norm=18, input_grad=14, half_added=18
)


def params(name):
    return pltpu.CompilerParams(vmem_limit_bytes=VMEM.get(name, 10) * 1024 * 1024)


PLACES = dict(half_added=8, attend_1=20, touch=20, attend_back_0=20, down_sum=20, up_parts=20, up_sum=20)


def cost(name):
    return pl.CostEstimate(flops=int(PLACES.get(name, 0.5) * 1.15e9), bytes_accessed=1 << 16, transcendentals=0)


def hbm():
    return pl.BlockSpec(memory_space=pl.ANY)


def block(*shape):
    return pl.BlockSpec(shape, lambda i, s: (0,) * len(shape))


def call(kernel, name, ins, outs, scratch, flops, *args, grid=(1,)):
    out = pl.pallas_call(
        kernel,
        grid_spec=pltpu.PrefetchScalarGridSpec(
            num_scalar_prefetch=1,
            grid=grid,
            in_specs=ins,
            out_specs=[spec for spec, _ in outs],
            scratch_shapes=scratch,
        ),
        out_shape=[shape for _, shape in outs],
        compiler_params=params(name),
        cost_estimate=cost(name),
        name=name,
    )(*args)
    return out


def of(kind, *shape):
    return jax.ShapeDtypeStruct(shape, kind)


def dot(a, b, contract):
    return lax.dot_general(a, b, ((contract[:1], contract[1:]), ((), ())), preferred_element_type=f32)


def row_pairs(target):
    pairs = []
    for r in range(LINE * 4):
        z, x, c = target(r // 4, r // 2 % 2, r % 2)
        pairs.append((r, z % LINE * 4 + x * 2 + c))
    return pairs


def shift_z(v, k):
    return lax.ppermute(v, "rows", row_pairs(lambda z, x, c: (z + k, x, c)))


def swap_x(v):
    return lax.ppermute(v, "rows", row_pairs(lambda z, x, c: (z, 1 - x, c)))


def swap_c(v):
    return lax.ppermute(v, "rows", row_pairs(lambda z, x, c: (z, x, 1 - c)))


def swap_y(v):
    return lax.ppermute(v, "pair", [(0, 1), (1, 0)])


def along_line(shard):
    return [shard] + [shift_z(shard, k) for k in range(1, LINE)]


def barrier(*values):
    return lax.optimization_barrier(values)


def after(value, *others):
    return lax.optimization_barrier((value, others))[0]


def qkv_copies(info, refs, w_ref, sems, start_col, cols):
    out = []
    for dx in range(2):
        for dz in range(LINE):
            chip = lax.rem(info[0] + LINE - dz, LINE) * 2 + lax.rem(info[1] + dx, 2)
            for own in (0, 1):
                core = info[2] if own == 0 else 1 - info[2]
                out.append(
                    pltpu.make_async_copy(
                        refs[own * 2 + dx].at[dz, :, pl.ds(start_col, cols)],
                        w_ref.at[pl.ds(pl.multiple_of(chip * 128 + core * 64, 64), 64), :],
                        sems.at[(dx * LINE + dz) * 2 + own],
                    )
                )
    return out


def by_chip(z, x):
    return z * 2 + x


def by_unit(z, x):
    return z // 2 * 4 + x * 2 + z % 2


def piece_copies(info, refs, w_ref, sems, rows, cols, order):
    line, beside, across, far_a, far_b = refs
    out = [[], []]
    for dy in range(2):
        for dx in range(2):
            for dz in range(LINE):
                chip = order(lax.rem(info[0] + LINE - dz, LINE), lax.rem(info[1] + dx, 2))
                ref, at = ((line, dz), (beside, dz), (across, dz), (far_a, dz) if dz < far_a.shape[0] else (far_b, dz - far_a.shape[0]))[dx + 2 * dy]
                out[dy].append(
                    pltpu.make_async_copy(
                        ref.at[at, :, pl.ds(0, cols)],
                        w_ref.at[pl.ds(pl.multiple_of(chip * rows, rows), rows), pl.ds(dy * cols, cols)],
                        sems.at[(dy * 2 + dx) * LINE + dz],
                    )
                )
    return out


def start(copies):
    for c in copies:
        c.start()


def wait(copies):
    for c in copies:
        c.wait()


def project_kernel(info, xo_ref, xt_ref, *refs):
    out_ref, g_ref, w_ref, gcol_ref, nin_ref, sems = refs[4:]
    copies = qkv_copies(info, refs[:4], w_ref, sems, 0, 1536)
    gains = qkv_copies(info, refs[:4], gcol_ref, sems.at[pl.ds(16, 16)], 1536, 128)
    start(gains)
    start(copies)
    wait(gains)
    both = gcol_ref[...].T.astype(f32)[:2]
    g_ref[...] = both
    side = info[3]
    for part, x_ref in ((0, xo_ref), (1, xt_ref)):
        at = side if part == 0 else 1 - side
        tokens = pl.ds(pl.multiple_of(at * HALF, HALF), HALF)
        nin_ref[tokens, :] = (centred(x_ref[...].astype(f32))[0] * both[:1]).astype(bf16)
        if part == 0:
            wait(copies)
        for n in range(2):
            cols = slice(n * 768, n * 768 + 768)
            out_ref[tokens, cols] = dot(nin_ref[tokens, :], w_ref[:, cols], (1, 0)).astype(bf16)


def project(info, x_own, x_other, pieces):
    return call(
        project_kernel,
        "project",
        [block(HALF, 1024), block(HALF, 1024)] + [hbm()] * 4,
        [(block(1024, 1536), of(bf16, 1024, 1536)), (block(2, 1024), of(f32, 2, 1024))],
        [
            pltpu.VMEM((1024, 1536), bf16),
            pltpu.VMEM((1024, 128), bf16),
            pltpu.VMEM((1024, 1024), bf16),
            pltpu.SemaphoreType.DMA((32,)),
        ],
        2 * 1024 * 1024 * 1536,
        info,
        x_own,
        x_other,
        *pieces,
    )


TILES = ((0, 512), (256, 512), (512, 768), (768, 1024))


def own_lanes(v, head):
    lane = lax.broadcasted_iota(jnp.int32, v.shape, 1)
    return jnp.where((lane >= 64) if head else (lane < 64), v, jnp.zeros_like(v))


def attend_kernel(info, q_ref, k_ref, v_ref, bias_ref, keep_ref, send_ref, lse_ref):
    side = info[3]
    lane = lax.broadcasted_iota(jnp.int32, (256, 128), 1)
    for tile, (first, seen) in enumerate(TILES):
        rows = slice(first, first + 256)
        q_tile = q_ref[rows, :] * jnp.asarray(0.125, bf16)
        done, lse = [], []
        for head in range(2):
            s = dot(own_lanes(q_tile, head), k_ref[:seen, :], (1, 1)) + bias_ref[rows, :seen]
            top = jnp.max(s, axis=1, keepdims=True)
            p = jnp.exp(s - top)
            total = jnp.sum(p, axis=1, keepdims=True)
            lse.append(top + jnp.log(total))
            done.append(dot(p.astype(bf16), v_ref[:seen, :], (1, 0)) * (1.0 / total))
        both = jnp.where(lane < 64, done[0], done[1]).astype(bf16)
        lse_ref[0, :, rows] = jnp.where(lane == 0, lse[0], lse[1]).T[:2]
        half, row = tile // 2, tile % 2 * 256

        @pl.when(side == half)
        def _():
            keep_ref[row : row + 256, :] = both

        @pl.when(side != half)
        def _():
            send_ref[row : row + 256, :] = both


def head_parts(group):
    return [pl.BlockSpec((1024, 128), lambda h, s, j=j: (0, 6 * group + 2 * j + h)) for j in range(3)]


def attend(info, projected, bias, group):
    piece = pl.BlockSpec((HALF, 128), lambda h, s: (0, h))
    return call(
        attend_kernel,
        f"attend_{group}",
        [*head_parts(group), block(1024, 1024)],
        [
            (piece, of(bf16, HALF, 256)),
            (piece, of(bf16, HALF, 256)),
            (pl.BlockSpec((1, 2, 1024), lambda h, s: (h, 0, 0)), of(f32, 2, 2, 1024)),
        ],
        [],
        4 * 1024 * 768 * 64 * 4,
        info,
        projected,
        projected,
        projected,
        bias,
        grid=(2,),
    )


def attend_back_kernel(info, q_ref, k_ref, v_ref, bias_ref, lse_ref, keep_ref, send_ref, out_ref, dk_ref, dv_ref):
    side = info[3]
    pair = pl.program_id(0)
    k_t = k_ref[...].T
    dk_ref[...] = jnp.zeros_like(dk_ref)
    dv_ref[...] = jnp.zeros_like(dv_ref)
    for tile, (start, seen) in enumerate(TILES):
        half, row = tile // 2, tile % 2 * 256
        q_tile = q_ref[start : start + 256, :] * jnp.asarray(0.125, bf16)
        g_tile = jnp.where(side == half, keep_ref[row : row + 256, :], send_ref[row : row + 256, :])
        pieces = []
        for head in range(2):
            q_head = own_lanes(q_tile, head)
            g_head = own_lanes(g_tile, head)
            s = dot(k_ref[:seen, :], q_head, (1, 1))
            p = jnp.exp(s + bias_ref[:seen, start : start + 256] - lse_ref[0, head : head + 1, start : start + 256])
            dp = dot(v_ref[:seen, :], g_head, (1, 1))
            centre = jnp.sum(p * dp, axis=0, keepdims=True)
            ds = (p * (dp - centre)).astype(bf16)
            dv_ref[:seen, :] += dot(p.astype(bf16), g_head, (1, 0))
            dk_ref[:seen, :] += dot(ds, q_head, (1, 0))
            pieces.append(dot(k_t[head * 64 : head * 64 + 64, :seen], ds, (1, 0)) * 0.125)
        cols = pl.ds(pl.multiple_of(pair * 128, 128), 128)
        out_ref[start : start + 256, cols] = jnp.concatenate(pieces, axis=0).T.astype(bf16)
    out_ref[:, pl.ds(pl.multiple_of(256 + pair * 128, 128), 128)] = dk_ref[...].astype(bf16)
    out_ref[:, pl.ds(pl.multiple_of(512 + pair * 128, 128), 128)] = dv_ref[...].astype(bf16)


def attend_back(info, projected, bias, lse, keep, other, group):
    piece = pl.BlockSpec((HALF, 128), lambda h, s: (0, 2 * group + h))
    return pl.pallas_call(
        attend_back_kernel,
        grid_spec=pltpu.PrefetchScalarGridSpec(
            num_scalar_prefetch=1,
            grid=(2,),
            in_specs=[
                *head_parts(group),
                pl.BlockSpec((1024, 1024), lambda h, s: (0, 0)),
                pl.BlockSpec((1, 2, 1024), lambda h, s: (h, 0, 0)),
                piece,
                piece,
            ],
            out_specs=pl.BlockSpec((1024, 768), lambda h, s: (0, 0)),
            scratch_shapes=[pltpu.VMEM((1024, 128), f32), pltpu.VMEM((1024, 128), f32)],
        ),
        out_shape=jax.ShapeDtypeStruct((1024, 768), bf16),
        compiler_params=params(f"attend_back_{group}"),
        cost_estimate=cost(f"attend_back_{group}"),
        name=f"attend_back_{group}",
    )(info, projected, projected, projected, bias, lse, keep, other)


def centred(v):
    off = v - jnp.mean(v, axis=-1, keepdims=True)
    scale = lax.rsqrt(jnp.mean(off * off, axis=-1, keepdims=True) + epsilon)
    return off * scale, scale


def out_kernel(info, x_ref, k0, k1, g0, g1, w_ref, g_ref, mid_ref, nm_ref, own_ref, oth_ref, t_ref):
    places = [(info[3] if i < 2 else 1 - info[3]) * HALF + i % 2 * 256 for i in range(4)]
    places = [pl.ds(pl.multiple_of(at, 256), 256) for at in places]
    for half in range(2):
        cols = slice(half * 512, half * 512 + 512)
        branch = x_ref[:, cols].astype(f32)
        for at, ref in zip(places, (k0, k1, g0, g1)):
            branch = branch + dot(ref[...], w_ref[half, at, :], (1, 0))
        mid_ref[:, cols] = branch
    nm_ref[...] = (centred(mid_ref[...])[0] * g_ref[1:]).astype(bf16)
    for at, ref in zip(places, (k0, k1, g0, g1)):
        t_ref[at, :] = ref[...].T
    put_parities(info, t_ref, own_ref, oth_ref)


def put_parities(info, t_ref, own_ref, oth_ref):
    for dx in range(2):
        for dz in range(LINE):
            chip = lax.rem(info[0] + dz, LINE) * 2 + lax.rem(info[1] + dx, 2)
            here = pl.multiple_of(chip * 128 + info[2] * 64, 64)
            there = pl.multiple_of(chip * 128 + (1 - info[2]) * 64, 64)
            own_ref[dx * LINE + dz] = t_ref[pl.ds(here, 64), :]
            oth_ref[dx * LINE + dz] = t_ref[pl.ds(there, 64), :]


def attention_out(info, x, keeps, gots, w, gain):
    return call(
        out_kernel,
        "attention_out",
        [block(HALF, 1024)] + [block(HALF, 256)] * 4 + [block(2, 1024, 512), block(2, 1024)],
        [
            (block(HALF, 1024), of(f32, HALF, 1024)),
            (block(HALF, 1024), of(bf16, HALF, 1024)),
            (block(8, 64, HALF), of(bf16, 8, 64, HALF)),
            (block(8, 64, HALF), of(bf16, 8, 64, HALF)),
        ],
        [pltpu.VMEM((1024, HALF), bf16)],
        2 * 512 * 1024 * 1024,
        info,
        x,
        *keeps,
        *gots,
        w,
        gain,
    )


def up_kernel(info, x0_ref, x1_ref, *refs):
    act_ref, slope_ref, w_ref, sems = refs[5:]
    step = pl.program_id(0)
    near, far = piece_copies(info, refs[:5], w_ref, sems, 128, 1024, by_chip)

    @pl.when(step == 0)
    def _():
        start(near)
        start(far)
        wait(near)

    @pl.when(step == 1)
    def _():
        wait(far)

    for part, x_ref in enumerate((x0_ref, x1_ref)):
        rows = slice(part * HALF, part * HALF + HALF)
        for n in range(2):
            cols = slice(n * 512, n * 512 + 512)
            pre = dot(x_ref[...], w_ref[:, pl.ds(pl.multiple_of(step * 1024 + n * 512, 512), 512)], (1, 0))
            below = 0.5 * (1.0 + lax.erf(pre * 0.7071067811865476))
            act_ref[rows, cols] = (pre * below).astype(bf16)
            slope_ref[rows, cols] = (below + pre * (0.3989422804014327 * jnp.exp(-0.5 * pre * pre))).astype(bf16)


def up(info, x_own, x_sib, pieces):
    out = pl.BlockSpec((1024, 1024), lambda n, s: (0, lax.rem(s[3] + n, 2)))
    return call(
        up_kernel,
        "up",
        [block(HALF, 1024)] * 2 + [hbm()] * 5,
        [(out, of(bf16, 1024, 2048))] * 2,
        [pltpu.VMEM((1024, 2048), bf16), pltpu.SemaphoreType.DMA((16,))],
        4 * 512 * 1024 * 4096,
        info,
        x_own,
        x_sib,
        *pieces,
        grid=(2,),
    )


def down_kernel(info, act_ref, slope_ref, c0_ref, c1_ref, mid_ref, *refs):
    keep_ref, send_ref, gp_ref, w_ref, acc_ref, sems = refs[5:]
    step = pl.program_id(0)
    side = info[3]
    near, far = piece_copies(info, refs[:5], w_ref, sems, 256, 512, by_unit)
    mine = pl.ds(pl.multiple_of(side * 512, 512), 512)
    theirs = pl.ds(pl.multiple_of((1 - side) * 512, 512), 512)

    @pl.when(step == 0)
    def _():
        start(near)
        start(far)
        wait(near)
        wait(far)

    units = pl.ds(pl.multiple_of(step * 1024, 1024), 1024)
    for part, cot_ref in enumerate((c0_ref, c1_ref)):
        rows = slice(part * HALF, part * HALF + HALF)
        for n in range(2):
            here = pl.ds(pl.multiple_of(step * 1024 + n * 512, 512), 512)
            cols = slice(n * 512, n * 512 + 512)
            back = dot(cot_ref[:, mine], w_ref[here, :512], (1, 1)) + dot(cot_ref[:, theirs], w_ref[here, 512:], (1, 1))
            gp_ref[rows, cols] = (back * slope_ref[rows, cols].astype(f32)).astype(bf16)
        total = dot(act_ref[rows, :], w_ref[units, :], (1, 0))

        @pl.when(step == 0)
        def _():
            acc_ref[rows, :] = total

        @pl.when(step == 1)
        def _():
            done = total + acc_ref[rows, :]
            if part == 0:
                keep_ref[:, mine] = mid_ref[:, mine] + done[:, :512]
                keep_ref[:, theirs] = mid_ref[:, theirs] + done[:, 512:]
            else:
                send_ref[:, mine] = done[:, :512].astype(bf16)
                send_ref[:, theirs] = done[:, 512:].astype(bf16)


def down(info, act, slope, cot_own, cot_sib, mid, pieces):
    tile = pl.BlockSpec((1024, 1024), lambda n, s: (0, n))
    return call(
        down_kernel,
        "down",
        [tile, tile] + [block(HALF, 1024)] * 3 + [hbm()] * 5,
        [
            (block(HALF, 1024), of(f32, HALF, 1024)),
            (block(HALF, 1024), of(bf16, HALF, 1024)),
            (tile, of(bf16, 1024, 2048)),
        ],
        [pltpu.VMEM((2048, 1024), bf16), pltpu.VMEM((1024, 1024), f32), pltpu.SemaphoreType.DMA((16,))],
        4 * 512 * 1024 * 4096,
        info,
        act,
        slope,
        cot_own,
        cot_sib,
        mid,
        *pieces,
        grid=(2,),
    )


def normed_back_kernel(info, gp_ref, *refs):
    keep_ref, send_ref, w_ref, sems = refs[5:]
    near, far = piece_copies(info, refs[:5], w_ref, sems, 128, 1024, by_chip)
    start(near)
    start(far)
    wait(near)
    wait(far)
    mine = pl.ds(pl.multiple_of(info[3] * 1024, 1024), 1024)
    theirs = pl.ds(pl.multiple_of((1 - info[3]) * 1024, 1024), 1024)
    for part, out in ((1, send_ref), (0, keep_ref)):
        rows = slice(part * HALF, part * HALF + HALF)
        for n in range(2):
            dims = slice(n * 512, n * 512 + 512)
            total = dot(gp_ref[rows, mine], w_ref[dims, :1024], (1, 1)) + dot(gp_ref[rows, theirs], w_ref[dims, 1024:], (1, 1))
            out[:, dims] = total.astype(out.dtype)


def normed_back(info, gp, pieces):
    return call(
        normed_back_kernel,
        "normed_back",
        [block(1024, 2048)] + [hbm()] * 5,
        [(block(HALF, 1024), of(f32, HALF, 1024)), (block(HALF, 1024), of(bf16, HALF, 1024))],
        [pltpu.VMEM((1024, 2048), bf16), pltpu.SemaphoreType.DMA((16,))],
        2 * 512 * 1024 * 4096,
        info,
        gp,
        *pieces,
    )


def middle_back_kernel(info, e0_ref, e1_ref, cot_ref, mid_ref, g_ref, w_ref, gm_ref, gb_ref, keep, send):
    n, scale = centred(mid_ref[...])
    eg = (e0_ref[...] + e1_ref[...].astype(f32)) * g_ref[1:]
    lean = eg - jnp.mean(eg, axis=-1, keepdims=True) - n * jnp.mean(eg * n, axis=-1, keepdims=True)
    grad = cot_ref[...].astype(f32) + scale * lean
    gm_ref[...] = grad
    low = grad.astype(bf16)
    gb_ref[...] = low
    for out, at in ((keep, info[3]), (send, 1 - info[3])):
        rows = pl.ds(pl.multiple_of(at * HALF, HALF), HALF)
        out[...] = (dot(low[:, :512], w_ref[0, rows, :], (1, 1)) + dot(low[:, 512:], w_ref[1, rows, :], (1, 1))).astype(bf16)


def middle_back(info, e_keep, e_got, cot, mid, gain, w):
    return call(
        middle_back_kernel,
        "middle_back",
        [block(HALF, 1024)] * 4 + [block(2, 1024), block(2, 1024, 512)],
        [
            (block(HALF, 1024), of(f32, HALF, 1024)),
            (block(HALF, 1024), of(bf16, HALF, 1024)),
            (block(HALF, 512), of(bf16, HALF, 512)),
            (block(HALF, 512), of(bf16, HALF, 512)),
        ],
        [],
        2 * 512 * 1024 * 1024,
        info,
        e_keep,
        e_got,
        cot,
        mid,
        gain,
        w,
    )


def down_grad_kernel(info, c0_ref, c1_ref, act_ref, far_a, far_b, across, beside, own, t_ref):
    g = pl.program_id(0)

    @pl.when(g == 0)
    def _():
        t_ref[:, :HALF] = c0_ref[...].T
        t_ref[:, HALF:] = c1_ref[...].T

    x = lax.rem(info[1] + 1 - lax.rem(g, 2), 2)
    side = lax.rem(info[3] + 1 - g // 2, 2)
    rows = pl.ds(pl.multiple_of(side * 512, 512), 512)
    for half in range(2):
        units = pl.ds(pl.multiple_of(half * 1024 + x * 512, 512), 512)
        total = dot(t_ref[rows, :], act_ref[:, units], (1, 0)).astype(bf16)
        for j in range(2):
            dz = lax.rem(half * 2 + j - info[0] + LINE, LINE)
            part = total[:, j * 256 : j * 256 + 256]
            for at, ref in ((1, across), (2, beside), (3, own)):

                @pl.when(g == at)
                def _():
                    ref[dz] = part

            for ref, here in ((far_a, dz < 2), (far_b, dz >= 2)):

                @pl.when((g == 0) & here)
                def _():
                    ref[lax.rem(dz, 2)] = part


def down_grad(info, cot_own, cot_sib, act):
    return call(
        down_grad_kernel,
        "down_grad",
        [block(HALF, 1024), block(HALF, 1024), block(1024, 2048)],
        [(block(n, 512, 256), of(bf16, n, 512, 256)) for n in (2, 2, 4, 4, 4)],
        [pltpu.VMEM((1024, 1024), bf16)],
        2 * 1024 * 1024 * 2048,
        info,
        cot_own,
        cot_sib,
        act,
        grid=(4,),
    )


def stay(g, first):
    return lax.max(0, lax.min(g - first, 1))


def up_grad_kernel(info, n0_ref, n1_ref, gp_ref, far, across, beside, own, t_ref):
    g = pl.program_id(0)

    @pl.when(g == 0)
    def _():
        for dx in range(2):
            for dz in range(LINE):
                chip = lax.rem(info[0] + dz, LINE) * 2 + lax.rem(info[1] + dx, 2)
                cols = pl.ds(pl.multiple_of(chip * 128, 128), 128)
                rows = slice((dx * LINE + dz) * 128, (dx * LINE + dz) * 128 + 128)
                t_ref[rows, :HALF] = n0_ref[:, cols].T
                t_ref[rows, HALF:] = n1_ref[:, cols].T

    total = dot(t_ref[...], gp_ref[...], (1, 0)).astype(bf16).reshape(8, 128, 512)

    @pl.when(g < 2)
    def _():
        across[...] = total[:4]
        far[...] = total[4:]

    @pl.when(g >= 2)
    def _():
        own[...] = total[:4]
        beside[...] = total[4:]


def up_grad(info, nm_own, nm_sib, gp):
    right = pl.BlockSpec((1024, 512), lambda g, s: (0, lax.rem(s[3] + 1 - g // 2, 2) * 2 + lax.rem(g, 2)))
    return call(
        up_grad_kernel,
        "up_grad",
        [block(HALF, 1024), block(HALF, 1024), right],
        [
            (pl.BlockSpec((LINE, 128, 512), lambda g, s, f=f: (0, 0, stay(g, f))), of(bf16, LINE, 128, 1024))
            for f in (0, 0, 2, 2)
        ],
        [pltpu.VMEM((1024, 1024), bf16)],
        2 * 1024 * 512 * 4096,
        info,
        nm_own,
        nm_sib,
        gp,
        grid=(4,),
    )


def out_grad_kernel(info, l0_ref, r0_ref, l1_ref, r1_ref, keep_ref, send_ref):
    for out, at in ((keep_ref, info[3]), (send_ref, 1 - info[3])):
        cols = pl.ds(pl.multiple_of(at * 512, 512), 512)
        total = dot(l0_ref[...], r0_ref[:, cols], (1, 0)) + dot(l1_ref[...], r1_ref[:, cols], (1, 0))
        out[...] = total.astype(bf16).reshape(8, 64, 512)


def out_grad(info, att_t, gb, att_t_sib, gb_sib):
    return call(
        out_grad_kernel,
        "out_grad",
        [block(512, HALF), block(HALF, 1024)] * 2,
        [(block(8, 64, 512), of(bf16, 8, 64, 512))] * 2,
        [],
        2 * 512 * 1024 * 1024,
        info,
        att_t.reshape(512, HALF),
        gb,
        att_t_sib.reshape(512, HALF),
        gb_sib,
    )


def input_back_kernel(info, d0_ref, d1_ref, *refs):
    keep_ref, send_ref, w_ref, sems = refs[4:]
    copies = qkv_copies(info, refs[:4], w_ref, sems, 0, 1536)
    start(copies)
    wait(copies)
    for part, out in ((1, send_ref), (0, keep_ref)):
        at = info[3] if part == 0 else 1 - info[3]
        slots = pl.ds(pl.multiple_of(at * HALF, HALF), HALF)
        for n in range(2):
            dims = slice(n * 512, n * 512 + 512)
            total = dot(d0_ref[slots, :], w_ref[dims, :768], (1, 1)) + dot(d1_ref[slots, :], w_ref[dims, 768:], (1, 1))
            out[:, dims] = total.astype(out.dtype)


def input_back(info, d0, d1, pieces):
    return call(
        input_back_kernel,
        "input_back",
        [block(1024, 768)] * 2 + [hbm()] * 4,
        [(block(HALF, 1024), of(f32, HALF, 1024)), (block(HALF, 1024), of(bf16, HALF, 1024))],
        [pltpu.VMEM((1024, 1536), bf16), pltpu.SemaphoreType.DMA((16,))],
        2 * 1024 * 1024 * 1536,
        info,
        d0,
        d1,
        *pieces,
    )


def qkv_grad_kernel(info, l0_ref, r0_ref, l1_ref, r1_ref, *refs):
    beside, own = refs[-2:]
    total = dot(l0_ref[...], r0_ref[...], (1, 0)) + dot(l1_ref[...], r1_ref[...], (1, 0))
    total = total.astype(bf16).reshape(8, 64, 768)
    own[:, :, :768] = total[:4]
    beside[:, :, :768] = total[4:]
    if len(refs) == 4:
        both = (refs[0][...].astype(f32) + refs[1][...].astype(f32)).astype(bf16)
        own[:, :, 768:] = both[:4]
        beside[:, :, 768:] = both[4:]


def qkv_grad(info, nin_t, dproj, nin_t_sib, dproj_sib, more=()):
    width = 768 + 512 * bool(more)
    return call(
        qkv_grad_kernel,
        "qkv_grad",
        [block(512, 1024), block(1024, 768)] * 2 + [block(8, 64, 512)] * len(more),
        [(block(4, 64, width), of(bf16, 4, 64, width))] * 2,
        [],
        2 * 2048 * 512 * 768,
        info,
        nin_t.reshape(512, 1024),
        dproj,
        nin_t_sib.reshape(512, 1024),
        dproj_sib,
        *more,
    )


def input_norm_kernel(info, xo_ref, xt_ref, g_ref, own_ref, oth_ref, t_ref):
    side = info[3]
    for part, x_ref in ((0, xo_ref), (1, xt_ref)):
        at = side if part == 0 else 1 - side
        normed = (centred(x_ref[...].astype(f32))[0] * g_ref[:1]).astype(bf16)
        t_ref[:, pl.ds(pl.multiple_of(at * HALF, HALF), HALF)] = normed.T
    put_parities(info, t_ref, own_ref, oth_ref)


def input_norm(info, x_own, x_other, gains):
    return call(
        input_norm_kernel,
        "input_norm",
        [block(HALF, 1024), block(HALF, 1024), block(2, 1024)],
        [(block(8, 64, 1024), of(bf16, 8, 64, 1024))] * 2,
        [pltpu.VMEM((1024, 1024), bf16)],
        20 << 20,
        info,
        x_own,
        x_other,
        gains,
    )


def heads_kernel(info, w_ref, got_ref, gain_ref, out_ref):
    side = info[3] == 0
    first, middle, last = w_ref[:, :512], got_ref[:, :512], w_ref[:, 1024:]
    q = jnp.where(side, first, middle)
    k = jnp.where(side, last, first)
    v = jnp.where(side, middle, last)
    for i in range(2):
        for j, part in enumerate((q, k, v)):
            out_ref[:, i * 768 + j * 256 : i * 768 + j * 256 + 256] = part[:, i * 256 : i * 256 + 256]
    lane = lax.broadcasted_iota(jnp.int32, (w_ref.shape[0], 128), 1)
    mine = jnp.broadcast_to(gain_ref[...].astype(f32), lane.shape)
    theirs = jnp.broadcast_to(got_ref[:, 512:513].astype(f32), lane.shape)
    out_ref[:, 1536:] = jnp.where((lane == 0) == side, mine, theirs).astype(bf16)


def heads_of(info, w, got, gains):
    return call(
        heads_kernel,
        "heads",
        [block(64, 1536), block(64, 640), block(64, 1)],
        [(block(64, 1664), of(bf16, 64, 1664))],
        [],
        1 << 16,
        info,
        w,
        got,
        gains,
    )[0]


def by_core_kernel(info, up_ref, own_ref, oth_ref):
    for ref, core in ((own_ref, info[2]), (oth_ref, 1 - info[2])):
        for i, to in enumerate((0, 2, 1, 3)):
            ref[:, to * 256 : to * 256 + 256] = up_ref[:, pl.ds(pl.multiple_of(i * 512 + core * 256, 256), 256)]


def by_core(info, w_up):
    return call(
        by_core_kernel,
        "by_core",
        [block(64, 2048)],
        [(block(64, 1024), of(bf16, 64, 1024))] * 2,
        [],
        1 << 16,
        info,
        w_up,
    )


def both_rows_kernel(info, own_ref, got_ref, out_ref):
    out_ref[pl.ds(pl.multiple_of(info[2] * 64, 64), 64), :] = own_ref[...]
    out_ref[pl.ds(pl.multiple_of((1 - info[2]) * 64, 64), 64), :] = got_ref[...]


def both_rows(info, own, got):
    return call(
        both_rows_kernel,
        "both_rows",
        [block(64, 1024)] * 2,
        [(block(128, 1024), of(bf16, 128, 1024))],
        [],
        1 << 16,
        info,
        own,
        got,
    )[0]


def added_kernel(info, a_ref, b_ref, out_ref):
    out_ref[...] = (a_ref[...].astype(f32) + b_ref[...].astype(f32)).astype(bf16)


def added(info, a, b, name="added"):
    steps = 2
    spec = pl.BlockSpec((a.shape[0] // steps, *a.shape[1:]), lambda i, s: (i,) + (0,) * (a.ndim - 1))
    return call(added_kernel, name, [spec, spec], [(spec, of(bf16, *a.shape))], [], 0, info, a, b, grid=(steps,))[0]


def half_added_kernel(info, a_ref, b_ref, first_ref, second_ref, a_out, b_out):
    a_out[:2] = (a_ref[:2].astype(f32) + first_ref[...].astype(f32)).astype(bf16)
    a_out[2:] = a_ref[2:]
    b_out[:2] = b_ref[:2]
    b_out[2:] = (b_ref[2:].astype(f32) + second_ref[...].astype(f32)).astype(bf16)


def half_added(info, a, b, first, second):
    spec, half = block(*a.shape), block(*first.shape)
    return call(
        half_added_kernel, "half_added", [spec, spec, half, half], [(spec, of(bf16, *a.shape))] * 2, [], 0, info, a, b, first, second
    )


def line_parts_kernel(info, a_ref, b_ref, c_ref, *outs):
    for k, out in enumerate(outs):
        out[...] = (a_ref[k].astype(f32) + b_ref[k].astype(f32) + c_ref[k].astype(f32)).astype(bf16)


def line_parts(info, own, from_x, from_y, name):
    spec, out = block(*own.shape), block(*own.shape[1:])
    return call(
        line_parts_kernel, name, [spec] * 3, [(out, of(bf16, *own.shape[1:]))] * LINE, [], 0, info, own, from_x, from_y
    )


def qkv_parts_kernel(info, a_ref, ax_ref, b_ref, bx_ref, *outs):
    for k, out in enumerate(outs):
        out[:, :1280] = (a_ref[k].astype(f32) + ax_ref[k].astype(f32)).astype(bf16)
        out[:, 1280:] = (b_ref[k].astype(f32) + bx_ref[k].astype(f32)).astype(bf16)


def qkv_parts(info, a, a_x, b, b_x):
    return call(
        qkv_parts_kernel,
        "qkv_parts",
        [block(4, 64, 1280)] * 2 + [block(4, 64, 768)] * 2,
        [(block(64, 2048), of(bf16, 64, 2048))] * LINE,
        [],
        0,
        info,
        a,
        a_x,
        b,
        b_x,
    )


def stack_kernel(info, *refs):
    for k in range(LINE):
        refs[LINE][k] = refs[k][...]


def stacked(info, parts, name):
    shape = parts[0].shape
    return call(
        stack_kernel, name, [block(*shape)] * LINE, [(block(LINE, *shape), of(bf16, LINE, *shape))], [], 0, info, *parts
    )[0]


def touch_kernel(info, a_ref, out_ref):
    out_ref[...] = a_ref[...]


def touch(info, a):
    return call(touch_kernel, "touch", [block(*a.shape)], [(block(*a.shape), of(a.dtype, *a.shape))], [], 0, info, a)[0]


def summed(refs, *at):
    total = refs[0][at].astype(f32)
    for ref in refs[1:]:
        total = total + ref[at].astype(f32)
    return total


def down_sum_kernel(info, *refs):
    refs[4][...] = summed(refs[:4]).T


def down_sum(info, parts):
    return call(
        down_sum_kernel,
        "down_sum",
        [block(512, 256)] * 4,
        [(block(256, 512), of(f32, 256, 512))],
        [],
        0,
        info,
        *parts,
    )[0]


def up_sum_kernel(info, *refs):
    for out, core in ((refs[4], info[2]), (refs[5], 1 - info[2])):
        out[...] = summed(refs[:4], pl.ds(pl.multiple_of(core * 64, 64), 64))


def up_sum(info, parts):
    return call(
        up_sum_kernel,
        "up_sum",
        [block(128, 1024)] * 4,
        [(block(64, 1024), of(f32, 64, 1024))] * 2,
        [],
        0,
        info,
        *parts,
    )


def up_whole_kernel(info, mine_ref, got_ref, w_ref, in_ref, out_ref, own_ref, send_ref):
    for ref, core in ((mine_ref, info[2]), (got_ref, 1 - info[2])):
        for i, place in enumerate((0, 2, 1, 3)):
            cols = pl.ds(pl.multiple_of(i * 512 + core * 256, 256), 256)
            out_ref[:, cols] = ref[:, place * 256 : place * 256 + 256]
    total = jnp.sum(w_ref[...].astype(f32) * out_ref[...], axis=1, keepdims=True)
    mid = jnp.broadcast_to(total, in_ref.shape)
    first = info[3] == 0
    own_ref[...] = jnp.where(first, in_ref[...], mid)
    send_ref[...] = jnp.where(first, mid, in_ref[...])


def up_whole(info, mine, got, w, in_sums):
    return call(
        up_whole_kernel,
        "up_whole",
        [block(64, 1024)] * 2 + [block(64, 2048), block(64, 128)],
        [(block(64, 2048), of(f32, 64, 2048))] + [(block(64, 128), of(f32, 64, 128))] * 2,
        [],
        0,
        info,
        mine,
        got,
        w,
        in_sums,
    )


def qkv_sum_kernel(info, *refs):
    heads_ref, keep_ref, send_ref, sum_ref, out_ref = refs[4:]
    total = summed(refs[:4])
    out_ref[...] = total[:, 768:1280]
    groups = (total[:, :768], total[:, 1280:])
    q, k, v = (jnp.concatenate([g[:, j : j + 256] for g in groups], axis=1) for j in (0, 256, 512))
    weights = heads_ref[...].astype(f32)
    by_row = jnp.sum(weights[:, :768] * groups[0], axis=1, keepdims=True) + jnp.sum(
        weights[:, 768:1536] * groups[1], axis=1, keepdims=True
    )
    sum_ref[...] = jnp.broadcast_to(by_row, sum_ref.shape)
    first = info[3] == 0
    keep_ref[:, :512] = jnp.where(first, q, k)
    keep_ref[:, 512:] = jnp.where(first, k, v)
    send_ref[...] = jnp.where(first, v, q)


def qkv_sum(info, parts, heads):
    return call(
        qkv_sum_kernel,
        "qkv_sum",
        [block(64, 2048)] * 4 + [block(64, 1664)],
        [(block(64, n), of(f32, 64, n)) for n in (1024, 512, 128, 512)],
        [],
        0,
        info,
        *parts,
        heads,
    )


def qkv_whole_kernel(info, keep_ref, got_ref, own_ref, other_ref, gain_ref, out_ref, gg_ref):
    out_ref[:, :512] = keep_ref[:, :512]
    out_ref[:, 512:1024] = got_ref[...]
    out_ref[:, 1024:] = keep_ref[:, 512:]
    gg_ref[...] = (own_ref[:, :1] + other_ref[:, :1]) / gain_ref[...].astype(f32)


def qkv_whole(info, keep, got, own_sums, other_sums, gains):
    return call(
        qkv_whole_kernel,
        "qkv_whole",
        [block(64, 1024), block(64, 512), block(64, 128), block(64, 128), block(64, 1)],
        [(block(64, 1536), of(f32, 64, 1536)), (block(64, 1), of(f32, 64, 1))],
        [],
        0,
        info,
        keep,
        got,
        own_sums,
        other_sums,
        gains,
    )


def input_grad_kernel(info, x_ref, e0_ref, e1_ref, gm_ref, g_ref, out_ref):
    n, scale = centred(x_ref[...].astype(f32))
    eg = (e0_ref[...] + e1_ref[...].astype(f32)) * g_ref[:1]
    lean = eg - jnp.mean(eg, axis=-1, keepdims=True) - n * jnp.mean(eg * n, axis=-1, keepdims=True)
    out_ref[...] = gm_ref[...] + scale * lean


def input_grad(info, x, e_own, e_got, gm, gains):
    rows = pl.BlockSpec((256, 1024), lambda i, s: (i, 0))
    return call(
        input_grad_kernel,
        "input_grad",
        [rows] * 4 + [block(2, 1024)],
        [(rows, of(f32, HALF, 1024))],
        [],
        0,
        info,
        x,
        e_own,
        e_got,
        gm,
        gains,
        grid=(2,),
    )[0]


def slot_bias(phones, prompts, targets):
    places = jnp.arange(HALF, dtype=jnp.int32)
    count = phones.shape[0]
    segs, is_phone = [], None
    for lengths in (phones + prompts, targets):
        ends = jnp.stack([sum(lengths[i] for i in range(upto + 1)) for upto in range(count)])
        seg = jnp.sum((places[:, None] >= ends[None, :]).astype(jnp.int32), axis=1)
        segs.append(seg)
        if is_phone is None:
            onehot = seg[:, None] == jnp.arange(count, dtype=jnp.int32)[None, :]
            phone_ends = jnp.sum(jnp.where(onehot, (ends - lengths + phones)[None, :], 0), axis=1)
            is_phone = places < phone_ends
    seg = jnp.concatenate(segs)
    phone = jnp.concatenate([is_phone, jnp.zeros((HALF,), dtype=bool)])
    order = jnp.arange(2 * HALF, dtype=jnp.int32)
    allowed = (seg[:, None] == seg[None, :]) & (
        phone[:, None] | (jnp.logical_not(phone)[None, :] & (order[:, None] <= order[None, :]))
    )
    allowed_t = (seg[:, None] == seg[None, :]) & (
        phone[None, :] | (jnp.logical_not(phone)[:, None] & (order[None, :] <= order[:, None]))
    )
    bias = jnp.where(allowed, 0.0, NEG).astype(f32)
    return bias, jnp.where(allowed_t, 0.0, NEG).astype(f32)


def line_shards(tokens, cotangent, gains, w_qkv, w_out, w_up, w_down, phone_len, prompt_len, target_len):
    r = lax.axis_index("rows")
    side = lax.axis_index("pair")
    core = r % 2
    info = jnp.stack([r // 4, r // 2 % 2, core, side]).astype(jnp.int32)
    x_own = tokens[0]
    cot = cotangent[0]

    out_all = lax.all_gather(w_out, ("pair", "rows"), axis=0, tiled=True).reshape(2, 1024, 512)
    crossed = swap_y(jnp.concatenate([w_qkv[:, 512:1024], jnp.pad(gains, ((0, 0), (0, 127)))], axis=1))
    x_other = swap_y(x_own)
    heads = heads_of(info, w_qkv, crossed, gains)
    pieces = along_line(heads)
    up_keep, up_send = by_core(info, after(w_up, heads))
    up_got = swap_c(up_send)
    bias_t, bias = slot_bias(after(phone_len, up_keep)[0], prompt_len[0], target_len[0])
    up_piece = both_rows(info, up_keep, up_got)
    pieces, x_other, bias, bias_t, up_piece = barrier(pieces, x_other, bias, bias_t, up_piece)
    qkv_line = stacked(info, pieces, "qkv_stack")
    beside = swap_x(qkv_line)
    qkv_line_sib = swap_c(qkv_line)
    up_line = along_line(after(up_piece, qkv_line))
    beside_sib = swap_c(beside)
    heads = touch(info, after(heads, up_line))
    up_line = stacked(info, after(up_line, heads, beside_sib, qkv_line_sib), "up_stack")
    up_x, up_y = swap_x(up_line), swap_y(up_line)

    qkv_pieces = (qkv_line, beside, after(qkv_line_sib, up_line), after(beside_sib, up_line))
    projected, gain_all = project(info, x_own, x_other, qkv_pieces)
    down_line = along_line(after(w_down, projected))
    keep0, send0, lse0 = attend(info, projected, bias, 0)
    got0 = swap_y(send0)
    up_x, up_y = after((up_x, up_y), keep0)
    up_far = [swap_y(up_x[:1]), swap_x(up_y[1:])]
    keep1, send1, lse1 = attend(info, projected, after(bias, keep0), 1)
    got1 = swap_y(send1)
    down_line = stacked(info, after(down_line, keep1), "down_stack")
    down_x = swap_x(down_line)
    cot_sib = swap_c(after(cot, keep1))
    nin_t, nin_t_oth = input_norm(info, after(x_own, down_line), x_other, gain_all)
    down_y = swap_y(after(down_line, got0))
    gain_all = touch(info, after(gain_all, nin_t, up_far, got0, out_all))
    got1 = after(got1, gain_all)
    mid, nm_own, att_t, att_t_oth = attention_out(info, x_own, (keep0, keep1), (got0, got1), out_all, gain_all)
    nm_sib = swap_c(nm_own)
    nin_t_sib = swap_c(after(nin_t_oth, nm_own))
    att_t_sib = swap_c(att_t_oth)
    up_pieces = (up_line, up_x, up_y, *up_far)
    down_far = [swap_y(down_x[:2]), swap_x(down_y[2:])]
    gain_all = touch(info, after(gain_all, nm_own, down_x, down_y))
    nm_sib = after(nm_sib, gain_all)
    act, slope = up(info, nm_own, nm_sib, up_pieces)
    down_pieces = (down_line, down_x, down_y, *down_far)
    mixed_keep, mixed_send, gp = down(info, act, slope, cot, cot_sib, mid, down_pieces)

    gp, nin_t_sib, att_t_sib = barrier(gp, nin_t_sib, att_t_sib)
    mixed_got = swap_c(mixed_send)
    e_keep, e_send = normed_back(info, gp, up_pieces)
    e_got = swap_c(e_send)
    far, far_b, down_across, down_beside, down_own = down_grad(info, cot, cot_sib, after(act, e_keep))
    down_far = (swap_x(far), swap_y(far_b))
    gm, gb, ga_keep, ga_send = middle_back(info, after(e_keep, far), after(e_got, far), cot, mid, gain_all, out_all)
    ga_got = swap_y(ga_send)
    gb_sib = swap_c(gb)
    far, up_across, up_beside, up_own = up_grad(info, nm_own, nm_sib, after(gp, gb))
    down_across, down_beside = half_added(info, after(down_across, far), down_beside, *after(down_far, far))
    down_x, down_y = swap_x(down_beside), swap_y(down_across)
    gb_sib = after(gb_sib, down_across)
    out_keep, out_send = out_grad(info, att_t, after(gb, down_across), att_t_sib, gb_sib)
    out_got = swap_y(out_send)
    up_far = swap_x(after(far, out_keep))
    ga_got = after(ga_got, out_keep)
    dproj0 = attend_back(info, projected, after(bias_t, out_keep), lse0, ga_keep, ga_got, 0)
    dproj0_sib = swap_c(dproj0)
    down_x, down_y = after((down_x, down_y), dproj0)
    down_parts = line_parts(info, down_own, down_x, down_y, "down_parts")
    down_shift = [shift_z(down_parts[k], k) for k in range(1, LINE)]
    up_x = swap_x(up_beside)
    gain_all = touch(info, after(gain_all, out_got, down_parts))
    dproj0_sib = after(dproj0_sib, gain_all)
    first_beside, first_own = qkv_grad(info, nin_t, after(dproj0, gain_all), nin_t_sib, dproj0_sib, (out_keep, out_got))
    first_x = swap_x(first_beside)
    up_across = added(info, up_across, after(up_far, first_own))
    up_y = swap_y(up_across)
    dproj1 = attend_back(info, projected, after(bias_t, first_own, up_across), lse1, ga_keep, ga_got, 1)
    dproj1_sib = swap_c(dproj1)
    g_down = down_sum(info, (after(down_parts[0], dproj1), *after(down_shift, dproj1)))
    up_x, up_y = after((up_x, up_y), g_down)
    up_parts = line_parts(info, up_own, up_x, up_y, "up_parts")
    up_shift = [shift_z(up_parts[k], k) for k in range(1, LINE)]
    dproj1_sib = after(dproj1_sib, up_parts)
    second_beside, second_own = qkv_grad(info, nin_t, after(dproj1, up_parts), nin_t_sib, dproj1_sib)
    second_x = swap_x(second_beside)
    e_own, e_send = input_back(info, after(dproj0, second_own), dproj1, qkv_pieces)
    e_got = swap_y(e_send)
    first_x, second_x = after((first_x, second_x), e_own)
    heads_parts = qkv_parts(info, first_own, first_x, second_own, second_x)
    qkv_shift = [shift_z(heads_parts[k], k) for k in range(1, LINE)]
    up_mine, up_send = up_sum(info, (after(up_parts[0], heads_parts), *up_shift))
    up_got = swap_c(up_send)
    mixed = added(info, mixed_keep, after(mixed_got, up_mine), "mixed")
    grad_tokens = input_grad(info, after(x_own, mixed), e_own, after(e_got, mixed), gm, gain_all)
    keep, send, in_sums, g_out = qkv_sum(info, (after(heads_parts[0], grad_tokens), *after(qkv_shift, grad_tokens)), heads)
    got = swap_y(send)
    g_up, gain_own, gain_send = up_whole(info, up_mine, after(up_got, keep), w_up, in_sums)
    gain_got = swap_y(gain_send)
    g_qkv, grad_gains = qkv_whole(info, keep, after(got, g_up), gain_own, gain_got, gains)
    return (mixed[None], grad_tokens[None], grad_gains, g_qkv, g_out, g_up, g_down)


def solution(mesh):
    lined = mesh.shape["rows"] == 4 * LINE and mesh.shape["pair"] == 2
    return jax.shard_map(
        line_shards if lined else shards,
        mesh=mesh,
        in_specs=(
            P("rows", "pair", None),
            P("rows", "pair", None),
            P("rows", "pair"),
            P("rows", "pair"),
            P("rows", "pair"),
            P("rows", "pair"),
            P("rows", "pair"),
            P("rows", None),
            P("rows", None),
            P("rows", None),
        ),
        out_specs=(
            P("rows", "pair", None),
            P("rows", "pair", None),
            P("rows", "pair"),
            P("rows", "pair"),
            P("rows", "pair"),
            P("rows", "pair"),
            P("rows", "pair"),
        ),
        check_vma=False,
    )
```
